32 devices in a mesh: island: 4 (over z), fsdp: 4 (over y, core), tp: 2 (over x).
Axes of the slice: x: 2, y: 2, z: 4, core: 2. Of those that a mesh axis runs over, the one named last changes fastest.
Arguments:
- context: bfloat16 [4096, 3072], P(('island', 'fsdp'), 'tp'), may hold values from -6 to 6
- residual: bfloat16 [4096, 6144], P(('island', 'fsdp'), 'tp'), may hold values from -32 to 32
- cotangent: bfloat16 [4096, 6144], P(('island', 'fsdp'), 'tp'), may hold values from -8 to 8
- gain: bfloat16 [6144], replicated, may hold values from 0.5 to 1.5
- weight: bfloat16 [3072, 6144], P('tp', 'fsdp'), may hold values from -1 to 1
- first_moment: bfloat16 [4, 3072, 6144], P('island', 'tp', 'fsdp'), may hold values from -0.011962891 to 0.011962891
- second_moment: bfloat16 [4, 3072, 6144], P('island', 'tp', 'fsdp'), may hold values from 9.9651515e-08 to 9.983778e-07
- momentum: float32 [3072, 6144], P('tp', 'fsdp'), may hold values from -3 to 3
Outputs:
- new_momentum: float32 [3072, 6144], P('tp', 'fsdp')
- outer_step: bfloat16 [3072, 6144], P('tp', 'fsdp')
The draws below stay inside these ranges and needn't reach their ends.
All inputs are finite; a program needn't handle non-finite values.
Results may differ from the reference program's by a relative error of at most 0.014.
Values may be sent and summed in bfloat16 or wider, within the bound.
No kernel may reach another device: no remote copies, remote signals or barrier semaphores. Data moves between devices by JAX's collectives and lax.ppermute only.
A program may use at most 192 MiB of HBM per device.

```python
import math
import jax
import jax.numpy as jnp
from jax import lax

D = 6144
TOK_DEV = 256
HH = 3072
ISLANDS = 4
TOKENS = 4096
N_FSDP = 4
N_TP = 2


def shared_field(key):
    return jax.random.truncated_normal(key, -5.0, 5.0, (TOKENS, D), jnp.float32)


def column_profile(key):
    ramp = jnp.exp(jnp.linspace(math.log(0.5), math.log(1.5), D, dtype=jnp.float32))
    rough = jnp.exp(jax.random.uniform(key, (D,), jnp.float32, math.log(0.7), math.log(1.4)))
    return ramp * rough


def draw_residual(key, part):
    common = shared_field(key)
    key = jax.random.fold_in(key, 11)
    key_rows, key_cols = jax.random.split(key, 2)
    profile = column_profile(key_cols)
    base = common
    row_scale = jnp.exp(jax.random.uniform(key_rows, (TOKENS, 1), jnp.float32, math.log(0.2), math.log(2.0)))
    return (0.6 * base * row_scale * profile[None, :]).astype(jnp.bfloat16)


def draw_cotangent(key, part):
    common = shared_field(key)
    key = jax.random.fold_in(key, 23)
    noise = jax.random.truncated_normal(key, -5.0, 5.0, (TOKENS, D), jnp.float32)
    return (0.6 * noise + 0.8 * common).astype(jnp.bfloat16)


def draw_weight(key, part):
    key = jax.random.fold_in(key, 37)
    key_base, key_rows, key_dir, key_cols = jax.random.split(key, 4)
    profile = column_profile(key_cols)
    base = jax.random.truncated_normal(key_base, -5.0, 5.0, (HH, D), jnp.float32)
    strength = 0.8
    row_dir = jax.random.truncated_normal(key_rows, -3.0, 3.0, (HH, 1), jnp.float32)
    col_dir = jax.random.uniform(key_dir, (1, D), jnp.float32, -1.5, 1.5)
    values = (base + strength * row_dir * col_dir) * profile[None, :] / math.sqrt(HH)
    return jnp.clip(values, -1.0, 1.0).astype(jnp.bfloat16)


def shard_levels(own_key, extent, pieces, smallest, high):
    level = 1.0
    for axis_at, shards_of in pieces:
        steps = jax.random.uniform(jax.random.fold_in(jax.random.fold_in(own_key, 6), axis_at), (shards_of,), jnp.float32, smallest / len(pieces), high / len(pieces))
        level = level * jnp.repeat(jnp.exp(steps), extent[axis_at] // shards_of).reshape((-1,) + (1,) * (len(extent) - 1 - axis_at))
    return level


def bell_draw(stream_key, dims, spread, reach, cuts=(), kind=jnp.bfloat16):
    factor_of = shard_levels(stream_key, dims, cuts, -0.22, 0.18) if cuts else 1.0
    array = jax.random.normal(stream_key, dims, jnp.float32) * spread * factor_of
    return jnp.minimum(jnp.maximum(array, -reach), reach).astype(kind)


def setup_inputs(seed: int = 0) -> dict:
    seeds = jax.random.split(jax.random.key(seed), 9)
    return {
        "context": bell_draw(seeds[0], (TOKENS, HH), 1.0, 6.0, ((0, 16), (1, 2))),
        "residual": draw_residual(jax.random.fold_in(seeds[8], 71), 0),
        "cotangent": draw_cotangent(jax.random.fold_in(seeds[8], 71), 0),
        "gain": jnp.clip(1.0 + 0.1 * jax.random.normal(seeds[3], (D,), jnp.float32), 0.5, 1.5).astype(jnp.bfloat16),
        "weight": draw_weight(jax.random.fold_in(seeds[8], 71), 0),
        "first_moment": bell_draw(seeds[5], (ISLANDS, HH, D), 0.002, 0.011962891, ((0, 4), (1, 2), (2, 4))),
        "second_moment": jnp.clip(jnp.exp(math.log(9.98377799987793e-07) - 2.3044525 * jax.random.uniform(seeds[6], (ISLANDS, HH, D), jnp.float32) ** shard_levels(seeds[6], (ISLANDS, HH, D), ((0, 4), (1, 2), (2, 4)), -0.2, 0.2)), 9.96515154838562e-08, 9.98377799987793e-07).astype(jnp.bfloat16),
        "momentum": bell_draw(seeds[7], (HH, D), 0.5, 3.0, ((0, 2), (1, 4)), jnp.float32),
    }


norm_eps = 1e-06
adam_eps = 1e-08
beta_one = 0.9
beta_two = 0.999
bias_one = 1.0 - 0.9 ** 10
bias_two = 1.0 - 0.999 ** 10
decay_rate = 0.1
outer_mu = 0.9

def reference(context, residual, cotangent, gain, weight, first_moment, second_moment, momentum):
    group = HH // N_TP
    hidden = residual.astype(jnp.float32)
    for part in range(N_TP):
        cols = context[:, part * group:(part + 1) * group]
        rows = weight[part * group:(part + 1) * group, :]
        piece = jnp.dot(cols, rows, preferred_element_type=jnp.float32).astype(jnp.bfloat16)
        hidden = hidden + piece.astype(jnp.float32)
    inv_rms = lax.rsqrt(lax.optimization_barrier(jnp.mean(hidden * hidden, axis=-1, keepdims=True)) + norm_eps)
    weighted = gain.astype(jnp.float32)[None, :] * cotangent.astype(jnp.float32)
    row_dot = lax.optimization_barrier(jnp.sum(hidden * weighted, axis=-1, keepdims=True))
    d_hidden = (weighted * inv_rms - hidden * inv_rms ** 3 * row_dot / D).astype(jnp.bfloat16)
    ctx_blocks = context.reshape(ISLANDS, N_FSDP, TOK_DEV, HH)
    grad_blocks = d_hidden.reshape(ISLANDS, N_FSDP, TOK_DEV, D)
    weight_f = weight.astype(jnp.float32)

    def island_step(items):
        ctx_isl, grad_isl, first, second = items

        def add_term(total, pair):
            term = jnp.dot(pair[0].T, pair[1], preferred_element_type=jnp.float32).astype(jnp.bfloat16)
            term = lax.optimization_barrier(term)
            return (total + term.astype(jnp.float32), None)
        start = jnp.zeros((HH, D), jnp.float32)
        total, unused = lax.scan(add_term, start, (ctx_isl, grad_isl))
        grad = total / (TOK_DEV * N_FSDP)
        m_new = beta_one * first.astype(jnp.float32) + (1.0 - beta_one) * grad
        v_new = beta_two * second.astype(jnp.float32) + (1.0 - beta_two) * grad * grad
        update = m_new / bias_one / (jnp.sqrt(v_new / bias_two) + adam_eps) + decay_rate * weight_f
        return update.astype(jnp.bfloat16)
    pseudo = lax.map(island_step, (ctx_blocks, grad_blocks, first_moment, second_moment))
    pseudo = lax.optimization_barrier(pseudo)
    delta = lax.optimization_barrier(jnp.mean(pseudo.astype(jnp.float32), axis=0))
    new_momentum = outer_mu * momentum + delta
    outer_step = (delta + outer_mu * new_momentum).astype(jnp.bfloat16)
    return (new_momentum, outer_step)
```

```python
import jax
import jax.numpy as jnp
from jax import lax
from jax.sharding import PartitionSpec as P

norm_eps = 1e-06
adam_eps = 1e-08
beta_one = 0.9
beta_two = 0.999
bias_one = 1.0 - 0.9**10
bias_two = 1.0 - 0.999**10
decay_rate = 0.1
outer_mu = 0.9

f32 = jnp.float32
bf16 = jnp.bfloat16


def outer_update(delta, momentum):
    new_momentum = outer_mu * momentum + delta
    outer_step = (delta + outer_mu * new_momentum).astype(bf16)
    return (new_momentum, outer_step)


def swap(value, axis, bit):
    count = lax.axis_size(axis)
    return lax.ppermute(value, axis, [(i, i ^ bit) for i in range(count)])


def island_sum(value):
    count = lax.axis_size("island")
    half = count // 2
    me = lax.axis_index("island")
    held = value
    for hop in range(half - 1):
        pairs = [(hop, hop + 1), (count - 1 - hop, count - 2 - hop)]
        came = lax.ppermute(held, "island", pairs)
        held = (came.astype(f32) + value.astype(f32)).astype(bf16)
    came = lax.ppermute(held, "island", [(half - 1, half), (half, half - 1)])
    total = (held.astype(f32) + came.astype(f32)).astype(bf16)
    for hop in range(half - 1):
        inner, outer = half - 1 - hop, half - 2 - hop
        pairs = [(inner, outer), (count - 1 - inner, count - 1 - outer)]
        came = lax.ppermute(total, "island", pairs)
        total = jnp.where((me == outer) | (me == count - 1 - outer), came, total)
    return total


def body(context, residual, cotangent, gain, weight, first_moment, second_moment, momentum):
    tok_rows = context.shape[0]
    width = gain.shape[0]
    fsdp_count = lax.axis_size("fsdp")
    group = fsdp_count // 2
    cols = weight.shape[1]
    t = lax.axis_index("tp")
    f = lax.axis_index("fsdp")
    high = f // group
    low = f % group
    near = t == high

    blocks = {0: context}
    bit = group
    while bit:
        for delta in sorted(blocks):
            blocks[delta ^ bit] = swap(blocks[delta], "fsdp", bit)
        bit //= 2

    def regroup(array):
        parts = []
        for r in range(group):
            part = lax.dynamic_slice_in_dim(array, (low ^ r) * cols, cols, axis=1)
            parts.append(swap(part, "fsdp", r) if r else part)
        return parts

    residual_parts = regroup(residual)
    cotangent_parts = regroup(cotangent)
    gain_part = lax.dynamic_slice_in_dim(gain, t * (width // 2) + low * cols, cols).astype(f32)

    def project(block):
        return jnp.dot(block, weight, preferred_element_type=f32).astype(bf16)

    hidden, weighted, sums = [], [], []
    for r in range(group):
        far_out = swap(project(blocks[group ^ r]), "fsdp", group)
        own_out = project(blocks[r])
        keep = jnp.where(near, own_out, far_out)
        came = swap(jnp.where(near, far_out, own_out), "tp", 1)
        h = residual_parts[r].astype(f32) + keep.astype(f32) + came.astype(f32)
        w = gain_part[None, :] * cotangent_parts[r].astype(f32)
        hidden.append(h)
        weighted.append(w)
        sums.append(jnp.stack([jnp.sum(h * h, axis=-1), jnp.sum(h * w, axis=-1)]))
    own_sums = jnp.concatenate(sums, axis=1)
    totals = own_sums
    for r in range(1, group):
        came = swap(own_sums, "fsdp", r)
        order = [r ^ k for k in range(group)]
        came = jnp.concatenate(
            [came[:, k * tok_rows : (k + 1) * tok_rows] for k in order], axis=1
        )
        totals = totals + came
    totals = totals + swap(totals, "tp", 1)
    inv_rms = lax.rsqrt(totals[0] / width + norm_eps)
    pull = inv_rms**3 * totals[1] / width

    tokens = [blocks[r] for r in range(group)] + [blocks[group ^ r] for r in range(group)]
    context_all = jnp.concatenate(tokens, axis=0)
    chunks = 6
    step = cols // chunks
    momentum_out, step_out = [], []
    for c in range(chunks):
        lo = c * step
        d_local = jnp.concatenate(
            [
                weighted[r][:, lo : lo + step] * inv_rms[r * tok_rows : (r + 1) * tok_rows, None]
                - hidden[r][:, lo : lo + step] * pull[r * tok_rows : (r + 1) * tok_rows, None]
                for r in range(group)
            ],
            axis=0,
        ).astype(bf16)
        came = swap(d_local, "tp", 1)
        d_own = jnp.where(near, d_local, came)
        d_far = swap(jnp.where(near, came, d_local), "fsdp", group)
        d_all = jnp.concatenate([d_own, d_far], axis=0)
        grad = lax.dot_general(
            context_all, d_all, (((0,), (0,)), ((), ())), preferred_element_type=f32
        ) / (tok_rows * fsdp_count)
        first = first_moment[0, :, lo : lo + step].astype(f32)
        second = second_moment[0, :, lo : lo + step].astype(f32)
        m_new = beta_one * first + (1.0 - beta_one) * grad
        v_new = beta_two * second + (1.0 - beta_two) * grad * grad
        update = m_new / bias_one / (
            jnp.sqrt(v_new / bias_two) + adam_eps
        ) + decay_rate * weight[:, lo : lo + step].astype(f32)
        pseudo = update.astype(bf16)
        half = pseudo.shape[0] // 2
        total = jnp.concatenate([island_sum(pseudo[:half]), island_sum(pseudo[half:])], axis=0)
        delta = total.astype(f32) / lax.axis_size("island")
        new_momentum, outer_step = outer_update(delta, momentum[:, lo : lo + step])
        momentum_out.append(new_momentum)
        step_out.append(outer_step)
    return (jnp.concatenate(momentum_out, axis=1), jnp.concatenate(step_out, axis=1))


def solution(mesh):
    in_specs = (
        P(("island", "fsdp"), "tp"),
        P(("island", "fsdp"), "tp"),
        P(("island", "fsdp"), "tp"),
        P(),
        P("tp", "fsdp"),
        P("island", "tp", "fsdp"),
        P("island", "tp", "fsdp"),
        P("tp", "fsdp"),
    )
    out_specs = (P("tp", "fsdp"), P("tp", "fsdp"))
    return jax.shard_map(body, mesh=mesh, in_specs=in_specs, out_specs=out_specs, check_vma=False)
```

```python
import jax
import jax.numpy as jnp
from jax import lax
from jax.sharding import PartitionSpec as P

norm_eps = 1e-06
adam_eps = 1e-08
beta_one = 0.9
beta_two = 0.999
bias_one = 1.0 - 0.9**10
bias_two = 1.0 - 0.999**10
decay_rate = 0.1
outer_mu = 0.9

f32 = jnp.float32
bf16 = jnp.bfloat16


def outer_update(delta, momentum):
    new_momentum = outer_mu * momentum + delta
    outer_step = (delta + outer_mu * new_momentum).astype(bf16)
    return (new_momentum, outer_step)


def swap(value, axis, bit):
    count = lax.axis_size(axis)
    return lax.ppermute(value, axis, [(i, i ^ bit) for i in range(count)])


def tie(value, *others):
    return lax.optimization_barrier((value,) + others)[0]


class IslandLine:
    def __init__(self, total_chunks):
        self.n = lax.axis_size("island")
        self.me = lax.axis_index("island")
        self.chunks = total_chunks
        self.parts = []
        self.sent = ([], [])
        self.came = ([], [])

    def pick(self, choices):
        items = sorted(choices.items())
        value = items[-1][1]
        for at, other in reversed(items[:-1]):
            value = jnp.where(self.me == at, other, value)
        return value

    def stage(self):
        s = len(self.sent[0])
        n, half = self.n, self.n // 2
        fresh = []
        for way in (0, 1):
            choices = {}
            for i in range(n - 1):
                at = i if way == 0 else n - 1 - i
                k = s - i
                if not 0 <= k < self.chunks:
                    continue
                if i == 0:
                    value = self.parts[k]
                elif i < half:
                    value = (self.came[way][-1].astype(f32) + self.parts[k].astype(f32)).astype(bf16)
                elif i == half:
                    value = self.came[way][-1].astype(f32) + self.sent[1 - way][-1].astype(f32)
                    value = value.astype(bf16)
                else:
                    value = self.came[way][-1]
                choices[at] = value
            fresh.append((self.pick(choices), sorted(choices)))
        for way in (0, 1):
            value, sources = fresh[way]
            move = 1 if way == 0 else -1
            self.sent[way].append(value)
            self.came[way].append(lax.ppermute(value, "island", [(i, i + move) for i in sources]))

    def add(self, part):
        self.parts.append(part)
        self.stage()

    def total(self, k):
        n, half = self.n, self.n // 2
        choices = {0: self.came[1][k + n - 2], n - 1: self.came[0][k + n - 2]}
        for i in range(1, n - 1):
            choices[i] = self.sent[1][k + n - 1 - i] if i < half else self.sent[0][k + i]
        return self.pick(choices)


def body(context, residual, cotangent, gain, weight, first_moment, second_moment, momentum):
    tok_rows = context.shape[0]
    width = gain.shape[0]
    fsdp_count = lax.axis_size("fsdp")
    group = fsdp_count // 2
    cols = weight.shape[1]
    t = lax.axis_index("tp")
    f = lax.axis_index("fsdp")
    high = f // group
    low = f % group
    near = t == high

    pieces = 2
    rows = tok_rows // pieces

    def regroup(array):
        parts = []
        for r in range(group):
            part = lax.dynamic_slice_in_dim(array, (low ^ r) * cols, cols, axis=1)
            parts.append(swap(part, "fsdp", r) if r else part)
        return parts

    def project(block):
        return lax.optimization_barrier(
            jnp.dot(block, weight, preferred_element_type=f32).astype(bf16)
        )

    far_zero = [
        swap(context[p * rows : (p + 1) * rows], "fsdp", group) for p in range(pieces)
    ]
    near_blocks = [context] + [swap(context, "fsdp", r) for r in range(1, group)]
    near_out = [project(block) for block in near_blocks]
    far_zero[0] = tie(far_zero[0], *near_out)
    far_pieces = [far_zero]
    for r in range(1, group):
        far_pieces.append([swap(piece, "fsdp", r) for piece in far_zero])

    residual_parts = regroup(residual)
    cotangent_parts = regroup(cotangent)
    gain_part = lax.dynamic_slice_in_dim(gain, t * (width // 2) + low * cols, cols).astype(f32)

    hidden, weighted, sums = [], [], []
    for r in range(group):
        for p in range(pieces):
            span = slice(p * rows, (p + 1) * rows)
            far_out = swap(project(far_pieces[r][p]), "fsdp", group)
            own_out = near_out[r][span]
            keep = jnp.where(near, own_out, far_out)
            came = swap(jnp.where(near, far_out, own_out), "tp", 1)
            h = residual_parts[r][span].astype(f32) + keep.astype(f32) + came.astype(f32)
            w = gain_part[None, :] * cotangent_parts[r][span].astype(f32)
            hidden.append(h)
            weighted.append(w)
            sums.append(jnp.stack([jnp.sum(h * h, axis=-1), jnp.sum(h * w, axis=-1)]))
    own_sums = jnp.concatenate(sums, axis=1)
    totals = own_sums
    for r in range(1, group):
        came = swap(own_sums, "fsdp", r)
        order = [r ^ k for k in range(group)]
        came = jnp.concatenate(
            [came[:, k * tok_rows : (k + 1) * tok_rows] for k in order], axis=1
        )
        totals = totals + came
    totals = totals + swap(totals, "tp", 1)
    inv_rms = lax.rsqrt(totals[0] / width + norm_eps)
    pull = inv_rms**3 * totals[1] / width

    tokens = near_blocks + [piece for block in far_pieces for piece in block]
    context_all = jnp.concatenate(tokens, axis=0)
    chunks = 6
    cuts = 3
    step = cols // chunks
    high_rows = weight.shape[0] // cuts
    streams = 2
    order = [(c, q) for c in range(chunks) for q in range(cuts)]
    lines = [IslandLine(len(order[k::streams])) for k in range(streams)]
    pseudos = []
    for c in range(chunks):
        cols_at = slice(c * step, (c + 1) * step)
        d_local = jnp.concatenate(
            [
                weighted[k][:, cols_at] * inv_rms[k * rows : (k + 1) * rows, None]
                - hidden[k][:, cols_at] * pull[k * rows : (k + 1) * rows, None]
                for k in range(group * pieces)
            ],
            axis=0,
        ).astype(bf16)
        if c >= 2:
            d_local = tie(d_local, pseudos[c - 2])
        came = swap(d_local, "tp", 1)
        d_own = jnp.where(near, d_local, came)
        d_far = swap(jnp.where(near, came, d_local), "fsdp", group)
        d_all = jnp.concatenate([d_own, d_far], axis=0)
        grad = lax.dot_general(
            context_all, d_all, (((0,), (0,)), ((), ())), preferred_element_type=f32
        ) / (tok_rows * fsdp_count)
        first = first_moment[0, :, cols_at].astype(f32)
        second = second_moment[0, :, cols_at].astype(f32)
        m_new = beta_one * first + (1.0 - beta_one) * grad
        v_new = beta_two * second + (1.0 - beta_two) * grad * grad
        update = m_new / bias_one / (
            jnp.sqrt(v_new / bias_two) + adam_eps
        ) + decay_rate * weight[:, cols_at].astype(f32)
        pseudos.append(lax.optimization_barrier(update.astype(bf16)))
        for q in range(cuts):
            k = c * cuts + q
            lines[k % streams].add(pseudos[c][q * high_rows : (q + 1) * high_rows])
    for line in lines * (lines[0].n - 2):
        line.stage()
    momentum_out, step_out = [], []
    for c in range(chunks):
        cols_at = slice(c * step, (c + 1) * step)
        total = jnp.concatenate(
            [lines[k % streams].total(k // streams) for k in range(c * cuts, (c + 1) * cuts)],
            axis=0,
        )
        delta = total.astype(f32) / lax.axis_size("island")
        new_momentum, outer_step = outer_update(delta, momentum[:, cols_at])
        momentum_out.append(new_momentum)
        step_out.append(outer_step)
    return (jnp.concatenate(momentum_out, axis=1), jnp.concatenate(step_out, axis=1))


def solution(mesh):
    in_specs = (
        P(("island", "fsdp"), "tp"),
        P(("island", "fsdp"), "tp"),
        P(("island", "fsdp"), "tp"),
        P(),
        P("tp", "fsdp"),
        P("island", "tp", "fsdp"),
        P("island", "tp", "fsdp"),
        P("tp", "fsdp"),
    )
    out_specs = (P("tp", "fsdp"), P("tp", "fsdp"))
    return jax.shard_map(body, mesh=mesh, in_specs=in_specs, out_specs=out_specs, check_vma=False)
```

```python
import jax
import jax.numpy as jnp
from jax import lax
from jax.sharding import PartitionSpec as P

norm_eps = 1e-06
adam_eps = 1e-08
beta_one = 0.9
beta_two = 0.999
bias_one = 1.0 - 0.9**10
bias_two = 1.0 - 0.999**10
decay_rate = 0.1
outer_mu = 0.9

f32 = jnp.float32
bf16 = jnp.bfloat16


def outer_update(delta, momentum):
    new_momentum = outer_mu * momentum + delta
    outer_step = (delta + outer_mu * new_momentum).astype(bf16)
    return (new_momentum, outer_step)


def swap(value, axis, bit):
    count = lax.axis_size(axis)
    return lax.ppermute(value, axis, [(i, i ^ bit) for i in range(count)])


def tie(value, *others):
    return lax.optimization_barrier((value,) + others)[0]


class IslandLine:
    def __init__(self, total_chunks):
        self.n = lax.axis_size("island")
        self.me = lax.axis_index("island")
        self.chunks = total_chunks
        self.parts = []
        self.sent = ([], [])
        self.came = ([], [])

    def pick(self, choices):
        items = sorted(choices.items())
        value = items[-1][1]
        for at, other in reversed(items[:-1]):
            value = jnp.where(self.me == at, other, value)
        return value

    def stage(self):
        s = len(self.sent[0])
        n, half = self.n, self.n // 2
        used = [k for k in range(s - half + 1, s + 1) if 0 <= k < self.chunks]
        last = [] if s == 0 else [self.came[0][-1], self.came[1][-1], self.sent[0][-1], self.sent[1][-1]]
        held = lax.optimization_barrier(tuple(last + [self.parts[k] for k in used]))
        came, sent = held[:2], held[2:4]
        parts = dict(zip(used, held[len(last) :]))
        fresh = []
        for way in (0, 1):
            choices = {}
            for i in range(n - 1):
                at = i if way == 0 else n - 1 - i
                k = s - i
                if not 0 <= k < self.chunks:
                    continue
                if i == 0:
                    value = parts[k]
                elif i < half:
                    value = (came[way].astype(f32) + parts[k].astype(f32)).astype(bf16)
                elif i == half:
                    value = (came[way].astype(f32) + sent[1 - way].astype(f32)).astype(bf16)
                else:
                    value = came[way]
                choices[at] = value
            fresh.append((self.pick(choices), sorted(choices)))
        for way in (0, 1):
            value, sources = fresh[way]
            move = 1 if way == 0 else -1
            self.sent[way].append(value)
            self.came[way].append(lax.ppermute(value, "island", [(i, i + move) for i in sources]))

    def add(self, part):
        self.parts.append(part)
        self.stage()

    def total(self, k):
        n, half = self.n, self.n // 2
        choices = {0: self.came[1][k + n - 2], n - 1: self.came[0][k + n - 2]}
        for i in range(1, n - 1):
            choices[i] = self.sent[1][k + n - 1 - i] if i < half else self.sent[0][k + i]
        spots = sorted(choices)
        return self.pick(dict(zip(spots, lax.optimization_barrier(tuple(choices[i] for i in spots)))))


def body(context, residual, cotangent, gain, weight, first_moment, second_moment, momentum):
    tok_rows = context.shape[0]
    width = gain.shape[0]
    fsdp_count = lax.axis_size("fsdp")
    group = fsdp_count // 2
    cols = weight.shape[1]
    t = lax.axis_index("tp")
    f = lax.axis_index("fsdp")
    high = f // group
    low = f % group
    near = t == high

    pieces = 2
    rows = tok_rows // pieces

    def regroup(array):
        parts = []
        for r in range(group):
            part = lax.dynamic_slice_in_dim(array, (low ^ r) * cols, cols, axis=1)
            parts.append(swap(part, "fsdp", r) if r else part)
        return parts

    def project(block):
        return lax.optimization_barrier(
            jnp.dot(block, weight, preferred_element_type=f32).astype(bf16)
        )

    far_zero = [
        swap(context[p * rows : (p + 1) * rows], "fsdp", group) for p in range(pieces)
    ]
    near_blocks = [context] + [swap(context, "fsdp", r) for r in range(1, group)]
    near_out = [project(block) for block in near_blocks]
    far_zero[0] = tie(far_zero[0], *near_out)
    far_pieces = [far_zero]
    for r in range(1, group):
        far_pieces.append([swap(piece, "fsdp", r) for piece in far_zero])

    residual_parts = regroup(residual)
    cotangent_parts = regroup(cotangent)
    gain_part = lax.dynamic_slice_in_dim(gain, t * (width // 2) + low * cols, cols).astype(f32)

    hidden, weighted, sums = [], [], []
    for r in range(group):
        for p in range(pieces):
            span = slice(p * rows, (p + 1) * rows)
            far_out = swap(project(far_pieces[r][p]), "fsdp", group)
            far_out, own_out = lax.optimization_barrier((far_out, near_out[r]))
            own_out = own_out[span]
            keep = jnp.where(near, own_out, far_out)
            came = swap(jnp.where(near, far_out, own_out), "tp", 1)
            keep, came, res, cot = lax.optimization_barrier(
                (keep, came, residual_parts[r], cotangent_parts[r])
            )
            h = res[span].astype(f32) + keep.astype(f32) + came.astype(f32)
            w = gain_part[None, :] * cot[span].astype(f32)
            hidden.append(h)
            weighted.append(w)
            sums.append(jnp.stack([jnp.sum(h * h, axis=-1), jnp.sum(h * w, axis=-1)]))
    own_sums = jnp.concatenate(sums, axis=1)
    totals = own_sums
    for r in range(1, group):
        came = swap(own_sums, "fsdp", r)
        order = [r ^ k for k in range(group)]
        came = jnp.concatenate(
            [came[:, k * tok_rows : (k + 1) * tok_rows] for k in order], axis=1
        )
        totals = totals + came
    totals = totals + swap(totals, "tp", 1)
    inv_rms = lax.rsqrt(totals[0] / width + norm_eps)
    pull = inv_rms**3 * totals[1] / width

    tokens = near_blocks + [piece for block in far_pieces for piece in block]
    context_all = jnp.concatenate(tokens, axis=0)
    narrow = 128
    widths = [1, 1] + [2] * ((cols // narrow - 2) // 2)
    streams = 2
    chunk_count = sum(widths)
    lines = [IslandLine(len(range(k, chunk_count, streams))) for k in range(streams)]
    pseudos, arrivals = [], []
    k = 0
    for c, units in enumerate(widths):
        cols_at = slice(k * narrow, (k + units) * narrow)
        d_local = jnp.concatenate(
            [
                weighted[j][:, cols_at] * inv_rms[j * rows : (j + 1) * rows, None]
                - hidden[j][:, cols_at] * pull[j * rows : (j + 1) * rows, None]
                for j in range(group * pieces)
            ],
            axis=0,
        ).astype(bf16)
        if c == 2:
            d_local = tie(d_local, arrivals[0])
        elif c > 2:
            d_local = tie(d_local, pseudos[c - 2])
        came = swap(d_local, "tp", 1)
        arrivals.append(came)
        d_own = jnp.where(near, d_local, came)
        d_far = swap(jnp.where(near, came, d_local), "fsdp", group)
        d_all = jnp.concatenate([d_own, d_far], axis=0)
        grad = lax.dot_general(
            context_all, d_all, (((0,), (0,)), ((), ())), preferred_element_type=f32
        ) / (tok_rows * fsdp_count)
        first = first_moment[0, :, cols_at].astype(f32)
        second = second_moment[0, :, cols_at].astype(f32)
        m_new = beta_one * first + (1.0 - beta_one) * grad
        v_new = beta_two * second + (1.0 - beta_two) * grad * grad
        update = m_new / bias_one / (
            jnp.sqrt(v_new / bias_two) + adam_eps
        ) + decay_rate * weight[:, cols_at].astype(f32)
        pseudos.append(lax.optimization_barrier(update.astype(bf16)))
        for u in range(units):
            lines[k % streams].add(pseudos[c][:, u * narrow : (u + 1) * narrow])
            k += 1
    for line in lines * (lines[0].n - 2):
        line.stage()
    momentum_out, step_out = [], []
    for k in range(chunk_count):
        cols_at = slice(k * narrow, (k + 1) * narrow)
        total = lines[k % streams].total(k // streams)
        delta = total.astype(f32) / lax.axis_size("island")
        new_momentum, outer_step = outer_update(delta, momentum[:, cols_at])
        momentum_out.append(new_momentum)
        step_out.append(outer_step)
    return (jnp.concatenate(momentum_out, axis=1), jnp.concatenate(step_out, axis=1))


def solution(mesh):
    in_specs = (
        P(("island", "fsdp"), "tp"),
        P(("island", "fsdp"), "tp"),
        P(("island", "fsdp"), "tp"),
        P(),
        P("tp", "fsdp"),
        P("island", "tp", "fsdp"),
        P("island", "tp", "fsdp"),
        P("tp", "fsdp"),
    )
    out_specs = (P("tp", "fsdp"), P("tp", "fsdp"))
    return jax.shard_map(body, mesh=mesh, in_specs=in_specs, out_specs=out_specs, check_vma=False)
```

```python
import jax
import jax.numpy as jnp
from jax import lax
from jax.sharding import PartitionSpec as P

norm_eps = 1e-06
adam_eps = 1e-08
beta_one = 0.9
beta_two = 0.999
bias_one = 1.0 - 0.9**10
bias_two = 1.0 - 0.999**10
decay_rate = 0.1
outer_mu = 0.9

f32 = jnp.float32
bf16 = jnp.bfloat16


def outer_update(delta, momentum):
    new_momentum = outer_mu * momentum + delta
    outer_step = (delta + outer_mu * new_momentum).astype(bf16)
    return (new_momentum, outer_step)


def swap(value, axis, bit):
    count = lax.axis_size(axis)
    return lax.ppermute(value, axis, [(i, i ^ bit) for i in range(count)])


def tie(value, *others):
    return lax.optimization_barrier((value,) + others)[0]


class IslandLine:
    def __init__(self, total_chunks):
        self.n = lax.axis_size("island")
        self.me = lax.axis_index("island")
        self.chunks = total_chunks
        self.parts = []
        self.sent = ([], [])
        self.came = ([], [])

    def pick(self, choices):
        items = sorted(choices.items())
        value = items[-1][1]
        for at, other in reversed(items[:-1]):
            value = jnp.where(self.me == at, other, value)
        return value

    def stage(self):
        s = len(self.sent[0])
        n, half = self.n, self.n // 2
        used = [k for k in range(s - half + 1, s + 1) if 0 <= k < self.chunks]
        last = [] if s == 0 else [self.came[0][-1], self.came[1][-1], self.sent[0][-1], self.sent[1][-1]]
        held = lax.optimization_barrier(tuple(last + [self.parts[k] for k in used]))
        came, sent = held[:2], held[2:4]
        parts = dict(zip(used, held[len(last) :]))
        fresh = []
        for way in (0, 1):
            choices = {}
            for i in range(n - 1):
                at = i if way == 0 else n - 1 - i
                k = s - i
                if not 0 <= k < self.chunks:
                    continue
                if i == 0:
                    value = parts[k]
                elif i < half:
                    value = (came[way].astype(f32) + parts[k].astype(f32)).astype(bf16)
                elif i == half:
                    value = (came[way].astype(f32) + sent[1 - way].astype(f32)).astype(bf16)
                else:
                    value = came[way]
                choices[at] = value
            fresh.append((self.pick(choices), sorted(choices)))
        for way in (0, 1):
            value, sources = fresh[way]
            move = 1 if way == 0 else -1
            self.sent[way].append(value)
            self.came[way].append(lax.ppermute(value, "island", [(i, i + move) for i in sources]))

    def add(self, part):
        self.parts.append(part)
        self.stage()

    def total(self, k):
        n, half = self.n, self.n // 2
        choices = {0: self.came[1][k + n - 2], n - 1: self.came[0][k + n - 2]}
        for i in range(1, n - 1):
            choices[i] = self.sent[1][k + n - 1 - i] if i < half else self.sent[0][k + i]
        spots = sorted(choices)
        return self.pick(dict(zip(spots, lax.optimization_barrier(tuple(choices[i] for i in spots)))))


def body(context, residual, cotangent, gain, weight, first_moment, second_moment, momentum):
    tok_rows = context.shape[0]
    width = gain.shape[0]
    fsdp_count = lax.axis_size("fsdp")
    group = fsdp_count // 2
    cols = weight.shape[1]
    t = lax.axis_index("tp")
    f = lax.axis_index("fsdp")
    high = f // group
    low = f % group
    near = t == high

    pieces = 2
    rows = tok_rows // pieces

    def regroup(array):
        parts = []
        for r in range(group):
            part = lax.dynamic_slice_in_dim(array, (low ^ r) * cols, cols, axis=1)
            parts.append(swap(part, "fsdp", r) if r else part)
        return parts

    def project(block):
        return lax.optimization_barrier(
            jnp.dot(block, weight, preferred_element_type=f32).astype(bf16)
        )

    far_pieces = [[swap(context[p * rows : (p + 1) * rows], "fsdp", group) for p in range(pieces)]]
    near_blocks = [context] + [swap(context, "fsdp", r) for r in range(1, group)]
    for r in range(1, group):
        far_pieces.append([swap(piece, "fsdp", r) for piece in far_pieces[0]])
    near_out = [project(context)]
    issued = near_out[0]
    far_outs = []
    for r in range(group):
        for p in range(pieces):
            issued = project(tie(far_pieces[r][p], issued))
            far_outs.append(swap(issued, "fsdp", group))
        if r + 1 < group:
            near_out.append(project(tie(near_blocks[r + 1], issued)))
            issued = tie(issued, near_out[-1])

    residual_parts = regroup(residual)
    cotangent_parts = regroup(cotangent)
    gain_part = lax.dynamic_slice_in_dim(gain, t * (width // 2) + low * cols, cols).astype(f32)

    hidden, weighted, sums = [], [], []
    for r in range(group):
        for p in range(pieces):
            span = slice(p * rows, (p + 1) * rows)
            far_out, own_out, _ = lax.optimization_barrier(
                (far_outs[r * pieces + p], near_out[r], issued)
            )
            own_out = own_out[span]
            keep = jnp.where(near, own_out, far_out)
            came = swap(jnp.where(near, far_out, own_out), "tp", 1)
            keep, came, res, cot = lax.optimization_barrier(
                (keep, came, residual_parts[r], cotangent_parts[r])
            )
            h = res[span].astype(f32) + keep.astype(f32) + came.astype(f32)
            w = gain_part[None, :] * cot[span].astype(f32)
            hidden.append(h)
            weighted.append(w)
            sums.append(jnp.stack([jnp.sum(h * h, axis=-1), jnp.sum(h * w, axis=-1)]))
    own_sums = jnp.concatenate(sums, axis=1)
    totals = own_sums
    for r in range(1, group):
        came = swap(own_sums, "fsdp", r)
        order = [r ^ k for k in range(group)]
        came = jnp.concatenate(
            [came[:, k * tok_rows : (k + 1) * tok_rows] for k in order], axis=1
        )
        totals = totals + came
    totals = totals + swap(totals, "tp", 1)
    inv_rms = lax.rsqrt(totals[0] / width + norm_eps)
    pull = inv_rms**3 * totals[1] / width

    tokens = near_blocks + [piece for block in far_pieces for piece in block]
    context_all = jnp.concatenate(tokens, axis=0)
    narrow = 128
    units = cols // narrow
    widths = [1, 1, 2]
    while sum(widths) < units:
        widths.append(min(4, units - sum(widths)))
    unit_rows = weight.shape[0]
    chunk_rows = 1024 if units * unit_rows % 1024 == 0 else unit_rows
    chunk_count = units * unit_rows // chunk_rows
    streams = 2
    lines = [IslandLine(len(range(k, chunk_count, streams))) for k in range(streams)]

    def stretch(items, size, lo, hi):
        found = []
        for k in range(lo // size, -(-hi // size)):
            first, last = max(lo - k * size, 0), min(hi - k * size, size)
            found.append(items[k][first:last])
        return found[0] if len(found) == 1 else jnp.concatenate(found, axis=0)

    parts = []
    added = 0
    pseudos, arrivals = [], []
    k = 0
    for c, wide in enumerate(widths):
        cols_at = slice(k * narrow, (k + wide) * narrow)
        d_local = jnp.concatenate(
            [
                weighted[j][:, cols_at] * inv_rms[j * rows : (j + 1) * rows, None]
                - hidden[j][:, cols_at] * pull[j * rows : (j + 1) * rows, None]
                for j in range(group * pieces)
            ],
            axis=0,
        ).astype(bf16)
        if c in (2, 3):
            d_local = tie(d_local, arrivals[c - 2 if c == 2 else 2])
        elif c > 3:
            d_local = tie(d_local, pseudos[c - 2])
        came = swap(d_local, "tp", 1)
        if c:
            came = tie(came, d_sent)
        arrivals.append(came)
        d_own = jnp.where(near, d_local, came)
        d_sent = jnp.where(near, came, d_local)
        d_far = swap(d_sent, "fsdp", group)
        d_all = jnp.concatenate([d_own, d_far], axis=0)
        grad = lax.dot_general(
            context_all, d_all, (((0,), (0,)), ((), ())), preferred_element_type=f32
        ) / (tok_rows * fsdp_count)
        first = first_moment[0, :, cols_at].astype(f32)
        second = second_moment[0, :, cols_at].astype(f32)
        m_new = beta_one * first + (1.0 - beta_one) * grad
        v_new = beta_two * second + (1.0 - beta_two) * grad * grad
        update = m_new / bias_one / (
            jnp.sqrt(v_new / bias_two) + adam_eps
        ) + decay_rate * weight[:, cols_at].astype(f32)
        pseudos.append(lax.optimization_barrier(update.astype(bf16)))
        parts += [pseudos[c][:, u * narrow : (u + 1) * narrow] for u in range(wide)]
        k += wide
        while (added + 1) * chunk_rows <= len(parts) * unit_rows:
            part = stretch(parts, unit_rows, added * chunk_rows, (added + 1) * chunk_rows)
            lines[added % streams].add(part)
            added += 1
    for line in lines * (lines[0].n - 2):
        line.stage()
    totals = [lines[k % streams].total(k // streams) for k in range(chunk_count)]
    momentum_out, step_out = [], []
    for k in range(units):
        cols_at = slice(k * narrow, (k + 1) * narrow)
        total = stretch(totals, chunk_rows, k * unit_rows, (k + 1) * unit_rows)
        delta = total.astype(f32) / lax.axis_size("island")
        new_momentum, outer_step = outer_update(delta, momentum[:, cols_at])
        momentum_out.append(new_momentum)
        step_out.append(outer_step)
    return (jnp.concatenate(momentum_out, axis=1), jnp.concatenate(step_out, axis=1))


def solution(mesh):
    in_specs = (
        P(("island", "fsdp"), "tp"),
        P(("island", "fsdp"), "tp"),
        P(("island", "fsdp"), "tp"),
        P(),
        P("tp", "fsdp"),
        P("island", "tp", "fsdp"),
        P("island", "tp", "fsdp"),
        P("tp", "fsdp"),
    )
    out_specs = (P("tp", "fsdp"), P("tp", "fsdp"))
    return jax.shard_map(body, mesh=mesh, in_specs=in_specs, out_specs=out_specs, check_vma=False)
```

```python
import jax
import jax.numpy as jnp
from jax import lax
from jax.sharding import PartitionSpec as P

norm_eps = 1e-06
adam_eps = 1e-08
beta_one = 0.9
beta_two = 0.999
bias_one = 1.0 - 0.9**10
bias_two = 1.0 - 0.999**10
decay_rate = 0.1
outer_mu = 0.9

f32 = jnp.float32
bf16 = jnp.bfloat16


def outer_update(delta, momentum):
    new_momentum = outer_mu * momentum + delta
    outer_step = (delta + outer_mu * new_momentum).astype(bf16)
    return (new_momentum, outer_step)


def swap(value, axis, bit):
    count = lax.axis_size(axis)
    return lax.ppermute(value, axis, [(i, i ^ bit) for i in range(count)])


def tie(value, *others):
    return lax.optimization_barrier((value,) + others)[0]


class IslandLine:
    def __init__(self, total_chunks):
        self.n = lax.axis_size("island")
        self.me = lax.axis_index("island")
        self.chunks = total_chunks
        self.parts = []
        self.sent = ([], [])
        self.came = ([], [])

    def pick(self, choices):
        items = sorted(choices.items())
        value = items[-1][1]
        for at, other in reversed(items[:-1]):
            value = jnp.where(self.me == at, other, value)
        return value

    def stage(self):
        s = len(self.sent[0])
        n, half = self.n, self.n // 2
        used = [k for k in range(s - half + 1, s + 1) if 0 <= k < self.chunks]
        last = [] if s == 0 else [self.came[0][-1], self.came[1][-1], self.sent[0][-1], self.sent[1][-1]]
        held = lax.optimization_barrier(tuple(last + [self.parts[k] for k in used]))
        came, sent = held[:2], held[2:4]
        parts = dict(zip(used, held[len(last) :]))
        fresh = []
        for way in (0, 1):
            choices = {}
            for i in range(n - 1):
                at = i if way == 0 else n - 1 - i
                k = s - i
                if not 0 <= k < self.chunks:
                    continue
                if i == 0:
                    value = parts[k]
                elif i < half:
                    value = (came[way].astype(f32) + parts[k].astype(f32)).astype(bf16)
                elif i == half:
                    value = (came[way].astype(f32) + sent[1 - way].astype(f32)).astype(bf16)
                else:
                    value = came[way]
                choices[at] = value
            fresh.append((self.pick(choices), sorted(choices)))
        for way in (0, 1):
            value, sources = fresh[way]
            move = 1 if way == 0 else -1
            self.sent[way].append(value)
            self.came[way].append(lax.ppermute(value, "island", [(i, i + move) for i in sources]))

    def add(self, part):
        self.parts.append(part)
        self.stage()

    def total(self, k):
        n, half = self.n, self.n // 2
        choices = {0: self.came[1][k + n - 2], n - 1: self.came[0][k + n - 2]}
        for i in range(1, n - 1):
            choices[i] = self.sent[1][k + n - 1 - i] if i < half else self.sent[0][k + i]
        spots = sorted(choices)
        return self.pick(dict(zip(spots, lax.optimization_barrier(tuple(choices[i] for i in spots)))))


def body(context, residual, cotangent, gain, weight, first_moment, second_moment, momentum):
    tok_rows = context.shape[0]
    width = gain.shape[0]
    fsdp_count = lax.axis_size("fsdp")
    group = fsdp_count // 2
    cols = weight.shape[1]
    t = lax.axis_index("tp")
    f = lax.axis_index("fsdp")
    high = f // group
    low = f % group
    near = t == high

    pieces = 2
    rows = tok_rows // pieces

    def regroup(array):
        parts = []
        for r in range(group):
            part = lax.dynamic_slice_in_dim(array, (low ^ r) * cols, cols, axis=1)
            parts.append(swap(part, "fsdp", r) if r else part)
        return parts

    def project(block):
        return lax.optimization_barrier(
            jnp.dot(block, weight, preferred_element_type=f32).astype(bf16)
        )

    residual_parts = regroup(residual)
    cotangent_parts = regroup(cotangent)

    near_blocks = [context] + [swap(context, "fsdp", r) for r in range(1, group)]
    later = tie(context, residual_parts[0], cotangent_parts[0])
    far_pieces = [
        [
            swap((later if p else context)[p * rows : (p + 1) * rows], "fsdp", group)
            for p in range(pieces)
        ]
    ]
    for r in range(1, group):
        far_pieces.append([swap(piece, "fsdp", r) for piece in far_pieces[0]])
    near_out = [project(context)]
    issued = near_out[0]
    far_outs = []
    for r in range(group):
        for p in range(pieces):
            issued = project(tie(far_pieces[r][p], issued))
            far_outs.append(swap(issued, "fsdp", group))
        if r + 1 < group:
            near_out.append(project(tie(near_blocks[r + 1], issued)))
            issued = tie(near_out[-1], *residual_parts, *cotangent_parts)

    gain_part = lax.dynamic_slice_in_dim(gain, t * (width // 2) + low * cols, cols).astype(f32)

    hidden, weighted, sums = [], [], []
    for r in range(group):
        for p in range(pieces):
            span = slice(p * rows, (p + 1) * rows)
            far_out, own_out, _ = lax.optimization_barrier(
                (far_outs[r * pieces + p], near_out[r], issued)
            )
            own_out = own_out[span]
            keep = jnp.where(near, own_out, far_out)
            came = swap(jnp.where(near, far_out, own_out), "tp", 1)
            keep, came, res, cot = lax.optimization_barrier(
                (keep, came, residual_parts[r], cotangent_parts[r])
            )
            h = res[span].astype(f32) + keep.astype(f32) + came.astype(f32)
            w = gain_part[None, :] * cot[span].astype(f32)
            hidden.append(h)
            weighted.append(w)
            sums.append(jnp.stack([jnp.sum(h * h, axis=-1), jnp.sum(h * w, axis=-1)]))
    own_sums = jnp.concatenate(sums, axis=1)
    totals = own_sums
    for r in range(1, group):
        came = swap(own_sums, "fsdp", r)
        order = [r ^ k for k in range(group)]
        came = jnp.concatenate(
            [came[:, k * tok_rows : (k + 1) * tok_rows] for k in order], axis=1
        )
        totals = totals + came
    totals = totals + swap(totals, "tp", 1)
    inv_rms = lax.rsqrt(totals[0] / width + norm_eps)
    pull = inv_rms**3 * totals[1] / width

    tokens = near_blocks + [piece for block in far_pieces for piece in block]
    context_all = jnp.concatenate(tokens, axis=0)
    narrow = 128
    units = cols // narrow
    widths = [1, 1, 2]
    while sum(widths) < units:
        widths.append(min(4, units - sum(widths)))
    unit_rows = weight.shape[0]
    chunk_rows = 1024 if units * unit_rows % 1024 == 0 else unit_rows
    chunk_count = units * unit_rows // chunk_rows
    streams = 2
    lines = [IslandLine(len(range(k, chunk_count, streams))) for k in range(streams)]

    def stretch(items, size, lo, hi):
        found = []
        for k in range(lo // size, -(-hi // size)):
            first, last = max(lo - k * size, 0), min(hi - k * size, size)
            found.append(items[k][first:last])
        return found[0] if len(found) == 1 else jnp.concatenate(found, axis=0)

    def at(h, q, x):
        return (h * group + q) * 2 + x

    square_groups = [[at(h, q, x) for h in (0, 1) for x in (0, 1)] for q in range(group)]
    ring_pairs, cross_pairs = [], []
    for q in range(group):
        ring_pairs += [(at(x, q, x), at(x, q, 1 - x)) for x in (0, 1)]
        ring_pairs += [(at(1 - x, q, x), at(x, q, x)) for x in (0, 1)]
        cross_pairs += [(at(1 - x, q, x), at(x, q, 1 - x)) for x in (0, 1)]

    parts = []
    added = 0
    pseudos, arrivals = [], []
    k = 0
    for c, wide in enumerate(widths):
        cols_at = slice(k * narrow, (k + wide) * narrow)
        d_local = jnp.concatenate(
            [
                weighted[j][:, cols_at] * inv_rms[j * rows : (j + 1) * rows, None]
                - hidden[j][:, cols_at] * pull[j * rows : (j + 1) * rows, None]
                for j in range(group * pieces)
            ],
            axis=0,
        ).astype(bf16)
        if wide > 2:
            if len(arrivals) > 0:
                d_local = tie(d_local, arrivals[0])
            blocks = lax.all_gather(
                d_local, ("fsdp", "tp"), axis_index_groups=square_groups, axis=0, tiled=False
            )
            d_near = lax.dynamic_index_in_dim(blocks, 3 * high, 0, keepdims=False)
            d_far = lax.dynamic_index_in_dim(blocks, 2 - high, 0, keepdims=False)
        else:
            if c > 0:
                d_local = tie(d_local, arrivals[-1])
            ring = lax.ppermute(d_local, ("fsdp", "tp"), ring_pairs)
            cross = lax.ppermute(d_local, ("fsdp", "tp"), cross_pairs)
            arrivals.append(ring)
            d_near = jnp.where(near, d_local, ring)
            d_far = jnp.where(near, ring, cross)
        d_all = jnp.concatenate([d_near, d_far], axis=0)
        grad = lax.dot_general(
            context_all, d_all, (((0,), (0,)), ((), ())), preferred_element_type=f32
        ) / (tok_rows * fsdp_count)
        first = first_moment[0, :, cols_at].astype(f32)
        second = second_moment[0, :, cols_at].astype(f32)
        m_new = beta_one * first + (1.0 - beta_one) * grad
        v_new = beta_two * second + (1.0 - beta_two) * grad * grad
        update = m_new / bias_one / (
            jnp.sqrt(v_new / bias_two) + adam_eps
        ) + decay_rate * weight[:, cols_at].astype(f32)
        pseudos.append(lax.optimization_barrier(update.astype(bf16)))
        parts += [pseudos[c][:, u * narrow : (u + 1) * narrow] for u in range(wide)]
        k += wide
        while (added + 1) * chunk_rows <= len(parts) * unit_rows:
            part = stretch(parts, unit_rows, added * chunk_rows, (added + 1) * chunk_rows)
            lines[added % streams].add(part)
            added += 1
    for line in lines * (lines[0].n - 2):
        line.stage()
    totals = [lines[k % streams].total(k // streams) for k in range(chunk_count)]
    momentum_out, step_out = [], []
    for k in range(units):
        cols_at = slice(k * narrow, (k + 1) * narrow)
        total = stretch(totals, chunk_rows, k * unit_rows, (k + 1) * unit_rows)
        delta = total.astype(f32) / lax.axis_size("island")
        new_momentum, outer_step = outer_update(delta, momentum[:, cols_at])
        momentum_out.append(new_momentum)
        step_out.append(outer_step)
    return (jnp.concatenate(momentum_out, axis=1), jnp.concatenate(step_out, axis=1))


def solution(mesh):
    in_specs = (
        P(("island", "fsdp"), "tp"),
        P(("island", "fsdp"), "tp"),
        P(("island", "fsdp"), "tp"),
        P(),
        P("tp", "fsdp"),
        P("island", "tp", "fsdp"),
        P("island", "tp", "fsdp"),
        P("tp", "fsdp"),
    )
    out_specs = (P("tp", "fsdp"), P("tp", "fsdp"))
    return jax.shard_map(body, mesh=mesh, in_specs=in_specs, out_specs=out_specs, check_vma=False)
```

```python
import jax
import jax.numpy as jnp
from jax import lax
from jax.sharding import PartitionSpec as P

norm_eps = 1e-06
adam_eps = 1e-08
beta_one = 0.9
beta_two = 0.999
bias_one = 1.0 - 0.9**10
bias_two = 1.0 - 0.999**10
decay_rate = 0.1
outer_mu = 0.9

f32 = jnp.float32
bf16 = jnp.bfloat16


def outer_update(delta, momentum):
    new_momentum = outer_mu * momentum + delta
    outer_step = (delta + outer_mu * new_momentum).astype(bf16)
    return (new_momentum, outer_step)


def swap(value, axis, bit):
    count = lax.axis_size(axis)
    return lax.ppermute(value, axis, [(i, i ^ bit) for i in range(count)])


def tie(value, *others):
    for other in others:
        mark = other[(0,) * other.ndim]
        value = jnp.where(mark == mark, value, jnp.zeros_like(value))
    return value


def island_sums(values):
    count = lax.axis_size("island")
    half = count // 2
    me = lax.axis_index("island")
    passed = {}
    totals = []
    for j, value in enumerate(values):

        def send(payload, hop, pairs):
            passed[j, hop - 1] = payload
            if (j - 2, hop) in passed:
                payload = tie(payload, passed[j - 2, hop])
            return lax.ppermute(lax.optimization_barrier(payload), "island", pairs)

        held = value
        for hop in range(half - 1):
            came = send(held, hop, [(hop, hop + 1), (count - 1 - hop, count - 2 - hop)])
            held = (came.astype(f32) + value.astype(f32)).astype(bf16)
        came = send(held, half - 1, [(half - 1, half), (half, half - 1)])
        total = (held.astype(f32) + came.astype(f32)).astype(bf16)
        for step in range(half - 1):
            inner, outer = half - 1 - step, half - 2 - step
            pairs = [(inner, outer), (count - 1 - inner, count - 1 - outer)]
            came = send(total, half + step, pairs)
            total = jnp.where((me == outer) | (me == count - 1 - outer), came, total)
        total = lax.optimization_barrier(total)
        passed[j, 2 * half - 2] = total
        totals.append(total)
    return totals


def body(context, residual, cotangent, gain, weight, first_moment, second_moment, momentum):
    tok_rows = context.shape[0]
    width = gain.shape[0]
    fsdp_count = lax.axis_size("fsdp")
    group = fsdp_count // 2
    cols = weight.shape[1]
    t = lax.axis_index("tp")
    f = lax.axis_index("fsdp")
    high = f // group
    low = f % group
    near = t == high

    pieces = 2
    rows = tok_rows // pieces

    def regroup(array):
        parts = []
        for r in range(group):
            part = lax.dynamic_slice_in_dim(array, (low ^ r) * cols, cols, axis=1)
            parts.append(swap(part, "fsdp", r) if r else part)
        return parts

    def project(block):
        return lax.optimization_barrier(
            jnp.dot(block, weight, preferred_element_type=f32).astype(bf16)
        )

    residual_parts = regroup(residual)
    cotangent_parts = regroup(cotangent)

    near_blocks = [context] + [swap(context, "fsdp", r) for r in range(1, group)]
    far_pieces = [[swap(context[p * rows : (p + 1) * rows], "fsdp", group) for p in range(pieces)]]
    for r in range(1, group):
        far_pieces.append([swap(piece, "fsdp", r) for piece in far_pieces[0]])
    near_out = [project(block) for block in near_blocks]
    far_outs = []
    for r in range(group):
        for p in range(pieces):
            out = jnp.dot(far_pieces[r][p], weight, preferred_element_type=f32).astype(bf16)
            if r:
                out = tie(out, residual_parts[r], cotangent_parts[r], near_out[r])
            far_outs.append(swap(lax.optimization_barrier(out), "fsdp", group))

    gain_part = lax.dynamic_slice_in_dim(gain, t * (width // 2) + low * cols, cols).astype(f32)

    hidden, weighted, sums = [], [], []
    before = None
    for r in range(group):
        for p in range(pieces):
            span = slice(p * rows, (p + 1) * rows)
            far_out, own_out = lax.optimization_barrier((far_outs[r * pieces + p], near_out[r]))
            own_out = own_out[span]
            keep = jnp.where(near, own_out, far_out)
            sent = jnp.where(near, far_out, own_out)
            if before is not None:
                sent = tie(sent, before)
            before = sent
            came = swap(sent, "tp", 1)
            keep, came, res, cot = lax.optimization_barrier(
                (keep, came, residual_parts[r], cotangent_parts[r])
            )
            h = res[span].astype(f32) + keep.astype(f32) + came.astype(f32)
            w = gain_part[None, :] * cot[span].astype(f32)
            hidden.append(h)
            weighted.append(w)
            sums.append(jnp.stack([jnp.sum(h * h, axis=-1), jnp.sum(h * w, axis=-1)]))
    own_sums = jnp.concatenate(sums, axis=1)
    totals = own_sums
    for r in range(1, group):
        came = swap(own_sums, "fsdp", r)
        order = [r ^ k for k in range(group)]
        came = jnp.concatenate(
            [came[:, k * tok_rows : (k + 1) * tok_rows] for k in order], axis=1
        )
        totals = totals + came
    totals = totals + swap(totals, "tp", 1)
    inv_rms = lax.rsqrt(totals[0] / width + norm_eps)
    pull = inv_rms**3 * totals[1] / width

    tokens = near_blocks + [piece for block in far_pieces for piece in block]
    context_all = jnp.concatenate(tokens, axis=0)
    narrow = 128
    units = cols // narrow
    widths = [1, 1, 2]
    while sum(widths) < units:
        widths.append(min(4, units - sum(widths)))
    def at(h, q, x):
        return (h * group + q) * 2 + x

    ring_pairs, cross_pairs = [], []
    for q in range(group):
        ring_pairs += [(at(x, q, x), at(x, q, 1 - x)) for x in (0, 1)]
        ring_pairs += [(at(1 - x, q, x), at(x, q, x)) for x in (0, 1)]
        cross_pairs += [(at(1 - x, q, x), at(x, q, 1 - x)) for x in (0, 1)]

    parts = []
    pseudos, arrivals = [], []
    k = 0
    for c, wide in enumerate(widths):
        cols_at = slice(k * narrow, (k + wide) * narrow)
        d_local = jnp.concatenate(
            [
                weighted[j][:, cols_at] * inv_rms[j * rows : (j + 1) * rows, None]
                - hidden[j][:, cols_at] * pull[j * rows : (j + 1) * rows, None]
                for j in range(group * pieces)
            ],
            axis=0,
        ).astype(bf16)
        if c > 1:
            d_local = tie(d_local, arrivals[0 if c == 2 else c - 1])
        d_local = lax.optimization_barrier(d_local)
        ring = lax.ppermute(d_local, ("fsdp", "tp"), ring_pairs)
        cross = lax.ppermute(d_local, ("fsdp", "tp"), cross_pairs)
        arrivals.append(ring)
        d_near = jnp.where(near, d_local, ring)
        d_far = jnp.where(near, ring, cross)
        d_all = jnp.concatenate([d_near, d_far], axis=0)
        grad = lax.dot_general(
            context_all, d_all, (((0,), (0,)), ((), ())), preferred_element_type=f32
        ) / (tok_rows * fsdp_count)
        first = first_moment[0, :, cols_at].astype(f32)
        second = second_moment[0, :, cols_at].astype(f32)
        m_new = beta_one * first + (1.0 - beta_one) * grad
        v_new = beta_two * second + (1.0 - beta_two) * grad * grad
        update = m_new / bias_one / (
            jnp.sqrt(v_new / bias_two) + adam_eps
        ) + decay_rate * weight[:, cols_at].astype(f32)
        pseudos.append(lax.optimization_barrier(update.astype(bf16)))
        parts += [pseudos[c][:, u * narrow : (u + 1) * narrow] for u in range(wide)]
        k += wide
    momentum_out, step_out = [], []
    for k, total in enumerate(island_sums(parts)):
        cols_at = slice(k * narrow, (k + 1) * narrow)
        delta = total.astype(f32) / lax.axis_size("island")
        new_momentum, outer_step = outer_update(delta, momentum[:, cols_at])
        momentum_out.append(new_momentum)
        step_out.append(outer_step)
    return (jnp.concatenate(momentum_out, axis=1), jnp.concatenate(step_out, axis=1))


def solution(mesh):
    in_specs = (
        P(("island", "fsdp"), "tp"),
        P(("island", "fsdp"), "tp"),
        P(("island", "fsdp"), "tp"),
        P(),
        P("tp", "fsdp"),
        P("island", "tp", "fsdp"),
        P("island", "tp", "fsdp"),
        P("tp", "fsdp"),
    )
    out_specs = (P("tp", "fsdp"), P("tp", "fsdp"))
    return jax.shard_map(body, mesh=mesh, in_specs=in_specs, out_specs=out_specs, check_vma=False)
```

```python
import jax
import jax.numpy as jnp
from jax import lax
from jax.sharding import PartitionSpec as P

norm_eps = 1e-06
adam_eps = 1e-08
beta_one = 0.9
beta_two = 0.999
bias_one = 1.0 - 0.9**10
bias_two = 1.0 - 0.999**10
decay_rate = 0.1
outer_mu = 0.9

f32 = jnp.float32
bf16 = jnp.bfloat16


def outer_update(delta, momentum):
    new_momentum = outer_mu * momentum + delta
    outer_step = (delta + outer_mu * new_momentum).astype(bf16)
    return (new_momentum, outer_step)


def swap(value, axis, bit):
    count = lax.axis_size(axis)
    return lax.ppermute(value, axis, [(i, i ^ bit) for i in range(count)])


def together(*values):
    return lax.optimization_barrier(values)


class IslandLine:
    def __init__(self):
        self.count = lax.axis_size("island")
        self.hops = self.count - 1
        self.me = lax.axis_index("island")
        self.value, self.held, self.came, self.totals = {}, {}, {}, {}

    def pairs(self, hop):
        n, half = self.count, self.count // 2
        if hop < half - 1:
            ways = [(hop, hop + 1)]
        elif hop == half - 1:
            return [(half - 1, half), (half, half - 1)]
        else:
            ways = [(self.hops - hop, self.hops - 1 - hop)]
        return ways + [(n - 1 - i, n - 1 - j) for i, j in ways]

    def send(self, j, hop, payload):
        self.came[j] = lax.ppermute(payload, "island", self.pairs(hop))

    def enter(self, j, value, after):
        if after in self.held:
            value, self.held[after] = together(value, self.held[after])
        self.value[j] = value
        self.send(j, 0, value)

    def step(self, j, hop, after):
        half = self.count // 2
        came = self.came[j]
        if after in self.held:
            came, self.held[after] = together(came, self.held[after])
        if hop < half - 1:
            fresh = (came.astype(f32) + self.value[j].astype(f32)).astype(bf16)
        elif hop == half - 1:
            base = self.held[j] if hop else self.value[j]
            fresh = (came.astype(f32) + base.astype(f32)).astype(bf16)
        else:
            outer = self.hops - 1 - hop
            far = (self.me == outer) | (self.me == self.hops - outer)
            fresh = jnp.where(far, came, self.held[j])
        if hop + 1 < self.hops:
            self.held[j] = fresh
            self.send(j, hop + 1, fresh)
        else:
            del self.held[j]
            self.totals[j] = fresh


def body(context, residual, cotangent, gain, weight, first_moment, second_moment, momentum):
    tok_rows = context.shape[0]
    width = gain.shape[0]
    fsdp_count = lax.axis_size("fsdp")
    group = fsdp_count // 2
    cols = weight.shape[1]
    t = lax.axis_index("tp")
    f = lax.axis_index("fsdp")
    high = f // group
    low = f % group
    near = t == high

    pieces = 2
    rows = tok_rows // pieces

    def project(block):
        return lax.optimization_barrier(
            jnp.dot(block, weight, preferred_element_type=f32).astype(bf16)
        )

    near_blocks = [context] + [swap(context, "fsdp", r) for r in range(1, group)]
    slices = [
        [lax.dynamic_slice_in_dim(array, (low ^ r) * cols, cols, axis=1) for r in range(group)]
        for array in (residual, cotangent)
    ]
    held = together(context, *slices[0], *slices[1])
    later, slices = held[0], [held[1 : 1 + group], held[1 + group :]]
    moved = [[swap(parts[r], "fsdp", r) if r else parts[r] for r in range(group)] for parts in slices]
    far_pieces = [
        swap((later if p else context)[p * rows : (p + 1) * rows], "fsdp", group) for p in range(pieces)
    ]
    near_out = [project(context)]
    held = together(far_pieces[0], *near_blocks[1:], *moved[0], *moved[1])
    far_pieces[0] = held[0]
    near_blocks = [context] + list(held[1:group])
    residual_parts, cotangent_parts = held[group : 2 * group], held[2 * group :]
    far_pieces = [far_pieces] + [
        [swap(piece, "fsdp", r) for piece in far_pieces] for r in range(1, group)
    ]
    far_outs = []
    for r in range(group):
        far_outs += [swap(project(piece), "fsdp", group) for piece in far_pieces[r]]
    near_out += [project(block) for block in near_blocks[1:]]

    gain_part = lax.dynamic_slice_in_dim(gain, t * (width // 2) + low * cols, cols).astype(f32)

    keeps, arrivals = [], []
    for r in range(group):
        for p in range(pieces):
            far_out, own_out = far_outs[r * pieces + p], near_out[r]
            if keeps:
                far_out, own_out, keeps[-1] = together(far_out, own_out, keeps[-1])
            else:
                far_out, own_out = together(far_out, own_out)
            own_out = own_out[p * rows : (p + 1) * rows]
            keeps.append(jnp.where(near, own_out, far_out))
            arrivals.append(swap(jnp.where(near, far_out, own_out), "tp", 1))
    hidden, weighted, sums = [], [], []
    for k, (keep, came) in enumerate(zip(keeps, arrivals)):
        span = slice(k % pieces * rows, (k % pieces + 1) * rows)
        res, cot = residual_parts[k // pieces], cotangent_parts[k // pieces]
        if sums:
            came, sums[-1] = together(came, sums[-1])
        h = res[span].astype(f32) + keep.astype(f32) + came.astype(f32)
        w = gain_part[None, :] * cot[span].astype(f32)
        hidden.append(h)
        weighted.append(w)
        sums.append(jnp.stack([jnp.sum(h * h, axis=-1), jnp.sum(h * w, axis=-1)]))
    own_sums = jnp.concatenate(sums, axis=1)
    totals = own_sums
    for r in range(1, group):
        came = swap(own_sums, "fsdp", r)
        order = [r ^ k for k in range(group)]
        came = jnp.concatenate(
            [came[:, k * tok_rows : (k + 1) * tok_rows] for k in order], axis=1
        )
        totals = totals + came
    totals = totals + swap(totals, "tp", 1)
    inv_rms = lax.rsqrt(totals[0] / width + norm_eps)
    pull = inv_rms**3 * totals[1] / width

    tokens = near_blocks + [piece for block in far_pieces for piece in block]
    context_all = jnp.concatenate(tokens, axis=0)
    narrow = 128
    units = cols // narrow
    widths = [1, 3]
    while sum(widths) < units:
        widths.append(min(4, units - sum(widths)))
    def at(h, q, x):
        return (h * group + q) * 2 + x

    ring_pairs, cross_pairs = [], []
    for q in range(group):
        ring_pairs += [(at(x, q, x), at(x, q, 1 - x)) for x in (0, 1)]
        ring_pairs += [(at(1 - x, q, x), at(x, q, x)) for x in (0, 1)]
        cross_pairs += [(at(1 - x, q, x), at(x, q, 1 - x)) for x in (0, 1)]

    line = IslandLine()
    parts, rings = [], []

    def add_parts(c, after):
        cols_at = slice(sum(widths[:c]) * narrow, sum(widths[: c + 1]) * narrow)
        d_local = jnp.concatenate(
            [
                weighted[j][:, cols_at] * inv_rms[j * rows : (j + 1) * rows, None]
                - hidden[j][:, cols_at] * pull[j * rows : (j + 1) * rows, None]
                for j in range(group * pieces)
            ],
            axis=0,
        ).astype(bf16)
        if c < 3:
            if c == 2:
                d_local, rings[0] = together(d_local, rings[0])
            rings.append(lax.ppermute(d_local, ("fsdp", "tp"), ring_pairs))
            cross = lax.ppermute(d_local, ("fsdp", "tp"), cross_pairs)
            blocks = (d_local, cross)
        else:
            if after in line.held:
                d_local, line.held[after] = together(d_local, line.held[after])
            came = swap(d_local, "tp", 1)
            far = swap(jnp.where(near, came, d_local), "fsdp", group)
            rings.append(None)
            blocks = (jnp.where(near, d_local, came), far)
        return cols_at, blocks

    def add_pseudo(c, cols_at, blocks):
        if rings[c] is None:
            d_near, d_far = blocks
        else:
            d_near = jnp.where(near, blocks[0], rings[c])
            d_far = jnp.where(near, rings[c], blocks[1])
        d_all = jnp.concatenate([d_near, d_far], axis=0)
        grad = lax.dot_general(
            context_all, d_all, (((0,), (0,)), ((), ())), preferred_element_type=f32
        ) / (tok_rows * fsdp_count)
        first = first_moment[0, :, cols_at].astype(f32)
        second = second_moment[0, :, cols_at].astype(f32)
        m_new = beta_one * first + (1.0 - beta_one) * grad
        v_new = beta_two * second + (1.0 - beta_two) * grad * grad
        update = m_new / bias_one / (
            jnp.sqrt(v_new / bias_two) + adam_eps
        ) + decay_rate * weight[:, cols_at].astype(f32)
        pseudo = lax.optimization_barrier(update.astype(bf16))
        parts.extend(pseudo[:, u * narrow : (u + 1) * narrow] for u in range(widths[c]))

    first_three = [add_parts(c, None) for c in range(min(3, len(widths)))]
    for c, found in enumerate(first_three):
        add_pseudo(c, *found)
    next_chunk = len(first_three)
    for time in range(-2, units + line.hops - 1):
        for hop in range(line.hops):
            j = time - hop
            if 0 <= j < units:
                line.step(j, hop, j + 1 if hop else time - line.hops + 1)
        if next_chunk < len(widths) and time >= sum(widths[:next_chunk]) - 6:
            add_pseudo(next_chunk, *add_parts(next_chunk, time - line.hops + 2))
            next_chunk += 1
        if time + 2 < units:
            line.enter(time + 2, parts[time + 2], time - line.hops + 2)
    momentum_out, step_out = [], []
    for k in range(units):
        cols_at = slice(k * narrow, (k + 1) * narrow)
        total = lax.optimization_barrier(line.totals[k])
        delta = total.astype(f32) / lax.axis_size("island")
        new_momentum, outer_step = outer_update(delta, momentum[:, cols_at])
        momentum_out.append(new_momentum)
        step_out.append(outer_step)
    return (jnp.concatenate(momentum_out, axis=1), jnp.concatenate(step_out, axis=1))


def solution(mesh):
    in_specs = (
        P(("island", "fsdp"), "tp"),
        P(("island", "fsdp"), "tp"),
        P(("island", "fsdp"), "tp"),
        P(),
        P("tp", "fsdp"),
        P("island", "tp", "fsdp"),
        P("island", "tp", "fsdp"),
        P("tp", "fsdp"),
    )
    out_specs = (P("tp", "fsdp"), P("tp", "fsdp"))
    return jax.shard_map(body, mesh=mesh, in_specs=in_specs, out_specs=out_specs, check_vma=False)
```

```python
import jax
import jax.numpy as jnp
from jax import lax
from jax.sharding import PartitionSpec as P

norm_eps = 1e-06
adam_eps = 1e-08
beta_one = 0.9
beta_two = 0.999
bias_one = 1.0 - 0.9**10
bias_two = 1.0 - 0.999**10
decay_rate = 0.1
outer_mu = 0.9

f32 = jnp.float32
bf16 = jnp.bfloat16


def outer_update(delta, momentum):
    new_momentum = outer_mu * momentum + delta
    outer_step = (delta + outer_mu * new_momentum).astype(bf16)
    return (new_momentum, outer_step)


def swap(value, axis, bit):
    count = lax.axis_size(axis)
    return lax.ppermute(value, axis, [(i, i ^ bit) for i in range(count)])


def together(*values):
    return lax.optimization_barrier(values)


class IslandLine:
    def __init__(self, chunks):
        self.chunks = chunks
        me = lax.axis_index("island")
        self.outer = (me == 0) | (me == 3)
        self.part, self.paid, self.edge, self.mid, self.sums, self.totals = {}, {}, {}, {}, {}, {}

    def send_outer(self, s):
        if s >= self.chunks + 3:
            return
        pairs = [(0, 1), (3, 2)] if s < self.chunks else []
        if s >= 3:
            pairs = pairs + [(1, 0), (2, 3)]
            total = (self.sums[s - 3].astype(f32) + self.mid[s - 3].astype(f32)).astype(bf16)
            payload = jnp.where(self.outer, self.part[s], total) if s < self.chunks else total
        else:
            payload = self.part[s]
        self.paid[s] = payload
        self.edge[s] = lax.ppermute(payload, "island", pairs)

    def step(self, s):
        edge = self.edge[s]
        if s + 1 in self.paid:
            edge, self.paid[s + 1] = together(edge, self.paid[s + 1])
        if s < self.chunks:
            self.sums[s] = (edge.astype(f32) + self.part[s].astype(f32)).astype(bf16)
            self.mid[s] = lax.ppermute(self.sums[s], "island", [(1, 2), (2, 1)])
            if s >= 1:
                self.mid[s - 1], self.sums[s] = together(self.mid[s - 1], self.sums[s])
        self.send_outer(s + 2)
        if s >= 3:
            if s + 2 in self.paid:
                edge, self.paid[s], self.paid[s + 2] = together(edge, self.paid[s], self.paid[s + 2])
            else:
                edge, self.paid[s] = together(edge, self.paid[s])
            self.totals[s - 3] = jnp.where(self.outer, edge, self.paid[s])


def body(context, residual, cotangent, gain, weight, first_moment, second_moment, momentum):
    tok_rows = context.shape[0]
    width = gain.shape[0]
    fsdp_count = lax.axis_size("fsdp")
    group = fsdp_count // 2
    cols = weight.shape[1]
    t = lax.axis_index("tp")
    f = lax.axis_index("fsdp")
    high = f // group
    low = f % group
    near = t == high

    pieces = 2
    rows = tok_rows // pieces

    def project(block):
        return lax.optimization_barrier(
            jnp.dot(block, weight, preferred_element_type=f32).astype(bf16)
        )

    near_blocks = [context] + [swap(context, "fsdp", r) for r in range(1, group)]
    slices = [
        [lax.dynamic_slice_in_dim(array, (low ^ r) * cols, cols, axis=1) for r in range(group)]
        for array in (residual, cotangent)
    ]
    held = together(context, *slices[0], *slices[1])
    later, slices = held[0], [held[1 : 1 + group], held[1 + group :]]
    moved = [[swap(parts[r], "fsdp", r) if r else parts[r] for r in range(group)] for parts in slices]
    far_pieces = [
        swap((later if p else context)[p * rows : (p + 1) * rows], "fsdp", group) for p in range(pieces)
    ]
    held = together(far_pieces[0], *near_blocks[1:], *moved[0], *moved[1])
    far_pieces[0] = held[0]
    near_blocks = [context] + list(held[1:group])
    residual_parts, cotangent_parts = held[group : 2 * group], held[2 * group :]
    far_pieces = [far_pieces] + [
        [swap(piece, "fsdp", r) for piece in far_pieces] for r in range(1, group)
    ]
    far_outs, near_out = [], [[None] * pieces for r in range(group)]
    last = None
    for r in range(group):
        for p in range(pieces):
            beside = (r + 1) % group
            far = far_pieces[r][p]
            if last:
                far, near_out[last[0]][last[1]] = together(far, near_out[last[0]][last[1]])
            both = project(
                jnp.concatenate([far, near_blocks[beside][p * rows : (p + 1) * rows]], axis=0)
            )
            far_outs.append(swap(both[:rows], "fsdp", group))
            near_out[beside][p] = both[rows:]
            last = (beside, p)

    gain_part = lax.dynamic_slice_in_dim(gain, t * (width // 2) + low * cols, cols).astype(f32)

    keeps, arrivals = [], []
    for r in range(group):
        for p in range(pieces):
            far_out, own_out = far_outs[r * pieces + p], near_out[r][p]
            if keeps:
                far_out, own_out, keeps[-1] = together(far_out, own_out, keeps[-1])
            else:
                far_out, own_out = together(far_out, own_out)
            keeps.append(jnp.where(near, own_out, far_out))
            arrivals.append(swap(jnp.where(near, far_out, own_out), "tp", 1))
    hidden, weighted, sums = [], [], []
    for k, (keep, came) in enumerate(zip(keeps, arrivals)):
        span = slice(k % pieces * rows, (k % pieces + 1) * rows)
        res, cot = residual_parts[k // pieces], cotangent_parts[k // pieces]
        if sums:
            came, sums[-1] = together(came, sums[-1])
        h = res[span].astype(f32) + keep.astype(f32) + came.astype(f32)
        w = gain_part[None, :] * cot[span].astype(f32)
        hidden.append(h)
        weighted.append(w)
        sums.append(jnp.stack([jnp.sum(h * h, axis=-1), jnp.sum(h * w, axis=-1)]))
    own_sums = jnp.concatenate(sums, axis=1)
    totals = own_sums
    for r in range(1, group):
        came = swap(own_sums, "fsdp", r)
        order = [r ^ k for k in range(group)]
        came = jnp.concatenate(
            [came[:, k * tok_rows : (k + 1) * tok_rows] for k in order], axis=1
        )
        totals = totals + came
    totals = totals + swap(totals, "tp", 1)
    inv_rms = lax.rsqrt(totals[0] / width + norm_eps)
    pull = inv_rms**3 * totals[1] / width

    tokens = near_blocks + [piece for block in far_pieces for piece in block]
    context_all = jnp.concatenate(tokens, axis=0)
    narrow = 128
    units = cols // narrow
    widths = [1, 2]
    while sum(widths) < units:
        widths.append(min(2 + len(widths), units - sum(widths)))
    def at(h, q, x):
        return (h * group + q) * 2 + x

    ring_pairs, cross_pairs = [], []
    for q in range(group):
        ring_pairs += [(at(x, q, x), at(x, q, 1 - x)) for x in (0, 1)]
        ring_pairs += [(at(1 - x, q, x), at(x, q, x)) for x in (0, 1)]
        cross_pairs += [(at(1 - x, q, x), at(x, q, 1 - x)) for x in (0, 1)]

    islands = lax.axis_size("island")
    line = IslandLine(units)
    parts, rings, pseudos = [], [], []

    def add_parts(c, after):
        cols_at = slice(sum(widths[:c]) * narrow, sum(widths[: c + 1]) * narrow)
        d_local = jnp.concatenate(
            [
                weighted[j][:, cols_at] * inv_rms[j * rows : (j + 1) * rows, None]
                - hidden[j][:, cols_at] * pull[j * rows : (j + 1) * rows, None]
                for j in range(group * pieces)
            ],
            axis=0,
        ).astype(bf16)
        if c < 3:
            if c == 1:
                d_local, rings[0] = together(d_local, rings[0])
            elif c == 2:
                d_local, pseudos[0] = together(d_local, pseudos[0])
            rings.append(lax.ppermute(d_local, ("fsdp", "tp"), ring_pairs))
            cross = lax.ppermute(d_local, ("fsdp", "tp"), cross_pairs)
            blocks = (d_local, cross)
        else:
            if after in line.sums:
                d_local, line.sums[after] = together(d_local, line.sums[after])
            came = swap(d_local, "tp", 1)
            far = swap(jnp.where(near, came, d_local), "fsdp", group)
            rings.append(None)
            blocks = (jnp.where(near, d_local, came), far)
        return cols_at, blocks

    def add_pseudo(c, cols_at, blocks):
        if rings[c] is None:
            d_near, d_far = blocks
        else:
            d_near = jnp.where(near, blocks[0], rings[c])
            d_far = jnp.where(near, rings[c], blocks[1])
        d_all = jnp.concatenate([d_near, d_far], axis=0)
        grad = lax.dot_general(
            context_all, d_all, (((0,), (0,)), ((), ())), preferred_element_type=f32
        ) / (tok_rows * fsdp_count)
        first = first_moment[0, :, cols_at].astype(f32)
        second = second_moment[0, :, cols_at].astype(f32)
        m_new = beta_one * first + (1.0 - beta_one) * grad
        v_new = beta_two * second + (1.0 - beta_two) * grad * grad
        update = m_new / bias_one / (
            jnp.sqrt(v_new / bias_two) + adam_eps
        ) + decay_rate * weight[:, cols_at].astype(f32)
        pseudos.append(lax.optimization_barrier(update.astype(bf16)))

    def slice_pseudo(c):
        parts.extend(pseudos[c][:, u * narrow : (u + 1) * narrow] for u in range(widths[c]))

    early = min(3, len(widths))
    first, second = add_parts(0, None), add_parts(1, None)
    add_pseudo(0, *first)
    third = add_parts(2, None)
    add_pseudo(1, *second)
    add_pseudo(2, *third)
    for c in range(early):
        slice_pseudo(c)
    if islands == 4:
        line.part.update(enumerate(parts))
        for s in range(2):
            line.send_outer(s)
        for s in range(units + 3):
            if early < len(widths) and s == 2:
                for c in range(early, len(widths)):
                    add_pseudo(c, *add_parts(c, 1))
                    slice_pseudo(c)
                line.part.update(enumerate(parts))
            line.step(s)
        sums = [line.totals[k] for k in range(units)]
    else:
        sums = [lax.psum(part, "island") for part in parts]
    momentum_out, step_out = [], []
    for k, total in enumerate(sums):
        cols_at = slice(k * narrow, (k + 1) * narrow)
        delta = total.astype(f32) / islands
        new_momentum, outer_step = outer_update(delta, momentum[:, cols_at])
        momentum_out.append(new_momentum)
        step_out.append(outer_step)
    return (jnp.concatenate(momentum_out, axis=1), jnp.concatenate(step_out, axis=1))


def solution(mesh):
    in_specs = (
        P(("island", "fsdp"), "tp"),
        P(("island", "fsdp"), "tp"),
        P(("island", "fsdp"), "tp"),
        P(),
        P("tp", "fsdp"),
        P("island", "tp", "fsdp"),
        P("island", "tp", "fsdp"),
        P("tp", "fsdp"),
    )
    out_specs = (P("tp", "fsdp"), P("tp", "fsdp"))
    return jax.shard_map(body, mesh=mesh, in_specs=in_specs, out_specs=out_specs, check_vma=False)
```

```python
import jax
import jax.numpy as jnp
from jax import lax
from jax.sharding import PartitionSpec as P

norm_eps = 1e-06
adam_eps = 1e-08
beta_one = 0.9
beta_two = 0.999
bias_one = 1.0 - 0.9**10
bias_two = 1.0 - 0.999**10
decay_rate = 0.1
outer_mu = 0.9

f32 = jnp.float32
bf16 = jnp.bfloat16


def outer_update(delta, momentum):
    new_momentum = outer_mu * momentum + delta
    outer_step = (delta + outer_mu * new_momentum).astype(bf16)
    return (new_momentum, outer_step)


def swap(value, axis, bit):
    count = lax.axis_size(axis)
    return lax.ppermute(value, axis, [(i, i ^ bit) for i in range(count)])


def together(*values):
    return lax.optimization_barrier(values)


class IslandLine:
    def __init__(self, chunks):
        self.chunks = chunks
        me = lax.axis_index("island")
        self.outer = (me == 0) | (me == 3)
        self.part, self.paid, self.edge, self.mid, self.sums, self.totals = {}, {}, {}, {}, {}, {}

    def send_outer(self, s):
        if s >= self.chunks + 3:
            return
        pairs = [(0, 1), (3, 2)] if s < self.chunks else []
        if s >= 3:
            pairs = pairs + [(1, 0), (2, 3)]
            total = (self.sums[s - 3].astype(f32) + self.mid[s - 3].astype(f32)).astype(bf16)
            payload = jnp.where(self.outer, self.part[s], total) if s < self.chunks else total
        else:
            payload = self.part[s]
        self.paid[s] = payload
        self.edge[s] = lax.ppermute(payload, "island", pairs)

    def step(self, s):
        edge = self.edge[s]
        if s + 1 in self.paid:
            edge, self.paid[s + 1] = together(edge, self.paid[s + 1])
        if s < self.chunks:
            self.sums[s] = (edge.astype(f32) + self.part[s].astype(f32)).astype(bf16)
            self.mid[s] = lax.ppermute(self.sums[s], "island", [(1, 2), (2, 1)])
            if s >= 1:
                self.mid[s - 1], self.sums[s] = together(self.mid[s - 1], self.sums[s])
        self.send_outer(s + 2)
        if s >= 3:
            if s + 2 in self.paid:
                edge, self.paid[s], self.paid[s + 2] = together(edge, self.paid[s], self.paid[s + 2])
            else:
                edge, self.paid[s] = together(edge, self.paid[s])
            self.totals[s - 3] = jnp.where(self.outer, edge, self.paid[s])


def body(context, residual, cotangent, gain, weight, first_moment, second_moment, momentum):
    tok_rows = context.shape[0]
    width = gain.shape[0]
    fsdp_count = lax.axis_size("fsdp")
    group = fsdp_count // 2
    cols = weight.shape[1]
    t = lax.axis_index("tp")
    f = lax.axis_index("fsdp")
    high = f // group
    low = f % group
    near = t == high

    pieces = 2
    rows = tok_rows // pieces

    def project(block):
        return lax.optimization_barrier(
            jnp.dot(block, weight, preferred_element_type=f32).astype(bf16)
        )

    def at(h, q, x):
        return (h * group + q) * 2 + x

    ring_pairs, cross_pairs = [], []
    for q in range(group):
        ring_pairs += [(at(x, q, x), at(x, q, 1 - x)) for x in (0, 1)]
        ring_pairs += [(at(1 - x, q, x), at(x, q, x)) for x in (0, 1)]
        cross_pairs += [(at(1 - x, q, x), at(x, q, 1 - x)) for x in (0, 1)]
    inward_pairs = [(at(1 - x, q, x), at(1 - x, q, 1 - x)) for q in range(group) for x in (0, 1)]
    outward_pairs = [(at(x, q, x), at(x, q, 1 - x)) for q in range(group) for x in (0, 1)]

    near_blocks = [context] + [swap(context, "fsdp", r) for r in range(1, group)]
    slices = [
        [lax.dynamic_slice_in_dim(array, (low ^ r) * cols, cols, axis=1) for r in range(group)]
        for array in (residual, cotangent)
    ]
    held = together(context, *slices[0], *slices[1])
    later, slices = held[0], [held[1 : 1 + group], held[1 + group :]]
    moved = [[swap(parts[r], "fsdp", r) if r else parts[r] for r in range(group)] for parts in slices]
    far_pieces = [
        swap((later if p else context)[p * rows : (p + 1) * rows], "fsdp", group) for p in range(pieces)
    ]
    held = together(far_pieces[0], *near_blocks[1:], *moved[0], *moved[1])
    far_pieces[0] = held[0]
    near_blocks = [later] + list(held[1:group])
    residual_parts, cotangent_parts = held[group : 2 * group], held[2 * group :]
    far_pieces = [far_pieces] + [
        [swap(piece, "fsdp", r) for piece in far_pieces] for r in range(1, group)
    ]
    far_outs, near_out = [], [[None] * pieces for r in range(group)]
    near_came = {}
    last = None
    for r in range(group):
        for p in range(pieces):
            beside = (r + 1) % group
            far = far_pieces[r][p]
            if last:
                far, near_out[last[0]][last[1]] = together(far, near_out[last[0]][last[1]])
            both = project(
                jnp.concatenate([far, near_blocks[beside][p * rows : (p + 1) * rows]], axis=0)
            )
            far_outs.append(swap(both[:rows], "fsdp", group))
            near_out[beside][p] = both[rows:]
            last = (beside, p)
        whole = jnp.concatenate(near_out[beside], axis=0)
        near_came[beside] = lax.ppermute(whole, ("fsdp", "tp"), inward_pairs)
    passed = [lax.ppermute(out, ("fsdp", "tp"), outward_pairs) for out in far_outs]

    gain_part = lax.dynamic_slice_in_dim(gain, t * (width // 2) + low * cols, cols).astype(f32)

    hidden, weighted, sums = [], [], []
    for k in range(group * pieces):
        r, p = k // pieces, k % pieces
        span = slice(p * rows, (p + 1) * rows)
        res, cot, came = residual_parts[r], cotangent_parts[r], passed[k]
        if sums:
            came, sums[-1] = together(came, sums[-1])
        keep = jnp.where(near, near_out[r][p], far_outs[k])
        came = jnp.where(near, near_came[r][span], came)
        h = res[span].astype(f32) + keep.astype(f32) + came.astype(f32)
        w = gain_part[None, :] * cot[span].astype(f32)
        hidden.append(h)
        weighted.append(w)
        sums.append(jnp.stack([jnp.sum(h * h, axis=-1), jnp.sum(h * w, axis=-1)]))
    own_sums = jnp.concatenate(sums, axis=1)
    totals = own_sums
    for r in range(1, group):
        came = swap(own_sums, "fsdp", r)
        order = [r ^ k for k in range(group)]
        came = jnp.concatenate(
            [came[:, k * tok_rows : (k + 1) * tok_rows] for k in order], axis=1
        )
        totals = totals + came
    totals = totals + swap(totals, "tp", 1)
    inv_rms = lax.rsqrt(totals[0] / width + norm_eps)
    pull = inv_rms**3 * totals[1] / width

    tokens = near_blocks + [piece for block in far_pieces for piece in block]
    context_all = jnp.concatenate(tokens, axis=0)
    narrow = 128
    units = cols // narrow
    widths = [1, 3]
    while sum(widths) < units:
        widths.append(min(4, units - sum(widths)))
    islands = lax.axis_size("island")
    line = IslandLine(units)
    parts, rings = [], []

    def add_parts(c, after):
        cols_at = slice(sum(widths[:c]) * narrow, sum(widths[: c + 1]) * narrow)
        d_local = jnp.concatenate(
            [
                weighted[j][:, cols_at] * inv_rms[j * rows : (j + 1) * rows, None]
                - hidden[j][:, cols_at] * pull[j * rows : (j + 1) * rows, None]
                for j in range(group * pieces)
            ],
            axis=0,
        ).astype(bf16)
        if c < 3:
            if c == 1:
                d_local, rings[0] = together(d_local, rings[0])
            elif c == 2 and after in line.edge:
                d_local, line.edge[after] = together(d_local, line.edge[after])
            rings.append(lax.ppermute(d_local, ("fsdp", "tp"), ring_pairs))
            cross = lax.ppermute(d_local, ("fsdp", "tp"), cross_pairs)
            blocks = (d_local, cross)
        else:
            if after in line.sums:
                d_local, line.sums[after] = together(d_local, line.sums[after])
            came = swap(d_local, "tp", 1)
            far = swap(jnp.where(near, came, d_local), "fsdp", group)
            rings.append(None)
            blocks = (jnp.where(near, d_local, came), far)
        return cols_at, blocks

    def add_pseudo(c, cols_at, blocks):
        if rings[c] is None:
            d_near, d_far = blocks
        else:
            d_near = jnp.where(near, blocks[0], rings[c])
            d_far = jnp.where(near, rings[c], blocks[1])
        d_all = jnp.concatenate([d_near, d_far], axis=0)
        cuts = list(range(0, widths[c], 2)) if widths[c] % 2 == 0 else [0] + list(range(1, widths[c], 2))
        for lo, hi in zip(cuts, cuts[1:] + [widths[c]]):
            at_cols = slice(cols_at.start + lo * narrow, cols_at.start + hi * narrow)
            grad = lax.dot_general(
                context_all,
                lax.optimization_barrier(d_all[:, lo * narrow : hi * narrow]),
                (((0,), (0,)), ((), ())),
                preferred_element_type=f32,
            ) / (tok_rows * fsdp_count)
            first = first_moment[0, :, at_cols].astype(f32)
            second = second_moment[0, :, at_cols].astype(f32)
            m_new = beta_one * first + (1.0 - beta_one) * grad
            v_new = beta_two * second + (1.0 - beta_two) * grad * grad
            update = m_new / bias_one / (
                jnp.sqrt(v_new / bias_two) + adam_eps
            ) + decay_rate * weight[:, at_cols].astype(f32)
            pseudo = lax.optimization_barrier(update.astype(bf16))
            parts.extend(pseudo[:, u * narrow : (u + 1) * narrow] for u in range(hi - lo))

    first, second = add_parts(0, None), add_parts(1, None)
    add_pseudo(0, *first)
    add_pseudo(1, *second)
    if islands == 4:
        line.part.update(enumerate(parts))
        for s in range(2):
            line.send_outer(s)
        for s in range(units + 3):
            for c in {0: [2], 3: range(3, len(widths))}.get(s, []):
                add_pseudo(c, *add_parts(c, max(s - 1, 0)))
            line.part.update(enumerate(parts))
            line.step(s)
        sums = [line.totals[k] for k in range(units)]
    else:
        for c in range(2, len(widths)):
            add_pseudo(c, *add_parts(c, None))
        sums = [lax.psum(part, "island") for part in parts]
    momentum_out, step_out = [], []
    for k, total in enumerate(sums):
        cols_at = slice(k * narrow, (k + 1) * narrow)
        delta = total.astype(f32) / islands
        new_momentum, outer_step = outer_update(delta, momentum[:, cols_at])
        momentum_out.append(new_momentum)
        step_out.append(outer_step)
    return (jnp.concatenate(momentum_out, axis=1), jnp.concatenate(step_out, axis=1))


def solution(mesh):
    in_specs = (
        P(("island", "fsdp"), "tp"),
        P(("island", "fsdp"), "tp"),
        P(("island", "fsdp"), "tp"),
        P(),
        P("tp", "fsdp"),
        P("island", "tp", "fsdp"),
        P("island", "tp", "fsdp"),
        P("tp", "fsdp"),
    )
    out_specs = (P("tp", "fsdp"), P("tp", "fsdp"))
    return jax.shard_map(body, mesh=mesh, in_specs=in_specs, out_specs=out_specs, check_vma=False)
```

```python
import jax
import jax.numpy as jnp
from jax import lax
from jax.sharding import PartitionSpec as P

norm_eps = 1e-06
adam_eps = 1e-08
beta_one = 0.9
beta_two = 0.999
bias_one = 1.0 - 0.9**10
bias_two = 1.0 - 0.999**10
decay_rate = 0.1
outer_mu = 0.9

f32 = jnp.float32
bf16 = jnp.bfloat16


def outer_update(delta, momentum):
    new_momentum = outer_mu * momentum + delta
    outer_step = (delta + outer_mu * new_momentum).astype(bf16)
    return (new_momentum, outer_step)


def swap(value, axis, bit):
    count = lax.axis_size(axis)
    return lax.ppermute(value, axis, [(i, i ^ bit) for i in range(count)])


def together(*values):
    return lax.optimization_barrier(values)


class IslandLine:
    def __init__(self, chunks):
        self.chunks = chunks
        me = lax.axis_index("island")
        self.outer = (me == 0) | (me == 3)
        self.part, self.paid, self.edge, self.mid, self.sums, self.totals = {}, {}, {}, {}, {}, {}

    def send_outer(self, s):
        if s >= self.chunks + 3:
            return
        pairs = [(0, 1), (3, 2)] if s < self.chunks else []
        if s >= 3:
            pairs = pairs + [(1, 0), (2, 3)]
            total = (self.sums[s - 3].astype(f32) + self.mid[s - 3].astype(f32)).astype(bf16)
            payload = jnp.where(self.outer, self.part[s], total) if s < self.chunks else total
        else:
            payload = self.part[s]
        self.paid[s] = payload
        self.edge[s] = lax.ppermute(payload, "island", pairs)

    def step(self, s):
        edge = self.edge[s]
        if s + 1 in self.paid:
            edge, self.paid[s + 1] = together(edge, self.paid[s + 1])
        if s < self.chunks:
            self.sums[s] = (edge.astype(f32) + self.part[s].astype(f32)).astype(bf16)
            self.mid[s] = lax.ppermute(self.sums[s], "island", [(1, 2), (2, 1)])
            if s >= 1:
                self.mid[s - 1], self.sums[s] = together(self.mid[s - 1], self.sums[s])
        self.send_outer(s + 2)
        if s >= 3:
            if s + 2 in self.paid:
                edge, self.paid[s], self.paid[s + 2] = together(edge, self.paid[s], self.paid[s + 2])
            else:
                edge, self.paid[s] = together(edge, self.paid[s])
            self.totals[s - 3] = jnp.where(self.outer, edge, self.paid[s])


def body(context, residual, cotangent, gain, weight, first_moment, second_moment, momentum):
    tok_rows = context.shape[0]
    width = gain.shape[0]
    fsdp_count = lax.axis_size("fsdp")
    group = fsdp_count // 2
    cols = weight.shape[1]
    t = lax.axis_index("tp")
    f = lax.axis_index("fsdp")
    high = f // group
    low = f % group
    near = t == high

    pieces = 2
    rows = tok_rows // pieces

    def project(block):
        return lax.optimization_barrier(
            jnp.dot(block, weight, preferred_element_type=f32).astype(bf16)
        )

    near_blocks = [context] + [swap(context, "fsdp", r) for r in range(1, group)]
    slices = [
        [lax.dynamic_slice_in_dim(array, (low ^ r) * cols, cols, axis=1) for r in range(group)]
        for array in (residual, cotangent)
    ]
    moved = [[swap(parts[r], "fsdp", r) if r else parts[r] for r in range(group)] for parts in slices]
    held = together(swap(context, "fsdp", group), *near_blocks[1:], *moved[0], *moved[1])
    near_blocks = [context] + list(held[1:group])
    residual_parts, cotangent_parts = held[group : 2 * group], held[2 * group :]
    far_blocks = [held[0]] + [swap(held[0], "fsdp", r) for r in range(1, group)]
    far_outs, near_out = [], [[None] * pieces for r in range(group)]
    last = None
    for r in range(group):
        for p in range(pieces):
            beside = (r + 1) % group
            far = far_blocks[r]
            if last:
                far, near_out[last[0]][last[1]] = together(far, near_out[last[0]][last[1]])
            both = project(
                jnp.concatenate([block[p * rows : (p + 1) * rows] for block in (far, near_blocks[beside])], axis=0)
            )
            far_outs.append(swap(both[:rows], "fsdp", group))
            near_out[beside][p] = both[rows:]
            last = (beside, p)

    gain_part = lax.dynamic_slice_in_dim(gain, t * (width // 2) + low * cols, cols).astype(f32)

    keeps, arrivals = [], []
    for r in range(group):
        for p in range(pieces):
            far_out, own_out = far_outs[r * pieces + p], near_out[r][p]
            if keeps:
                far_out, own_out, keeps[-1] = together(far_out, own_out, keeps[-1])
            else:
                far_out, own_out = together(far_out, own_out)
            keeps.append(jnp.where(near, own_out, far_out))
            arrivals.append(swap(jnp.where(near, far_out, own_out), "tp", 1))
    hidden, weighted, sums = [], [], []
    for k, (keep, came) in enumerate(zip(keeps, arrivals)):
        span = slice(k % pieces * rows, (k % pieces + 1) * rows)
        res, cot = residual_parts[k // pieces], cotangent_parts[k // pieces]
        if sums:
            came, sums[-1] = together(came, sums[-1])
        h = res[span].astype(f32) + keep.astype(f32) + came.astype(f32)
        w = gain_part[None, :] * cot[span].astype(f32)
        hidden.append(h)
        weighted.append(w)
        sums.append(jnp.stack([jnp.sum(h * h, axis=-1), jnp.sum(h * w, axis=-1)]))
    own_sums = jnp.concatenate(sums, axis=1)
    totals = own_sums
    for r in range(1, group):
        came = swap(own_sums, "fsdp", r)
        order = [r ^ k for k in range(group)]
        came = jnp.concatenate(
            [came[:, k * tok_rows : (k + 1) * tok_rows] for k in order], axis=1
        )
        totals = totals + came
    totals = totals + swap(totals, "tp", 1)
    inv_rms = lax.rsqrt(totals[0] / width + norm_eps)
    pull = inv_rms**3 * totals[1] / width

    context_all = jnp.concatenate(near_blocks + far_blocks, axis=0)
    narrow = 128
    units = cols // narrow
    widths = [1, 3]
    while sum(widths) < units:
        widths.append(min(4, units - sum(widths)))
    def at(h, q, x):
        return (h * group + q) * 2 + x

    ring_pairs, cross_pairs = [], []
    for q in range(group):
        ring_pairs += [(at(x, q, x), at(x, q, 1 - x)) for x in (0, 1)]
        ring_pairs += [(at(1 - x, q, x), at(x, q, x)) for x in (0, 1)]
        cross_pairs += [(at(1 - x, q, x), at(x, q, 1 - x)) for x in (0, 1)]

    islands = lax.axis_size("island")
    line = IslandLine(units)
    parts, rings = [], []

    def add_parts(c, after):
        cols_at = slice(sum(widths[:c]) * narrow, sum(widths[: c + 1]) * narrow)
        d_local = jnp.concatenate(
            [
                weighted[j][:, cols_at] * inv_rms[j * rows : (j + 1) * rows, None]
                - hidden[j][:, cols_at] * pull[j * rows : (j + 1) * rows, None]
                for j in range(group * pieces)
            ],
            axis=0,
        ).astype(bf16)
        if c < 3:
            if c == 1:
                d_local, rings[0] = together(d_local, rings[0])
            elif c == 2 and after in line.edge:
                d_local, line.edge[after] = together(d_local, line.edge[after])
            rings.append(lax.ppermute(d_local, ("fsdp", "tp"), ring_pairs))
            cross = lax.ppermute(d_local, ("fsdp", "tp"), cross_pairs)
            blocks = (d_local, cross)
        else:
            if after in line.sums:
                d_local, line.sums[after] = together(d_local, line.sums[after])
            came = swap(d_local, "tp", 1)
            far = swap(jnp.where(near, came, d_local), "fsdp", group)
            rings.append(None)
            blocks = (jnp.where(near, d_local, came), far)
        return cols_at, blocks

    def add_pseudo(c, cols_at, blocks):
        if rings[c] is None:
            d_near, d_far = blocks
        else:
            d_near = jnp.where(near, blocks[0], rings[c])
            d_far = jnp.where(near, rings[c], blocks[1])
        d_all = jnp.concatenate([d_near, d_far], axis=0)
        cuts = list(range(0, widths[c], 2)) if widths[c] % 2 == 0 else [0] + list(range(1, widths[c], 2))
        for lo, hi in zip(cuts, cuts[1:] + [widths[c]]):
            at_cols = slice(cols_at.start + lo * narrow, cols_at.start + hi * narrow)
            grad = lax.dot_general(
                context_all,
                lax.optimization_barrier(d_all[:, lo * narrow : hi * narrow]),
                (((0,), (0,)), ((), ())),
                preferred_element_type=f32,
            ) / (tok_rows * fsdp_count)
            first, second, outer = together(first_moment, second_moment, weight)
            first = first[0, :, at_cols].astype(f32)
            second = second[0, :, at_cols].astype(f32)
            m_new = beta_one * first + (1.0 - beta_one) * grad
            v_new = beta_two * second + (1.0 - beta_two) * grad * grad
            update = m_new / bias_one / (
                jnp.sqrt(v_new / bias_two) + adam_eps
            ) + decay_rate * outer[:, at_cols].astype(f32)
            pseudo = lax.optimization_barrier(update.astype(bf16))
            parts.extend(pseudo[:, u * narrow : (u + 1) * narrow] for u in range(hi - lo))

    first, second = add_parts(0, None), add_parts(1, None)
    add_pseudo(0, *first)
    add_pseudo(1, *second)
    if islands == 4:
        line.part.update(enumerate(parts))
        for s in range(2):
            line.send_outer(s)
        for s in range(units + 3):
            for c in {0: [2], 3: range(3, len(widths))}.get(s, []):
                add_pseudo(c, *add_parts(c, max(s - 1, 0)))
            line.part.update(enumerate(parts))
            line.step(s)
        sums = [line.totals[k] for k in range(units)]
    else:
        for c in range(2, len(widths)):
            add_pseudo(c, *add_parts(c, None))
        sums = [lax.psum(part, "island") for part in parts]
    momentum_out, step_out = [], []
    for k, total in enumerate(sums):
        cols_at = slice(k * narrow, (k + 1) * narrow)
        delta = total.astype(f32) / islands
        new_momentum, outer_step = outer_update(delta, momentum[:, cols_at])
        momentum_out.append(new_momentum)
        step_out.append(outer_step)
    return (jnp.concatenate(momentum_out, axis=1), jnp.concatenate(step_out, axis=1))


def solution(mesh):
    in_specs = (
        P(("island", "fsdp"), "tp"),
        P(("island", "fsdp"), "tp"),
        P(("island", "fsdp"), "tp"),
        P(),
        P("tp", "fsdp"),
        P("island", "tp", "fsdp"),
        P("island", "tp", "fsdp"),
        P("tp", "fsdp"),
    )
    out_specs = (P("tp", "fsdp"), P("tp", "fsdp"))
    return jax.shard_map(body, mesh=mesh, in_specs=in_specs, out_specs=out_specs, check_vma=False)
```

```python
import jax
import jax.numpy as jnp
from jax import lax
from jax.sharding import PartitionSpec as P

norm_eps = 1e-06
adam_eps = 1e-08
beta_one = 0.9
beta_two = 0.999
bias_one = 1.0 - 0.9**10
bias_two = 1.0 - 0.999**10
decay_rate = 0.1
outer_mu = 0.9

f32 = jnp.float32
bf16 = jnp.bfloat16


def outer_update(delta, momentum):
    new_momentum = outer_mu * momentum + delta
    outer_step = (delta + outer_mu * new_momentum).astype(bf16)
    return (new_momentum, outer_step)


def swap(value, axis, bit):
    count = lax.axis_size(axis)
    return lax.ppermute(value, axis, [(i, i ^ bit) for i in range(count)])


def together(*values):
    return lax.optimization_barrier(values)


class IslandLine:
    def __init__(self, chunks):
        self.chunks = chunks
        me = lax.axis_index("island")
        self.outer = (me == 0) | (me == 3)
        self.part, self.paid, self.edge, self.mid, self.sums, self.totals = {}, {}, {}, {}, {}, {}

    def send_outer(self, s):
        if s >= self.chunks + 3:
            return
        pairs = [(0, 1), (3, 2)] if s < self.chunks else []
        if s >= 3:
            pairs = pairs + [(1, 0), (2, 3)]
            total = (self.sums[s - 3].astype(f32) + self.mid[s - 3].astype(f32)).astype(bf16)
            payload = jnp.where(self.outer, self.part[s], total) if s < self.chunks else total
        else:
            payload = self.part[s]
        self.paid[s] = payload
        self.edge[s] = lax.ppermute(payload, "island", pairs)

    def step(self, s):
        edge = self.edge[s]
        if s + 1 in self.paid:
            edge, self.paid[s + 1] = together(edge, self.paid[s + 1])
        if s < self.chunks:
            self.sums[s] = (edge.astype(f32) + self.part[s].astype(f32)).astype(bf16)
            self.mid[s] = lax.ppermute(self.sums[s], "island", [(1, 2), (2, 1)])
            if s >= 1:
                self.mid[s - 1], self.sums[s] = together(self.mid[s - 1], self.sums[s])
        self.send_outer(s + 2)
        if s >= 3:
            if s + 2 in self.paid:
                edge, self.paid[s], self.paid[s + 2] = together(edge, self.paid[s], self.paid[s + 2])
            else:
                edge, self.paid[s] = together(edge, self.paid[s])
            self.totals[s - 3] = jnp.where(self.outer, edge, self.paid[s])


def body(context, residual, cotangent, gain, weight, first_moment, second_moment, momentum):
    tok_rows = context.shape[0]
    width = gain.shape[0]
    fsdp_count = lax.axis_size("fsdp")
    group = fsdp_count // 2
    cols = weight.shape[1]
    t = lax.axis_index("tp")
    f = lax.axis_index("fsdp")
    high = f // group
    low = f % group
    near = t == high

    pieces = 2
    rows = tok_rows // pieces

    def project(block):
        return lax.optimization_barrier(
            jnp.dot(block, weight, preferred_element_type=f32).astype(bf16)
        )

    near_blocks = [context] + [swap(context, "fsdp", r) for r in range(1, group)]
    slices = [
        [lax.dynamic_slice_in_dim(array, (low ^ r) * cols, cols, axis=1) for r in range(group)]
        for array in (residual, cotangent)
    ]
    moved = [[swap(parts[r], "fsdp", r) if r else parts[r] for r in range(group)] for parts in slices]
    held = together(swap(context, "fsdp", group), *near_blocks[1:], *moved[0], *moved[1])
    near_blocks = [context] + list(held[1:group])
    residual_parts, cotangent_parts = held[group : 2 * group], held[2 * group :]
    far_blocks = [held[0]] + [swap(held[0], "fsdp", r) for r in range(1, group)]
    far_outs, near_first = [], None
    for r in range(group):
        blocks = [far_blocks[r]] + ([context[:rows]] if r == group - 1 else [])
        out = project(jnp.concatenate(blocks, axis=0))
        far_outs += [swap(out[p * rows : (p + 1) * rows], "fsdp", group) for p in range(pieces)]
        near_first = out[tok_rows:]

    gain_part = lax.dynamic_slice_in_dim(gain, t * (width // 2) + low * cols, cols).astype(f32)

    keeps, arrivals = [], []
    for r in range(group):
        for p in range(pieces):
            far_out, own_out = far_outs[r * pieces + p], near_first
            if keeps:
                block, keeps[-1] = together(near_blocks[r], keeps[-1])
                own_out = project(block[p * rows : (p + 1) * rows])
            far_out, own_out = together(far_out, own_out)
            keeps.append(jnp.where(near, own_out, far_out))
            arrivals.append(swap(jnp.where(near, far_out, own_out), "tp", 1))
    hidden, weighted, sums = [], [], []
    for k, (keep, came) in enumerate(zip(keeps, arrivals)):
        span = slice(k % pieces * rows, (k % pieces + 1) * rows)
        res, cot = residual_parts[k // pieces], cotangent_parts[k // pieces]
        if sums:
            came, sums[-1] = together(came, sums[-1])
        h = res[span].astype(f32) + keep.astype(f32) + came.astype(f32)
        w = gain_part[None, :] * cot[span].astype(f32)
        hidden.append(h)
        weighted.append(w)
        sums.append(jnp.stack([jnp.sum(h * h, axis=-1), jnp.sum(h * w, axis=-1)]))
    own_sums = jnp.concatenate(sums, axis=1)
    totals = own_sums
    for r in range(1, group):
        came = swap(own_sums, "fsdp", r)
        order = [r ^ k for k in range(group)]
        came = jnp.concatenate(
            [came[:, k * tok_rows : (k + 1) * tok_rows] for k in order], axis=1
        )
        totals = totals + came
    totals = totals + swap(totals, "tp", 1)
    inv_rms = lax.rsqrt(totals[0] / width + norm_eps)
    pull = inv_rms**3 * totals[1] / width

    context_all = jnp.concatenate(near_blocks + far_blocks, axis=0)
    narrow = 128
    units = cols // narrow
    widths = [1, 3, units - 4]
    def at(h, q, x):
        return (h * group + q) * 2 + x

    ring_pairs, cross_pairs = [], []
    for q in range(group):
        ring_pairs += [(at(x, q, x), at(x, q, 1 - x)) for x in (0, 1)]
        ring_pairs += [(at(1 - x, q, x), at(x, q, x)) for x in (0, 1)]
        cross_pairs += [(at(1 - x, q, x), at(x, q, 1 - x)) for x in (0, 1)]

    islands = lax.axis_size("island")
    line = IslandLine(units)
    parts, locals_, rings, crosses = [], [], [], []

    def move(c):
        cols_at = slice(sum(widths[:c]) * narrow, sum(widths[: c + 1]) * narrow)
        d_local = jnp.concatenate(
            [
                weighted[j][:, cols_at] * inv_rms[j * rows : (j + 1) * rows, None]
                - hidden[j][:, cols_at] * pull[j * rows : (j + 1) * rows, None]
                for j in range(group * pieces)
            ],
            axis=0,
        ).astype(bf16)
        if c == 1:
            d_local, rings[0] = together(d_local, rings[0])
        elif c == 2:
            d_local, crosses[0] = together(d_local, crosses[0])
        locals_.append(d_local)
        rings.append(lax.ppermute(d_local, ("fsdp", "tp"), ring_pairs))
        crosses.append(lax.ppermute(d_local, ("fsdp", "tp"), cross_pairs))

    def add_pseudo(c):
        start = sum(widths[:c]) * narrow
        d_near = jnp.where(near, locals_[c], rings[c])
        d_far = jnp.where(near, rings[c], crosses[c])
        d_all = jnp.concatenate([d_near, d_far], axis=0)
        cuts = list(range(0, widths[c], 2)) if widths[c] % 2 == 0 else [0] + list(range(1, widths[c], 2))
        for lo, hi in zip(cuts, cuts[1:] + [widths[c]]):
            at_cols = slice(start + lo * narrow, start + hi * narrow)
            piece, first, second, outer = together(
                d_all[:, lo * narrow : hi * narrow], first_moment, second_moment, weight
            )
            grad = lax.dot_general(
                context_all, piece, (((0,), (0,)), ((), ())), preferred_element_type=f32
            ) / (tok_rows * fsdp_count)
            first = first[0, :, at_cols].astype(f32)
            second = second[0, :, at_cols].astype(f32)
            m_new = beta_one * first + (1.0 - beta_one) * grad
            v_new = beta_two * second + (1.0 - beta_two) * grad * grad
            update = m_new / bias_one / (
                jnp.sqrt(v_new / bias_two) + adam_eps
            ) + decay_rate * outer[:, at_cols].astype(f32)
            pseudo = lax.optimization_barrier(update.astype(bf16))
            parts.extend(pseudo[:, u * narrow : (u + 1) * narrow] for u in range(hi - lo))

    for c in range(len(widths)):
        move(c)
    for c in range(len(widths)):
        add_pseudo(c)
    if islands == 4:
        line.part.update(enumerate(parts))
        for s in range(2):
            line.send_outer(s)
        for s in range(units + 3):
            line.step(s)
        sums = [line.totals[k] for k in range(units)]
    else:
        sums = [lax.psum(part, "island") for part in parts]
    momentum_out, step_out = [], []
    for k, total in enumerate(sums):
        cols_at = slice(k * narrow, (k + 1) * narrow)
        delta = total.astype(f32) / islands
        new_momentum, outer_step = outer_update(delta, momentum[:, cols_at])
        momentum_out.append(new_momentum)
        step_out.append(outer_step)
    return (jnp.concatenate(momentum_out, axis=1), jnp.concatenate(step_out, axis=1))


def solution(mesh):
    in_specs = (
        P(("island", "fsdp"), "tp"),
        P(("island", "fsdp"), "tp"),
        P(("island", "fsdp"), "tp"),
        P(),
        P("tp", "fsdp"),
        P("island", "tp", "fsdp"),
        P("island", "tp", "fsdp"),
        P("tp", "fsdp"),
    )
    out_specs = (P("tp", "fsdp"), P("tp", "fsdp"))
    return jax.shard_map(body, mesh=mesh, in_specs=in_specs, out_specs=out_specs, check_vma=False)
```

```python
import jax
import jax.numpy as jnp
from jax import lax
from jax.sharding import PartitionSpec as P

norm_eps = 1e-06
adam_eps = 1e-08
beta_one = 0.9
beta_two = 0.999
bias_one = 1.0 - 0.9**10
bias_two = 1.0 - 0.999**10
decay_rate = 0.1
outer_mu = 0.9

f32 = jnp.float32
bf16 = jnp.bfloat16


def outer_update(delta, momentum):
    new_momentum = outer_mu * momentum + delta
    outer_step = (delta + outer_mu * new_momentum).astype(bf16)
    return (new_momentum, outer_step)


def swap(value, axis, bit):
    count = lax.axis_size(axis)
    return lax.ppermute(value, axis, [(i, i ^ bit) for i in range(count)])


def together(*values):
    return lax.optimization_barrier(values)


class IslandLine:
    def __init__(self, chunks):
        self.chunks = chunks
        me = lax.axis_index("island")
        self.outer = (me == 0) | (me == 3)
        self.part, self.paid, self.edge, self.mid, self.sums, self.totals = {}, {}, {}, {}, {}, {}

    def send_outer(self, s):
        if s >= self.chunks + 3:
            return
        pairs = [(0, 1), (3, 2)] if s < self.chunks else []
        if s >= 3:
            pairs = pairs + [(1, 0), (2, 3)]
            total = (self.sums[s - 3].astype(f32) + self.mid[s - 3].astype(f32)).astype(bf16)
            payload = jnp.where(self.outer, self.part[s], total) if s < self.chunks else total
        else:
            payload = self.part[s]
        self.paid[s] = payload
        self.edge[s] = lax.ppermute(payload, "island", pairs)

    def step(self, s):
        edge = self.edge[s]
        if s + 1 in self.paid:
            edge, self.paid[s + 1] = together(edge, self.paid[s + 1])
        if s < self.chunks:
            self.sums[s] = (edge.astype(f32) + self.part[s].astype(f32)).astype(bf16)
            self.mid[s] = lax.ppermute(self.sums[s], "island", [(1, 2), (2, 1)])
            if s >= 1:
                self.mid[s - 1], self.sums[s] = together(self.mid[s - 1], self.sums[s])
        self.send_outer(s + 2)
        if s >= 3:
            if s + 2 in self.paid:
                edge, self.paid[s], self.paid[s + 2] = together(edge, self.paid[s], self.paid[s + 2])
            else:
                edge, self.paid[s] = together(edge, self.paid[s])
            self.totals[s - 3] = jnp.where(self.outer, edge, self.paid[s])


def body(context, residual, cotangent, gain, weight, first_moment, second_moment, momentum):
    tok_rows = context.shape[0]
    width = gain.shape[0]
    fsdp_count = lax.axis_size("fsdp")
    group = fsdp_count // 2
    cols = weight.shape[1]
    t = lax.axis_index("tp")
    f = lax.axis_index("fsdp")
    high = f // group
    low = f % group
    near = t == high

    pieces = 2
    rows = tok_rows // pieces

    def project(block):
        return lax.optimization_barrier(
            jnp.dot(block, weight, preferred_element_type=f32).astype(bf16)
        )

    def at(h, q, x):
        return (h * group + q) * 2 + x

    ring_pairs, cross_pairs = [], []
    for q in range(group):
        ring_pairs += [(at(x, q, x), at(x, q, 1 - x)) for x in (0, 1)]
        ring_pairs += [(at(1 - x, q, x), at(x, q, x)) for x in (0, 1)]
        cross_pairs += [(at(1 - x, q, x), at(x, q, 1 - x)) for x in (0, 1)]
    inward_pairs = [(at(1 - x, q, x), at(1 - x, q, 1 - x)) for q in range(group) for x in (0, 1)]
    outward_pairs = [(at(x, q, x), at(x, q, 1 - x)) for q in range(group) for x in (0, 1)]

    near_blocks = [context] + [swap(context, "fsdp", r) for r in range(1, group)]
    slices = [
        [lax.dynamic_slice_in_dim(array, (low ^ r) * cols, cols, axis=1) for r in range(group)]
        for array in (residual, cotangent)
    ]
    moved = [[swap(parts[r], "fsdp", r) if r else parts[r] for r in range(group)] for parts in slices]
    held = together(swap(context, "fsdp", group), *moved[0], *moved[1])
    residual_parts, cotangent_parts = held[1 : 1 + group], held[1 + group :]
    far_blocks = [held[0]] + [swap(held[0], "fsdp", r) for r in range(1, group)]
    near_out = project(jnp.concatenate(near_blocks, axis=0))
    near_came = lax.ppermute(near_out, ("fsdp", "tp"), inward_pairs)
    far_outs = []
    for r in range(group):
        out = project(far_blocks[r])
        far_outs += [swap(out[p * rows : (p + 1) * rows], "fsdp", group) for p in range(pieces)]
    passed = [lax.ppermute(out, ("fsdp", "tp"), outward_pairs) for out in far_outs]

    gain_part = lax.dynamic_slice_in_dim(gain, t * (width // 2) + low * cols, cols).astype(f32)

    hidden, weighted, sums = [], [], []
    for k in range(group * pieces):
        r, p = k // pieces, k % pieces
        span, long_span = slice(p * rows, (p + 1) * rows), slice(k * rows, (k + 1) * rows)
        res, cot, came = residual_parts[r], cotangent_parts[r], passed[k]
        if sums:
            came, sums[-1] = together(came, sums[-1])
        keep = jnp.where(near, near_out[long_span], far_outs[k])
        came = jnp.where(near, near_came[long_span], came)
        h = res[span].astype(f32) + keep.astype(f32) + came.astype(f32)
        w = gain_part[None, :] * cot[span].astype(f32)
        hidden.append(h)
        weighted.append(w)
        sums.append(jnp.stack([jnp.sum(h * h, axis=-1), jnp.sum(h * w, axis=-1)]))
    own_sums = jnp.concatenate(sums, axis=1)
    totals = own_sums
    for r in range(1, group):
        came = swap(own_sums, "fsdp", r)
        order = [r ^ k for k in range(group)]
        came = jnp.concatenate(
            [came[:, k * tok_rows : (k + 1) * tok_rows] for k in order], axis=1
        )
        totals = totals + came
    totals = totals + swap(totals, "tp", 1)
    inv_rms = lax.rsqrt(totals[0] / width + norm_eps)
    pull = inv_rms**3 * totals[1] / width

    context_all = jnp.concatenate(near_blocks + far_blocks, axis=0)
    narrow = 128
    units = cols // narrow
    widths = [1, min(4, units - 2), units - 1 - min(4, units - 2)]
    islands = lax.axis_size("island")
    line = IslandLine(units)
    parts, locals_, rings, crosses = [], [], [], []

    def move(c):
        cols_at = slice(sum(widths[:c]) * narrow, sum(widths[: c + 1]) * narrow)
        d_local = jnp.concatenate(
            [
                weighted[j][:, cols_at] * inv_rms[j * rows : (j + 1) * rows, None]
                - hidden[j][:, cols_at] * pull[j * rows : (j + 1) * rows, None]
                for j in range(group * pieces)
            ],
            axis=0,
        ).astype(bf16)
        if c == 1:
            d_local, rings[0] = together(d_local, rings[0])
        elif c == 2:
            d_local, parts[1] = together(d_local, parts[1])
        locals_.append(d_local)
        rings.append(lax.ppermute(d_local, ("fsdp", "tp"), ring_pairs))
        crosses.append(lax.ppermute(d_local, ("fsdp", "tp"), cross_pairs))

    def gathered(c):
        d_near = jnp.where(near, locals_[c], rings[c])
        d_far = jnp.where(near, rings[c], crosses[c])
        return jnp.concatenate([d_near, d_far], axis=0)

    def add_pseudo(d_all, lo, hi, after=None):
        at_cols = slice(lo * narrow, hi * narrow)
        piece = d_all[:, : (hi - lo) * narrow]
        if after in line.sums:
            piece, line.sums[after] = together(piece, line.sums[after])
        piece, first, second, outer = together(piece, first_moment, second_moment, weight)
        grad = lax.dot_general(
            context_all, piece, (((0,), (0,)), ((), ())), preferred_element_type=f32
        ) / (tok_rows * fsdp_count)
        first = first[0, :, at_cols].astype(f32)
        second = second[0, :, at_cols].astype(f32)
        m_new = beta_one * first + (1.0 - beta_one) * grad
        v_new = beta_two * second + (1.0 - beta_two) * grad * grad
        update = m_new / bias_one / (
            jnp.sqrt(v_new / bias_two) + adam_eps
        ) + decay_rate * outer[:, at_cols].astype(f32)
        pseudo = lax.optimization_barrier(update.astype(bf16))
        for u in range(hi - lo):
            line.part[len(parts)] = pseudo[:, u * narrow : (u + 1) * narrow]
            parts.append(line.part[len(parts)])

    move(0)
    move(1)
    add_pseudo(gathered(0), 0, 1)
    early = sum(widths[:2])
    middle = gathered(1)
    for lo in range(1, early, 2):
        add_pseudo(middle[:, (lo - 1) * narrow :], lo, min(lo + 2, early))
        if lo == 1:
            move(2)
            line.part[1] = parts[1]
    last = gathered(2)
    todo = [(lo, min(lo + 2, units)) for lo in range(early, units, 2)]
    if islands == 4:
        for s in range(2):
            line.send_outer(s)
        for s in range(units + 3):
            while todo and todo[0][0] - 3 <= s:
                lo, hi = todo.pop(0)
                add_pseudo(last[:, (lo - early) * narrow :], lo, hi, s - 1)
            line.step(s)
        sums = [line.totals[k] for k in range(units)]
    else:
        for lo, hi in todo:
            add_pseudo(last[:, (lo - early) * narrow :], lo, hi)
        sums = [lax.psum(part, "island") for part in parts]
    momentum_out, step_out = [], []
    for k, total in enumerate(sums):
        cols_at = slice(k * narrow, (k + 1) * narrow)
        delta = total.astype(f32) / islands
        new_momentum, outer_step = outer_update(delta, momentum[:, cols_at])
        momentum_out.append(new_momentum)
        step_out.append(outer_step)
    return (jnp.concatenate(momentum_out, axis=1), jnp.concatenate(step_out, axis=1))


def solution(mesh):
    in_specs = (
        P(("island", "fsdp"), "tp"),
        P(("island", "fsdp"), "tp"),
        P(("island", "fsdp"), "tp"),
        P(),
        P("tp", "fsdp"),
        P("island", "tp", "fsdp"),
        P("island", "tp", "fsdp"),
        P("tp", "fsdp"),
    )
    out_specs = (P("tp", "fsdp"), P("tp", "fsdp"))
    return jax.shard_map(body, mesh=mesh, in_specs=in_specs, out_specs=out_specs, check_vma=False)
```

```python
import jax
import jax.numpy as jnp
from jax import lax
from jax.sharding import PartitionSpec as P

norm_eps = 1e-06
adam_eps = 1e-08
beta_one = 0.9
beta_two = 0.999
bias_one = 1.0 - 0.9**10
bias_two = 1.0 - 0.999**10
decay_rate = 0.1
outer_mu = 0.9

f32 = jnp.float32
bf16 = jnp.bfloat16


def outer_update(delta, momentum):
    new_momentum = outer_mu * momentum + delta
    outer_step = (delta + outer_mu * new_momentum).astype(bf16)
    return (new_momentum, outer_step)


def swap(value, axis, bit):
    count = lax.axis_size(axis)
    return lax.ppermute(value, axis, [(i, i ^ bit) for i in range(count)])


def together(*values):
    return lax.optimization_barrier(values)


class IslandLine:
    def __init__(self, chunks):
        self.chunks = chunks
        me = lax.axis_index("island")
        self.outer = (me == 0) | (me == 3)
        self.part, self.paid, self.edge, self.mid, self.sums, self.totals = {}, {}, {}, {}, {}, {}

    def send_outer(self, s):
        if s >= self.chunks + 3:
            return
        pairs = [(0, 1), (3, 2)] if s < self.chunks else []
        if s >= 3:
            pairs = pairs + [(1, 0), (2, 3)]
            total = (self.sums[s - 3].astype(f32) + self.mid[s - 3].astype(f32)).astype(bf16)
            payload = jnp.where(self.outer, self.part[s], total) if s < self.chunks else total
        else:
            payload = self.part[s]
        self.paid[s] = payload
        self.edge[s] = lax.ppermute(payload, "island", pairs)

    def step(self, s):
        edge = self.edge[s]
        if s + 1 in self.paid:
            edge, self.paid[s + 1] = together(edge, self.paid[s + 1])
        if s < self.chunks:
            self.sums[s] = (edge.astype(f32) + self.part[s].astype(f32)).astype(bf16)
            self.mid[s] = lax.ppermute(self.sums[s], "island", [(1, 2), (2, 1)])
            if s >= 1:
                self.mid[s - 1], self.sums[s] = together(self.mid[s - 1], self.sums[s])
        self.send_outer(s + 2)
        if s >= 3:
            if s + 2 in self.paid:
                edge, self.paid[s], self.paid[s + 2] = together(edge, self.paid[s], self.paid[s + 2])
            else:
                edge, self.paid[s] = together(edge, self.paid[s])
            self.totals[s - 3] = jnp.where(self.outer, edge, self.paid[s])


def body(context, residual, cotangent, gain, weight, first_moment, second_moment, momentum):
    tok_rows = context.shape[0]
    width = gain.shape[0]
    fsdp_count = lax.axis_size("fsdp")
    group = fsdp_count // 2
    cols = weight.shape[1]
    t = lax.axis_index("tp")
    f = lax.axis_index("fsdp")
    high = f // group
    low = f % group
    near = t == high

    pieces = 2
    rows = tok_rows // pieces

    def project(block):
        return lax.optimization_barrier(
            jnp.dot(block, weight, preferred_element_type=f32).astype(bf16)
        )

    def at(h, q, x):
        return (h * group + q) * 2 + x

    ring_pairs, cross_pairs = [], []
    for q in range(group):
        ring_pairs += [(at(x, q, x), at(x, q, 1 - x)) for x in (0, 1)]
        ring_pairs += [(at(1 - x, q, x), at(x, q, x)) for x in (0, 1)]
        cross_pairs += [(at(1 - x, q, x), at(x, q, 1 - x)) for x in (0, 1)]
    inward_pairs = [(at(1 - x, q, x), at(1 - x, q, 1 - x)) for q in range(group) for x in (0, 1)]
    outward_pairs = [(at(x, q, x), at(x, q, 1 - x)) for q in range(group) for x in (0, 1)]

    near_blocks = [context] + [swap(context, "fsdp", r) for r in range(1, group)]
    slices = [
        [lax.dynamic_slice_in_dim(array, (low ^ r) * cols, cols, axis=1) for r in range(group)]
        for array in (residual, cotangent)
    ]
    moved = [[swap(parts[r], "fsdp", r) if r else parts[r] for r in range(group)] for parts in slices]
    held = together(swap(context, "fsdp", group), *moved[0], *moved[1])
    residual_parts, cotangent_parts = held[1 : 1 + group], held[1 + group :]
    far_blocks = [held[0]] + [swap(held[0], "fsdp", r) for r in range(1, group)]
    near_out = project(jnp.concatenate(near_blocks, axis=0))
    near_came = lax.ppermute(near_out, ("fsdp", "tp"), inward_pairs)
    far_blocks[0], near_out = together(far_blocks[0], near_out)
    far_outs = [
        swap(project(far_blocks[r][p * rows : (p + 1) * rows]), "fsdp", group)
        for r in range(group)
        for p in range(pieces)
    ]
    passed = [lax.ppermute(out, ("fsdp", "tp"), outward_pairs) for out in far_outs]

    gain_part = lax.dynamic_slice_in_dim(gain, t * (width // 2) + low * cols, cols).astype(f32)

    hidden, weighted, sums = [], [], []
    for k in range(group * pieces):
        r, p = k // pieces, k % pieces
        span, long_span = slice(p * rows, (p + 1) * rows), slice(k * rows, (k + 1) * rows)
        keep = jnp.where(near, near_out[long_span], far_outs[k])
        base, w = lax.optimization_barrier(
            (
                residual_parts[r][span].astype(f32) + keep.astype(f32),
                gain_part[None, :] * cotangent_parts[r][span].astype(f32),
            )
        )
        came = passed[k]
        if sums:
            came, sums[-1] = together(came, sums[-1])
        h = base + jnp.where(near, near_came[long_span], came).astype(f32)
        hidden.append(h)
        weighted.append(w)
        sums.append(jnp.stack([jnp.sum(h * h, axis=-1), jnp.sum(h * w, axis=-1)]))
    own_sums = jnp.concatenate(sums, axis=1)
    totals = own_sums
    for r in range(1, group):
        came = swap(own_sums, "fsdp", r)
        order = [r ^ k for k in range(group)]
        came = jnp.concatenate(
            [came[:, k * tok_rows : (k + 1) * tok_rows] for k in order], axis=1
        )
        totals = totals + came
    totals = totals + swap(totals, "tp", 1)
    inv_rms = lax.rsqrt(totals[0] / width + norm_eps)
    pull = inv_rms**3 * totals[1] / width

    context_all = jnp.concatenate(near_blocks + far_blocks, axis=0)
    narrow = 128
    units = cols // narrow
    widths = [3, units - 3]
    islands = lax.axis_size("island")
    line = IslandLine(units)
    parts, locals_, rings, crosses = [], [], [], []

    def move(c):
        cols_at = slice(sum(widths[:c]) * narrow, sum(widths[: c + 1]) * narrow)
        d_local = jnp.concatenate(
            [
                weighted[j][:, cols_at] * inv_rms[j * rows : (j + 1) * rows, None]
                - hidden[j][:, cols_at] * pull[j * rows : (j + 1) * rows, None]
                for j in range(group * pieces)
            ],
            axis=0,
        ).astype(bf16)
        locals_.append(d_local)
        rings.append(lax.ppermute(d_local, ("fsdp", "tp"), ring_pairs))
        crosses.append(lax.ppermute(d_local, ("fsdp", "tp"), cross_pairs))

    def gathered(c):
        d_near = jnp.where(near, locals_[c], rings[c])
        d_far = jnp.where(near, rings[c], crosses[c])
        return jnp.concatenate([d_near, d_far], axis=0)

    def add_pseudo(d_all, lo, hi, after=None):
        at_cols = slice(lo * narrow, hi * narrow)
        piece = d_all[:, : (hi - lo) * narrow]
        if after in line.sums:
            piece, line.sums[after] = together(piece, line.sums[after])
        piece, first, second, outer = together(piece, first_moment, second_moment, weight)
        grad = lax.dot_general(
            context_all, piece, (((0,), (0,)), ((), ())), preferred_element_type=f32
        ) / (tok_rows * fsdp_count)
        first = first[0, :, at_cols].astype(f32)
        second = second[0, :, at_cols].astype(f32)
        m_new = beta_one * first + (1.0 - beta_one) * grad
        v_new = beta_two * second + (1.0 - beta_two) * grad * grad
        update = m_new / bias_one / (
            jnp.sqrt(v_new / bias_two) + adam_eps
        ) + decay_rate * outer[:, at_cols].astype(f32)
        pseudo = lax.optimization_barrier(update.astype(bf16))
        for u in range(hi - lo):
            line.part[len(parts)] = pseudo[:, u * narrow : (u + 1) * narrow]
            parts.append(line.part[len(parts)])

    for c in range(len(widths)):
        move(c)
    early = widths[0]
    found = gathered(0)
    add_pseudo(found, 0, 1)
    add_pseudo(found[:, narrow:], 1, early)
    last = gathered(1)
    todo = [(lo, min(lo + 2, units)) for lo in range(early, units, 2)]
    if islands == 4:
        for s in range(2):
            line.send_outer(s)
        for s in range(units + 3):
            while todo and todo[0][0] - 3 <= s:
                lo, hi = todo.pop(0)
                add_pseudo(last[:, (lo - early) * narrow :], lo, hi, s - 1)
            line.step(s)
        sums = [line.totals[k] for k in range(units)]
    else:
        for lo, hi in todo:
            add_pseudo(last[:, (lo - early) * narrow :], lo, hi)
        sums = [lax.psum(part, "island") for part in parts]
    momentum_out, step_out = [], []
    for k, total in enumerate(sums):
        cols_at = slice(k * narrow, (k + 1) * narrow)
        delta = total.astype(f32) / islands
        new_momentum, outer_step = outer_update(delta, momentum[:, cols_at])
        momentum_out.append(new_momentum)
        step_out.append(outer_step)
    return (jnp.concatenate(momentum_out, axis=1), jnp.concatenate(step_out, axis=1))


def solution(mesh):
    in_specs = (
        P(("island", "fsdp"), "tp"),
        P(("island", "fsdp"), "tp"),
        P(("island", "fsdp"), "tp"),
        P(),
        P("tp", "fsdp"),
        P("island", "tp", "fsdp"),
        P("island", "tp", "fsdp"),
        P("tp", "fsdp"),
    )
    out_specs = (P("tp", "fsdp"), P("tp", "fsdp"))
    return jax.shard_map(body, mesh=mesh, in_specs=in_specs, out_specs=out_specs, check_vma=False)
```

```python
import jax
import jax.numpy as jnp
from jax import lax
from jax.sharding import PartitionSpec as P

norm_eps = 1e-06
adam_eps = 1e-08
beta_one = 0.9
beta_two = 0.999
bias_one = 1.0 - 0.9**10
bias_two = 1.0 - 0.999**10
decay_rate = 0.1
outer_mu = 0.9

f32 = jnp.float32
bf16 = jnp.bfloat16


def outer_update(delta, momentum):
    new_momentum = outer_mu * momentum + delta
    outer_step = (delta + outer_mu * new_momentum).astype(bf16)
    return (new_momentum, outer_step)


def swap(value, axis, bit):
    count = lax.axis_size(axis)
    return lax.ppermute(value, axis, [(i, i ^ bit) for i in range(count)])


def together(*values):
    return lax.optimization_barrier(values)


class IslandLine:
    def __init__(self, chunks):
        self.chunks = chunks
        me = lax.axis_index("island")
        self.outer = (me == 0) | (me == 3)
        self.part, self.paid, self.edge, self.mid, self.sums, self.totals = {}, {}, {}, {}, {}, {}

    def send_outer(self, s):
        if s >= self.chunks + 3:
            return
        pairs = [(0, 1), (3, 2)] if s < self.chunks else []
        if s >= 3:
            pairs = pairs + [(1, 0), (2, 3)]
            total = (self.sums[s - 3].astype(f32) + self.mid[s - 3].astype(f32)).astype(bf16)
            payload = jnp.where(self.outer, self.part[s], total) if s < self.chunks else total
        else:
            payload = self.part[s]
        self.paid[s] = payload
        self.edge[s] = lax.ppermute(payload, "island", pairs)

    def step(self, s):
        edge = self.edge[s]
        if s + 1 in self.paid:
            edge, self.paid[s + 1] = together(edge, self.paid[s + 1])
        if s < self.chunks:
            self.sums[s] = (edge.astype(f32) + self.part[s].astype(f32)).astype(bf16)
            self.mid[s] = lax.ppermute(self.sums[s], "island", [(1, 2), (2, 1)])
            if s >= 1:
                self.mid[s - 1], self.sums[s] = together(self.mid[s - 1], self.sums[s])
        self.send_outer(s + 2)
        if s >= 3:
            if s + 2 in self.paid:
                edge, self.paid[s], self.paid[s + 2] = together(edge, self.paid[s], self.paid[s + 2])
            else:
                edge, self.paid[s] = together(edge, self.paid[s])
            self.totals[s - 3] = jnp.where(self.outer, edge, self.paid[s])


def body(context, residual, cotangent, gain, weight, first_moment, second_moment, momentum):
    tok_rows = context.shape[0]
    width = gain.shape[0]
    fsdp_count = lax.axis_size("fsdp")
    group = fsdp_count // 2
    cols = weight.shape[1]
    t = lax.axis_index("tp")
    f = lax.axis_index("fsdp")
    high = f // group
    low = f % group
    near = t == high

    pieces = 2
    rows = tok_rows // pieces

    def project(block):
        return lax.optimization_barrier(
            jnp.dot(block, weight, preferred_element_type=f32).astype(bf16)
        )

    def at(h, q, x):
        return (h * group + q) * 2 + x

    ring_pairs, cross_pairs = [], []
    for q in range(group):
        ring_pairs += [(at(x, q, x), at(x, q, 1 - x)) for x in (0, 1)]
        ring_pairs += [(at(1 - x, q, x), at(x, q, x)) for x in (0, 1)]
        cross_pairs += [(at(1 - x, q, x), at(x, q, 1 - x)) for x in (0, 1)]
    inward_pairs = [(at(1 - x, q, x), at(1 - x, q, 1 - x)) for q in range(group) for x in (0, 1)]
    outward_pairs = [(at(x, q, x), at(x, q, 1 - x)) for q in range(group) for x in (0, 1)]

    near_blocks = [context] + [swap(context, "fsdp", r) for r in range(1, group)]
    slices = [
        [lax.dynamic_slice_in_dim(array, (low ^ r) * cols, cols, axis=1) for r in range(group)]
        for array in (residual, cotangent)
    ]
    moved = [[swap(parts[r], "fsdp", r) if r else parts[r] for r in range(group)] for parts in slices]
    held = together(swap(context, "fsdp", group), *moved[0], *moved[1])
    residual_parts, cotangent_parts = held[1 : 1 + group], held[1 + group :]
    far_blocks = [held[0]] + [swap(held[0], "fsdp", r) for r in range(1, group)]
    far_outs = []
    for k in range(group * pieces):
        r, p = k // pieces, k % pieces
        blocks = [far_blocks[r][p * rows : (p + 1) * rows]]
        if k == group * pieces - 1:
            blocks += near_blocks
        out = project(jnp.concatenate(blocks, axis=0))
        far_outs.append(swap(out[:rows], "fsdp", group))
    near_out = out[rows:]
    near_came = lax.ppermute(near_out, ("fsdp", "tp"), inward_pairs)
    passed = [lax.ppermute(out, ("fsdp", "tp"), outward_pairs) for out in far_outs]

    gain_part = lax.dynamic_slice_in_dim(gain, t * (width // 2) + low * cols, cols).astype(f32)

    hidden, weighted, sums = [], [], []
    for k in range(group * pieces):
        r, p = k // pieces, k % pieces
        span, long_span = slice(p * rows, (p + 1) * rows), slice(k * rows, (k + 1) * rows)
        far_out, came = far_outs[k], passed[k]
        if sums:
            far_out, sums[-1] = together(far_out, sums[-1])
        keep = jnp.where(near, near_out[long_span], far_out)
        base, w = lax.optimization_barrier(
            (
                residual_parts[r][span].astype(f32) + keep.astype(f32),
                gain_part[None, :] * cotangent_parts[r][span].astype(f32),
            )
        )
        h = base + jnp.where(near, near_came[long_span], came).astype(f32)
        hidden.append(h)
        weighted.append(w)
        sums.append(jnp.stack([jnp.sum(h * h, axis=-1), jnp.sum(h * w, axis=-1)]))
    own_sums = jnp.concatenate(sums, axis=1)
    totals = own_sums
    for r in range(1, group):
        came = swap(own_sums, "fsdp", r)
        order = [r ^ k for k in range(group)]
        came = jnp.concatenate(
            [came[:, k * tok_rows : (k + 1) * tok_rows] for k in order], axis=1
        )
        totals = totals + came
    totals = totals + swap(totals, "tp", 1)
    inv_rms = lax.rsqrt(totals[0] / width + norm_eps)
    pull = inv_rms**3 * totals[1] / width

    context_all = jnp.concatenate(near_blocks + far_blocks, axis=0)
    narrow = 128
    units = cols // narrow
    widths = [1, 3, units - 4]
    islands = lax.axis_size("island")
    line = IslandLine(units)
    parts, locals_, rings, crosses = [], [], [], []

    def move(c):
        cols_at = slice(sum(widths[:c]) * narrow, sum(widths[: c + 1]) * narrow)
        d_local = jnp.concatenate(
            [
                weighted[j][:, cols_at] * inv_rms[j * rows : (j + 1) * rows, None]
                - hidden[j][:, cols_at] * pull[j * rows : (j + 1) * rows, None]
                for j in range(group * pieces)
            ],
            axis=0,
        ).astype(bf16)
        if c == 1:
            d_local, rings[0] = together(d_local, rings[0])
        elif c == 2:
            d_local, crosses[0] = together(d_local, crosses[0])
        locals_.append(d_local)
        rings.append(lax.ppermute(d_local, ("fsdp", "tp"), ring_pairs))
        crosses.append(lax.ppermute(d_local, ("fsdp", "tp"), cross_pairs))

    def gathered(c):
        d_near = jnp.where(near, locals_[c], rings[c])
        d_far = jnp.where(near, rings[c], crosses[c])
        return jnp.concatenate([d_near, d_far], axis=0)

    def add_pseudo(d_all, lo, hi, after=None):
        at_cols = slice(lo * narrow, hi * narrow)
        piece = d_all[:, : (hi - lo) * narrow]
        if after in line.sums:
            piece, line.sums[after] = together(piece, line.sums[after])
        piece, first, second, outer = together(piece, first_moment, second_moment, weight)
        grad = lax.dot_general(
            context_all, piece, (((0,), (0,)), ((), ())), preferred_element_type=f32
        ) / (tok_rows * fsdp_count)
        first = first[0, :, at_cols].astype(f32)
        second = second[0, :, at_cols].astype(f32)
        m_new = beta_one * first + (1.0 - beta_one) * grad
        v_new = beta_two * second + (1.0 - beta_two) * grad * grad
        update = m_new / bias_one / (
            jnp.sqrt(v_new / bias_two) + adam_eps
        ) + decay_rate * outer[:, at_cols].astype(f32)
        pseudo = lax.optimization_barrier(update.astype(bf16))
        for u in range(hi - lo):
            line.part[len(parts)] = pseudo[:, u * narrow : (u + 1) * narrow]
            parts.append(line.part[len(parts)])

    for c in range(len(widths)):
        move(c)
    add_pseudo(gathered(0), 0, 1)
    found = gathered(1)
    early = sum(widths[:2])
    add_pseudo(found, 1, 2)
    add_pseudo(found[:, narrow:], 2, early)
    last = gathered(2)
    todo = [(lo, min(lo + 2, units)) for lo in range(early, units, 2)]
    if islands == 4:
        for s in range(2):
            line.send_outer(s)
        for s in range(units + 3):
            while todo and todo[0][0] - 3 <= s:
                lo, hi = todo.pop(0)
                add_pseudo(last[:, (lo - early) * narrow :], lo, hi, s - 1)
            line.step(s)
        sums = [line.totals[k] for k in range(units)]
    else:
        for lo, hi in todo:
            add_pseudo(last[:, (lo - early) * narrow :], lo, hi)
        sums = [lax.psum(part, "island") for part in parts]
    momentum_out, step_out = [], []
    for k, total in enumerate(sums):
        cols_at = slice(k * narrow, (k + 1) * narrow)
        delta = total.astype(f32) / islands
        new_momentum, outer_step = outer_update(delta, momentum[:, cols_at])
        momentum_out.append(new_momentum)
        step_out.append(outer_step)
    return (jnp.concatenate(momentum_out, axis=1), jnp.concatenate(step_out, axis=1))


def solution(mesh):
    in_specs = (
        P(("island", "fsdp"), "tp"),
        P(("island", "fsdp"), "tp"),
        P(("island", "fsdp"), "tp"),
        P(),
        P("tp", "fsdp"),
        P("island", "tp", "fsdp"),
        P("island", "tp", "fsdp"),
        P("tp", "fsdp"),
    )
    out_specs = (P("tp", "fsdp"), P("tp", "fsdp"))
    return jax.shard_map(body, mesh=mesh, in_specs=in_specs, out_specs=out_specs, check_vma=False)
```

```python
import jax
import jax.numpy as jnp
from jax import lax
from jax.sharding import PartitionSpec as P

norm_eps = 1e-06
adam_eps = 1e-08
beta_one = 0.9
beta_two = 0.999
bias_one = 1.0 - 0.9**10
bias_two = 1.0 - 0.999**10
decay_rate = 0.1
outer_mu = 0.9

f32 = jnp.float32
bf16 = jnp.bfloat16


def outer_update(delta, momentum):
    new_momentum = outer_mu * momentum + delta
    outer_step = (delta + outer_mu * new_momentum).astype(bf16)
    return (new_momentum, outer_step)


def swap(value, axis, bit):
    count = lax.axis_size(axis)
    return lax.ppermute(value, axis, [(i, i ^ bit) for i in range(count)])


def together(*values):
    return lax.optimization_barrier(values)


class IslandLine:
    def __init__(self, chunks):
        self.chunks = chunks
        me = lax.axis_index("island")
        self.outer = (me == 0) | (me == 3)
        self.part, self.paid, self.edge, self.mid, self.sums, self.totals = {}, {}, {}, {}, {}, {}

    def send_outer(self, s):
        if s >= self.chunks + 3:
            return
        pairs = [(0, 1), (3, 2)] if s < self.chunks else []
        if s >= 3:
            pairs = pairs + [(1, 0), (2, 3)]
            total = (self.sums[s - 3].astype(f32) + self.mid[s - 3].astype(f32)).astype(bf16)
            payload = jnp.where(self.outer, self.part[s], total) if s < self.chunks else total
        else:
            payload = self.part[s]
        self.paid[s] = payload
        self.edge[s] = lax.ppermute(payload, "island", pairs)

    def step(self, s):
        edge = self.edge[s]
        if s + 1 in self.paid:
            edge, self.paid[s + 1] = together(edge, self.paid[s + 1])
        if s < self.chunks:
            self.sums[s] = (edge.astype(f32) + self.part[s].astype(f32)).astype(bf16)
            self.mid[s] = lax.ppermute(self.sums[s], "island", [(1, 2), (2, 1)])
            if s >= 1:
                self.mid[s - 1], self.sums[s] = together(self.mid[s - 1], self.sums[s])
        self.send_outer(s + 2)
        if s >= 3:
            if s + 2 in self.paid:
                edge, self.paid[s], self.paid[s + 2] = together(edge, self.paid[s], self.paid[s + 2])
            else:
                edge, self.paid[s] = together(edge, self.paid[s])
            self.totals[s - 3] = jnp.where(self.outer, edge, self.paid[s])


def body(context, residual, cotangent, gain, weight, first_moment, second_moment, momentum):
    tok_rows = context.shape[0]
    width = gain.shape[0]
    fsdp_count = lax.axis_size("fsdp")
    group = fsdp_count // 2
    cols = weight.shape[1]
    t = lax.axis_index("tp")
    f = lax.axis_index("fsdp")
    high = f // group
    low = f % group
    near = t == high

    pieces = 2
    rows = tok_rows // pieces

    def project(block):
        return lax.optimization_barrier(
            jnp.dot(block, weight, preferred_element_type=f32).astype(bf16)
        )

    def at(h, q, x):
        return (h * group + q) * 2 + x

    ring_pairs, cross_pairs = [], []
    for q in range(group):
        ring_pairs += [(at(x, q, x), at(x, q, 1 - x)) for x in (0, 1)]
        ring_pairs += [(at(1 - x, q, x), at(x, q, x)) for x in (0, 1)]
        cross_pairs += [(at(1 - x, q, x), at(x, q, 1 - x)) for x in (0, 1)]
    inward_pairs = [(at(1 - x, q, x), at(1 - x, q, 1 - x)) for q in range(group) for x in (0, 1)]
    outward_pairs = [(at(x, q, x), at(x, q, 1 - x)) for q in range(group) for x in (0, 1)]

    near_blocks = [context] + [swap(context, "fsdp", r) for r in range(1, group)]
    slices = [
        [lax.dynamic_slice_in_dim(array, (low ^ r) * cols, cols, axis=1) for r in range(group)]
        for array in (residual, cotangent)
    ]
    moved = [[swap(parts[r], "fsdp", r) if r else parts[r] for r in range(group)] for parts in slices]
    held = together(swap(context, "fsdp", group), *moved[0], *moved[1])
    residual_parts, cotangent_parts = held[1 : 1 + group], held[1 + group :]
    far_blocks = [held[0]] + [swap(held[0], "fsdp", r) for r in range(1, group)]
    far_outs, near_out, passed, near_came = [], [], [], []
    for k in range(group * pieces):
        r, p = k // pieces, k % pieces
        far = far_blocks[r]
        if 1 <= k <= group:
            far, near_out[k - 1] = together(far, near_out[k - 1])
        if k >= 2:
            far, far_outs[k - 2] = together(far, far_outs[k - 2])
        blocks = [far[p * rows : (p + 1) * rows]] + near_blocks[k : k + 1]
        out = project(jnp.concatenate(blocks, axis=0))
        far_outs.append(swap(out[:rows], "fsdp", group))
        passed.append(lax.ppermute(far_outs[k], ("fsdp", "tp"), outward_pairs))
        if k < group:
            near_out.append(out[rows:])
            near_came.append(lax.ppermute(near_out[k], ("fsdp", "tp"), inward_pairs))

    gain_part = lax.dynamic_slice_in_dim(gain, t * (width // 2) + low * cols, cols).astype(f32)

    hidden, weighted, sums = [], [], []
    for k in range(group * pieces):
        r, p = k // pieces, k % pieces
        span = slice(p * rows, (p + 1) * rows)
        far_out, came = far_outs[k], passed[k]
        if sums:
            far_out, sums[-1] = together(far_out, sums[-1])
        keep = jnp.where(near, near_out[r][span], far_out)
        base, w = lax.optimization_barrier(
            (
                residual_parts[r][span].astype(f32) + keep.astype(f32),
                gain_part[None, :] * cotangent_parts[r][span].astype(f32),
            )
        )
        h = base + jnp.where(near, near_came[r][span], came).astype(f32)
        hidden.append(h)
        weighted.append(w)
        sums.append(jnp.stack([jnp.sum(h * h, axis=-1), jnp.sum(h * w, axis=-1)]))
    own_sums = jnp.concatenate(sums, axis=1)
    totals = own_sums
    for r in range(1, group):
        came = swap(own_sums, "fsdp", r)
        order = [r ^ k for k in range(group)]
        came = jnp.concatenate(
            [came[:, k * tok_rows : (k + 1) * tok_rows] for k in order], axis=1
        )
        totals = totals + came
    totals = totals + swap(totals, "tp", 1)
    inv_rms = lax.rsqrt(totals[0] / width + norm_eps)
    pull = inv_rms**3 * totals[1] / width

    context_all = jnp.concatenate(near_blocks + far_blocks, axis=0)
    narrow = 128
    units = cols // narrow
    widths = [1, 3, units - 4]
    islands = lax.axis_size("island")
    line = IslandLine(units)
    parts, locals_, rings, crosses = [], [], [], []

    def move(c):
        cols_at = slice(sum(widths[:c]) * narrow, sum(widths[: c + 1]) * narrow)
        d_local = jnp.concatenate(
            [
                weighted[j][:, cols_at] * inv_rms[j * rows : (j + 1) * rows, None]
                - hidden[j][:, cols_at] * pull[j * rows : (j + 1) * rows, None]
                for j in range(group * pieces)
            ],
            axis=0,
        ).astype(bf16)
        if c == 1:
            d_local, rings[0] = together(d_local, rings[0])
        elif c == 2:
            d_local, crosses[0] = together(d_local, crosses[0])
        locals_.append(d_local)
        rings.append(lax.ppermute(d_local, ("fsdp", "tp"), ring_pairs))
        crosses.append(lax.ppermute(d_local, ("fsdp", "tp"), cross_pairs))

    def gathered(c):
        d_near = jnp.where(near, locals_[c], rings[c])
        d_far = jnp.where(near, rings[c], crosses[c])
        return jnp.concatenate([d_near, d_far], axis=0)

    def add_pseudo(d_all, lo, hi, after=None):
        at_cols = slice(lo * narrow, hi * narrow)
        piece = d_all[:, : (hi - lo) * narrow]
        if after in line.sums:
            piece, line.sums[after] = together(piece, line.sums[after])
        piece, first, second, outer = together(piece, first_moment, second_moment, weight)
        grad = lax.dot_general(
            context_all, piece, (((0,), (0,)), ((), ())), preferred_element_type=f32
        ) / (tok_rows * fsdp_count)
        first = first[0, :, at_cols].astype(f32)
        second = second[0, :, at_cols].astype(f32)
        m_new = beta_one * first + (1.0 - beta_one) * grad
        v_new = beta_two * second + (1.0 - beta_two) * grad * grad
        update = m_new / bias_one / (
            jnp.sqrt(v_new / bias_two) + adam_eps
        ) + decay_rate * outer[:, at_cols].astype(f32)
        pseudo = lax.optimization_barrier(update.astype(bf16))
        for u in range(hi - lo):
            line.part[len(parts)] = pseudo[:, u * narrow : (u + 1) * narrow]
            parts.append(line.part[len(parts)])

    for c in range(len(widths)):
        move(c)
    add_pseudo(gathered(0), 0, 1)
    found = gathered(1)
    early = sum(widths[:2])
    add_pseudo(found, 1, 2)
    add_pseudo(found[:, narrow:], 2, early)
    last = gathered(2)
    todo = [(lo, min(lo + 2, units)) for lo in range(early, units, 2)]
    if islands == 4:
        for s in range(2):
            line.send_outer(s)
        for s in range(units + 3):
            while todo and todo[0][0] - 3 <= s:
                lo, hi = todo.pop(0)
                add_pseudo(last[:, (lo - early) * narrow :], lo, hi, s - 1)
            line.step(s)
        sums = [line.totals[k] for k in range(units)]
    else:
        for lo, hi in todo:
            add_pseudo(last[:, (lo - early) * narrow :], lo, hi)
        sums = [lax.psum(part, "island") for part in parts]
    momentum_out, step_out = [], []
    for k, total in enumerate(sums):
        cols_at = slice(k * narrow, (k + 1) * narrow)
        delta = total.astype(f32) / islands
        new_momentum, outer_step = outer_update(delta, momentum[:, cols_at])
        momentum_out.append(new_momentum)
        step_out.append(outer_step)
    return (jnp.concatenate(momentum_out, axis=1), jnp.concatenate(step_out, axis=1))


def solution(mesh):
    in_specs = (
        P(("island", "fsdp"), "tp"),
        P(("island", "fsdp"), "tp"),
        P(("island", "fsdp"), "tp"),
        P(),
        P("tp", "fsdp"),
        P("island", "tp", "fsdp"),
        P("island", "tp", "fsdp"),
        P("tp", "fsdp"),
    )
    out_specs = (P("tp", "fsdp"), P("tp", "fsdp"))
    return jax.shard_map(body, mesh=mesh, in_specs=in_specs, out_specs=out_specs, check_vma=False)
```

```python
import jax
import jax.numpy as jnp
from jax import lax
from jax.sharding import PartitionSpec as P

norm_eps = 1e-06
adam_eps = 1e-08
beta_one = 0.9
beta_two = 0.999
bias_one = 1.0 - 0.9**10
bias_two = 1.0 - 0.999**10
decay_rate = 0.1
outer_mu = 0.9

f32 = jnp.float32
bf16 = jnp.bfloat16


def outer_update(delta, momentum):
    new_momentum = outer_mu * momentum + delta
    outer_step = (delta + outer_mu * new_momentum).astype(bf16)
    return (new_momentum, outer_step)


def swap(value, axis, bit):
    count = lax.axis_size(axis)
    return lax.ppermute(value, axis, [(i, i ^ bit) for i in range(count)])


def together(*values):
    return lax.optimization_barrier(values)


class IslandLine:
    def __init__(self, chunks):
        self.chunks = chunks
        me = lax.axis_index("island")
        self.outer = (me == 0) | (me == 3)
        self.part, self.paid, self.edge, self.mid, self.sums, self.totals = {}, {}, {}, {}, {}, {}

    def send_outer(self, s):
        if s >= self.chunks + 3:
            return
        pairs = [(0, 1), (3, 2)] if s < self.chunks else []
        if s >= 3:
            pairs = pairs + [(1, 0), (2, 3)]
            total = (self.sums[s - 3].astype(f32) + self.mid[s - 3].astype(f32)).astype(bf16)
            payload = jnp.where(self.outer, self.part[s], total) if s < self.chunks else total
        else:
            payload = self.part[s]
        self.paid[s] = payload
        self.edge[s] = lax.ppermute(payload, "island", pairs)

    def step(self, s):
        edge = self.edge[s]
        if s + 1 in self.paid:
            edge, self.paid[s + 1] = together(edge, self.paid[s + 1])
        if s < self.chunks:
            self.sums[s] = (edge.astype(f32) + self.part[s].astype(f32)).astype(bf16)
            self.mid[s] = lax.ppermute(self.sums[s], "island", [(1, 2), (2, 1)])
            if s >= 1:
                self.mid[s - 1], self.sums[s] = together(self.mid[s - 1], self.sums[s])
        self.send_outer(s + 2)
        if s >= 3:
            if s + 2 in self.paid:
                edge, self.paid[s], self.paid[s + 2] = together(edge, self.paid[s], self.paid[s + 2])
            else:
                edge, self.paid[s] = together(edge, self.paid[s])
            self.totals[s - 3] = jnp.where(self.outer, edge, self.paid[s])


def body(context, residual, cotangent, gain, weight, first_moment, second_moment, momentum):
    tok_rows = context.shape[0]
    width = gain.shape[0]
    fsdp_count = lax.axis_size("fsdp")
    group = fsdp_count // 2
    cols = weight.shape[1]
    t = lax.axis_index("tp")
    f = lax.axis_index("fsdp")
    high = f // group
    low = f % group
    near = t == high

    pieces = 2
    rows = tok_rows // pieces

    def project(block):
        return lax.optimization_barrier(
            jnp.dot(block, weight, preferred_element_type=f32).astype(bf16)
        )

    def at(h, q, x):
        return (h * group + q) * 2 + x

    ring_pairs, cross_pairs = [], []
    for q in range(group):
        ring_pairs += [(at(x, q, x), at(x, q, 1 - x)) for x in (0, 1)]
        ring_pairs += [(at(1 - x, q, x), at(x, q, x)) for x in (0, 1)]
        cross_pairs += [(at(1 - x, q, x), at(x, q, 1 - x)) for x in (0, 1)]
    inward_pairs = [(at(1 - x, q, x), at(1 - x, q, 1 - x)) for q in range(group) for x in (0, 1)]
    outward_pairs = [(at(x, q, x), at(x, q, 1 - x)) for q in range(group) for x in (0, 1)]

    near_blocks = [context] + [swap(context, "fsdp", r) for r in range(1, group)]
    slices = [
        [lax.dynamic_slice_in_dim(array, (low ^ r) * cols, cols, axis=1) for r in range(group)]
        for array in (residual, cotangent)
    ]
    moved = [[swap(parts[r], "fsdp", r) if r else parts[r] for r in range(group)] for parts in slices]
    held = together(swap(context, "fsdp", group), *moved[0], *moved[1])
    residual_parts, cotangent_parts = held[1 : 1 + group], held[1 + group :]
    far_blocks = [held[0]] + [swap(held[0], "fsdp", r) for r in range(1, group)]
    near_out = project(jnp.concatenate(near_blocks, axis=0))
    near_came = lax.ppermute(near_out, ("fsdp", "tp"), inward_pairs)
    far_outs = []
    for r in range(group):
        out = project(far_blocks[r])
        far_outs += [swap(out[p * rows : (p + 1) * rows], "fsdp", group) for p in range(pieces)]
    passed = [lax.ppermute(out, ("fsdp", "tp"), outward_pairs) for out in far_outs]

    gain_part = lax.dynamic_slice_in_dim(gain, t * (width // 2) + low * cols, cols).astype(f32)

    hidden, weighted, sums = [], [], []
    for k in range(group * pieces):
        r, p = k // pieces, k % pieces
        span, long_span = slice(p * rows, (p + 1) * rows), slice(k * rows, (k + 1) * rows)
        far_out, came = far_outs[k], passed[k]
        if sums:
            far_out, sums[-1] = together(far_out, sums[-1])
        keep = jnp.where(near, near_out[long_span], far_out)
        base, w = lax.optimization_barrier(
            (
                residual_parts[r][span].astype(f32) + keep.astype(f32),
                gain_part[None, :] * cotangent_parts[r][span].astype(f32),
            )
        )
        h = base + jnp.where(near, near_came[long_span], came).astype(f32)
        hidden.append(h)
        weighted.append(w)
        sums.append(jnp.stack([jnp.sum(h * h, axis=-1), jnp.sum(h * w, axis=-1)]))
    own_sums = jnp.concatenate(sums, axis=1)
    totals = own_sums
    for r in range(1, group):
        came = swap(own_sums, "fsdp", r)
        order = [r ^ k for k in range(group)]
        came = jnp.concatenate(
            [came[:, k * tok_rows : (k + 1) * tok_rows] for k in order], axis=1
        )
        totals = totals + came
    totals = totals + swap(totals, "tp", 1)
    inv_rms = lax.rsqrt(totals[0] / width + norm_eps)
    pull = inv_rms**3 * totals[1] / width

    context_all = jnp.concatenate(near_blocks + far_blocks, axis=0)
    narrow = 128
    units = cols // narrow
    widths = [1, 3, units - 4]
    islands = lax.axis_size("island")
    line = IslandLine(units)
    parts, locals_, rings, crosses = [], [], [], []

    def move(c):
        cols_at = slice(sum(widths[:c]) * narrow, sum(widths[: c + 1]) * narrow)
        d_local = jnp.concatenate(
            [
                weighted[j][:, cols_at] * inv_rms[j * rows : (j + 1) * rows, None]
                - hidden[j][:, cols_at] * pull[j * rows : (j + 1) * rows, None]
                for j in range(group * pieces)
            ],
            axis=0,
        ).astype(bf16)
        if c == 1:
            d_local, rings[0] = together(d_local, rings[0])
        elif c == 2:
            d_local, crosses[0] = together(d_local, crosses[0])
        locals_.append(d_local)
        rings.append(lax.ppermute(d_local, ("fsdp", "tp"), ring_pairs))
        crosses.append(lax.ppermute(d_local, ("fsdp", "tp"), cross_pairs))

    def gathered(c):
        d_near = jnp.where(near, locals_[c], rings[c])
        d_far = jnp.where(near, rings[c], crosses[c])
        return jnp.concatenate([d_near, d_far], axis=0)

    def add_pseudo(d_all, lo, hi, after=None):
        at_cols = slice(lo * narrow, hi * narrow)
        piece = d_all[:, : (hi - lo) * narrow]
        if after in line.sums:
            piece, line.sums[after] = together(piece, line.sums[after])
        piece, first, second, outer = together(piece, first_moment, second_moment, weight)
        grad = lax.dot_general(
            context_all, piece, (((0,), (0,)), ((), ())), preferred_element_type=f32
        ) / (tok_rows * fsdp_count)
        first = first[0, :, at_cols].astype(f32)
        second = second[0, :, at_cols].astype(f32)
        m_new = beta_one * first + (1.0 - beta_one) * grad
        v_new = beta_two * second + (1.0 - beta_two) * grad * grad
        update = m_new / bias_one / (
            jnp.sqrt(v_new / bias_two) + adam_eps
        ) + decay_rate * outer[:, at_cols].astype(f32)
        pseudo = lax.optimization_barrier(update.astype(bf16))
        for u in range(hi - lo):
            line.part[len(parts)] = pseudo[:, u * narrow : (u + 1) * narrow]
            parts.append(line.part[len(parts)])

    for c in range(len(widths)):
        move(c)
    add_pseudo(gathered(0), 0, 1)
    found = gathered(1)
    early = sum(widths[:2])
    add_pseudo(found, 1, 2)
    add_pseudo(found[:, narrow:], 2, early)
    last = gathered(2)
    todo = [(lo, min(lo + 2, units)) for lo in range(early, units, 2)]
    if islands == 4:
        for s in range(2):
            line.send_outer(s)
        for s in range(units + 3):
            while todo and todo[0][0] - 3 <= s:
                lo, hi = todo.pop(0)
                add_pseudo(last[:, (lo - early) * narrow :], lo, hi, s - 1)
            line.step(s)
        sums = [line.totals[k] for k in range(units)]
    else:
        for lo, hi in todo:
            add_pseudo(last[:, (lo - early) * narrow :], lo, hi)
        sums = [lax.psum(part, "island") for part in parts]
    momentum_out, step_out = [], []
    for k, total in enumerate(sums):
        cols_at = slice(k * narrow, (k + 1) * narrow)
        delta = total.astype(f32) / islands
        new_momentum, outer_step = outer_update(delta, momentum[:, cols_at])
        momentum_out.append(new_momentum)
        step_out.append(outer_step)
    return (jnp.concatenate(momentum_out, axis=1), jnp.concatenate(step_out, axis=1))


def solution(mesh):
    in_specs = (
        P(("island", "fsdp"), "tp"),
        P(("island", "fsdp"), "tp"),
        P(("island", "fsdp"), "tp"),
        P(),
        P("tp", "fsdp"),
        P("island", "tp", "fsdp"),
        P("island", "tp", "fsdp"),
        P("tp", "fsdp"),
    )
    out_specs = (P("tp", "fsdp"), P("tp", "fsdp"))
    return jax.shard_map(body, mesh=mesh, in_specs=in_specs, out_specs=out_specs, check_vma=False)
```

```python
import jax
import jax.numpy as jnp
from jax import lax
from jax.sharding import PartitionSpec as P

norm_eps = 1e-06
adam_eps = 1e-08
beta_one = 0.9
beta_two = 0.999
bias_one = 1.0 - 0.9**10
bias_two = 1.0 - 0.999**10
decay_rate = 0.1
outer_mu = 0.9

f32 = jnp.float32
bf16 = jnp.bfloat16


def outer_update(delta, momentum):
    new_momentum = outer_mu * momentum + delta
    outer_step = (delta + outer_mu * new_momentum).astype(bf16)
    return (new_momentum, outer_step)


def swap(value, axis, bit):
    count = lax.axis_size(axis)
    return lax.ppermute(value, axis, [(i, i ^ bit) for i in range(count)])


def together(*values):
    return lax.optimization_barrier(values)


class IslandLine:
    def __init__(self, chunks):
        self.chunks = chunks
        me = lax.axis_index("island")
        self.outer = (me == 0) | (me == 3)
        self.part, self.paid, self.edge, self.mid, self.sums, self.totals = {}, {}, {}, {}, {}, {}

    def send_outer(self, s):
        if s >= self.chunks + 3:
            return
        pairs = [(0, 1), (3, 2)] if s < self.chunks else []
        if s >= 3:
            pairs = pairs + [(1, 0), (2, 3)]
            total = (self.sums[s - 3].astype(f32) + self.mid[s - 3].astype(f32)).astype(bf16)
            payload = jnp.where(self.outer, self.part[s], total) if s < self.chunks else total
        else:
            payload = self.part[s]
        self.paid[s] = payload
        self.edge[s] = lax.ppermute(payload, "island", pairs)

    def step(self, s):
        edge = self.edge[s]
        if s + 1 in self.paid:
            edge, self.paid[s + 1] = together(edge, self.paid[s + 1])
        if s < self.chunks:
            self.sums[s] = (edge.astype(f32) + self.part[s].astype(f32)).astype(bf16)
            self.mid[s] = lax.ppermute(self.sums[s], "island", [(1, 2), (2, 1)])
            if s >= 1:
                self.mid[s - 1], self.sums[s] = together(self.mid[s - 1], self.sums[s])
        self.send_outer(s + 2)
        if s >= 3:
            if s + 2 in self.paid:
                edge, self.paid[s], self.paid[s + 2] = together(edge, self.paid[s], self.paid[s + 2])
            else:
                edge, self.paid[s] = together(edge, self.paid[s])
            self.totals[s - 3] = jnp.where(self.outer, edge, self.paid[s])


def body(context, residual, cotangent, gain, weight, first_moment, second_moment, momentum):
    tok_rows = context.shape[0]
    width = gain.shape[0]
    fsdp_count = lax.axis_size("fsdp")
    group = fsdp_count // 2
    cols = weight.shape[1]
    t = lax.axis_index("tp")
    f = lax.axis_index("fsdp")
    high = f // group
    low = f % group
    near = t == high

    pieces = 2
    rows = tok_rows // pieces

    def project(block):
        return lax.optimization_barrier(
            jnp.dot(block, weight, preferred_element_type=f32).astype(bf16)
        )

    def at(h, q, x):
        return (h * group + q) * 2 + x

    ring_pairs, cross_pairs = [], []
    for q in range(group):
        ring_pairs += [(at(x, q, x), at(x, q, 1 - x)) for x in (0, 1)]
        ring_pairs += [(at(1 - x, q, x), at(x, q, x)) for x in (0, 1)]
        cross_pairs += [(at(1 - x, q, x), at(x, q, 1 - x)) for x in (0, 1)]
    inward_pairs = [(at(1 - x, q, x), at(1 - x, q, 1 - x)) for q in range(group) for x in (0, 1)]
    outward_pairs = [(at(x, q, x), at(x, q, 1 - x)) for q in range(group) for x in (0, 1)]

    near_blocks = [context] + [swap(context, "fsdp", r) for r in range(1, group)]
    slices = [
        [lax.dynamic_slice_in_dim(array, (low ^ r) * cols, cols, axis=1) for r in range(group)]
        for array in (residual, cotangent)
    ]
    moved = [[swap(parts[r], "fsdp", r) if r else parts[r] for r in range(group)] for parts in slices]
    held = together(swap(context, "fsdp", group), *moved[0], *moved[1])
    residual_parts, cotangent_parts = held[1 : 1 + group], held[1 + group :]
    far_blocks = [held[0]] + [swap(held[0], "fsdp", r) for r in range(1, group)]
    near_out = project(jnp.concatenate(near_blocks, axis=0))
    near_came = lax.ppermute(near_out, ("fsdp", "tp"), inward_pairs)
    far_outs = []
    for r in range(group):
        out = project(far_blocks[r])
        far_outs += [swap(out[p * rows : (p + 1) * rows], "fsdp", group) for p in range(pieces)]
    passed = [lax.ppermute(out, ("fsdp", "tp"), outward_pairs) for out in far_outs]

    gain_part = lax.dynamic_slice_in_dim(gain, t * (width // 2) + low * cols, cols).astype(f32)

    hidden, weighted, sums = [], [], []
    for k in range(group * pieces):
        r, p = k // pieces, k % pieces
        span, long_span = slice(p * rows, (p + 1) * rows), slice(k * rows, (k + 1) * rows)
        res, cot, came = residual_parts[r], cotangent_parts[r], passed[k]
        if sums:
            came, sums[-1] = together(came, sums[-1])
        keep = jnp.where(near, near_out[long_span], far_outs[k])
        came = jnp.where(near, near_came[long_span], came)
        h = res[span].astype(f32) + keep.astype(f32) + came.astype(f32)
        w = gain_part[None, :] * cot[span].astype(f32)
        hidden.append(h)
        weighted.append(w)
        sums.append(jnp.stack([jnp.sum(h * h, axis=-1), jnp.sum(h * w, axis=-1)]))
    own_sums = jnp.concatenate(sums, axis=1)
    totals = own_sums
    for r in range(1, group):
        came = swap(own_sums, "fsdp", r)
        order = [r ^ k for k in range(group)]
        came = jnp.concatenate(
            [came[:, k * tok_rows : (k + 1) * tok_rows] for k in order], axis=1
        )
        totals = totals + came
    totals = totals + swap(totals, "tp", 1)
    inv_rms = lax.rsqrt(totals[0] / width + norm_eps)
    pull = inv_rms**3 * totals[1] / width

    context_all = jnp.concatenate(near_blocks + far_blocks, axis=0)
    narrow = 128
    units = cols // narrow
    widths = [1, 3, units - 4]
    islands = lax.axis_size("island")
    line = IslandLine(units)
    parts, locals_, rings, crosses = [], [], [], []

    def move(c):
        cols_at = slice(sum(widths[:c]) * narrow, sum(widths[: c + 1]) * narrow)
        d_local = jnp.concatenate(
            [
                weighted[j][:, cols_at] * inv_rms[j * rows : (j + 1) * rows, None]
                - hidden[j][:, cols_at] * pull[j * rows : (j + 1) * rows, None]
                for j in range(group * pieces)
            ],
            axis=0,
        ).astype(bf16)
        if c == 1:
            d_local, rings[0] = together(d_local, rings[0])
        elif c == 2:
            d_local, crosses[0] = together(d_local, crosses[0])
        locals_.append(d_local)
        rings.append(lax.ppermute(d_local, ("fsdp", "tp"), ring_pairs))
        crosses.append(lax.ppermute(d_local, ("fsdp", "tp"), cross_pairs))

    def gathered(c):
        d_near = jnp.where(near, locals_[c], rings[c])
        d_far = jnp.where(near, rings[c], crosses[c])
        return jnp.concatenate([d_near, d_far], axis=0)

    def add_pseudo(d_all, lo, hi, after=None):
        at_cols = slice(lo * narrow, hi * narrow)
        piece = d_all[:, : (hi - lo) * narrow]
        if after in line.sums:
            piece, line.sums[after] = together(piece, line.sums[after])
        piece, first, second, outer = together(piece, first_moment, second_moment, weight)
        grad = lax.dot_general(
            context_all, piece, (((0,), (0,)), ((), ())), preferred_element_type=f32
        ) / (tok_rows * fsdp_count)
        first = first[0, :, at_cols].astype(f32)
        second = second[0, :, at_cols].astype(f32)
        m_new = beta_one * first + (1.0 - beta_one) * grad
        v_new = beta_two * second + (1.0 - beta_two) * grad * grad
        update = m_new / bias_one / (
            jnp.sqrt(v_new / bias_two) + adam_eps
        ) + decay_rate * outer[:, at_cols].astype(f32)
        pseudo = lax.optimization_barrier(update.astype(bf16))
        for u in range(hi - lo):
            line.part[len(parts)] = pseudo[:, u * narrow : (u + 1) * narrow]
            parts.append(line.part[len(parts)])

    for c in range(len(widths)):
        move(c)
    add_pseudo(gathered(0), 0, 1)
    found = gathered(1)
    early = sum(widths[:2])
    add_pseudo(found, 1, 2)
    add_pseudo(found[:, narrow:], 2, early)
    last = gathered(2)
    todo = [(lo, min(lo + 2, units)) for lo in range(early, units, 2)]
    if islands == 4:
        for s in range(2):
            line.send_outer(s)
        for s in range(units + 3):
            while todo and todo[0][0] - 3 <= s:
                lo, hi = todo.pop(0)
                add_pseudo(last[:, (lo - early) * narrow :], lo, hi, s - 1)
            line.step(s)
        sums = [line.totals[k] for k in range(units)]
    else:
        for lo, hi in todo:
            add_pseudo(last[:, (lo - early) * narrow :], lo, hi)
        sums = [lax.psum(part, "island") for part in parts]
    momentum_out, step_out = [], []
    for k, total in enumerate(sums):
        cols_at = slice(k * narrow, (k + 1) * narrow)
        delta = total.astype(f32) / islands
        new_momentum, outer_step = outer_update(delta, momentum[:, cols_at])
        momentum_out.append(new_momentum)
        step_out.append(outer_step)
    return (jnp.concatenate(momentum_out, axis=1), jnp.concatenate(step_out, axis=1))


def solution(mesh):
    in_specs = (
        P(("island", "fsdp"), "tp"),
        P(("island", "fsdp"), "tp"),
        P(("island", "fsdp"), "tp"),
        P(),
        P("tp", "fsdp"),
        P("island", "tp", "fsdp"),
        P("island", "tp", "fsdp"),
        P("tp", "fsdp"),
    )
    out_specs = (P("tp", "fsdp"), P("tp", "fsdp"))
    return jax.shard_map(body, mesh=mesh, in_specs=in_specs, out_specs=out_specs, check_vma=False)
```

```python
import jax
import jax.numpy as jnp
from jax import lax
from jax.sharding import PartitionSpec as P

norm_eps = 1e-06
adam_eps = 1e-08
beta_one = 0.9
beta_two = 0.999
bias_one = 1.0 - 0.9**10
bias_two = 1.0 - 0.999**10
decay_rate = 0.1
outer_mu = 0.9

f32 = jnp.float32
bf16 = jnp.bfloat16


def outer_update(delta, momentum):
    new_momentum = outer_mu * momentum + delta
    outer_step = (delta + outer_mu * new_momentum).astype(bf16)
    return (new_momentum, outer_step)


def swap(value, axis, bit):
    count = lax.axis_size(axis)
    return lax.ppermute(value, axis, [(i, i ^ bit) for i in range(count)])


def together(*values):
    return lax.optimization_barrier(values)


class IslandLine:
    def __init__(self, chunks):
        self.chunks = chunks
        me = lax.axis_index("island")
        self.outer = (me == 0) | (me == 3)
        self.part, self.paid, self.edge, self.mid, self.sums, self.totals = {}, {}, {}, {}, {}, {}

    def send_outer(self, s):
        if s >= self.chunks + 3:
            return
        pairs = [(0, 1), (3, 2)] if s < self.chunks else []
        if s >= 3:
            pairs = pairs + [(1, 0), (2, 3)]
            total = (self.sums[s - 3].astype(f32) + self.mid[s - 3].astype(f32)).astype(bf16)
            payload = jnp.where(self.outer, self.part[s], total) if s < self.chunks else total
        else:
            payload = self.part[s]
        self.paid[s] = payload
        self.edge[s] = lax.ppermute(payload, "island", pairs)

    def step(self, s):
        edge = self.edge[s]
        if s + 1 in self.paid:
            edge, self.paid[s + 1] = together(edge, self.paid[s + 1])
        if s < self.chunks:
            self.sums[s] = (edge.astype(f32) + self.part[s].astype(f32)).astype(bf16)
            self.mid[s] = lax.ppermute(self.sums[s], "island", [(1, 2), (2, 1)])
            if s >= 1:
                self.mid[s - 1], self.sums[s] = together(self.mid[s - 1], self.sums[s])
        self.send_outer(s + 2)
        if s >= 3:
            if s + 2 in self.paid:
                edge, self.paid[s], self.paid[s + 2] = together(edge, self.paid[s], self.paid[s + 2])
            else:
                edge, self.paid[s] = together(edge, self.paid[s])
            self.totals[s - 3] = jnp.where(self.outer, edge, self.paid[s])


def body(context, residual, cotangent, gain, weight, first_moment, second_moment, momentum):
    tok_rows = context.shape[0]
    width = gain.shape[0]
    fsdp_count = lax.axis_size("fsdp")
    group = fsdp_count // 2
    cols = weight.shape[1]
    t = lax.axis_index("tp")
    f = lax.axis_index("fsdp")
    high = f // group
    low = f % group
    near = t == high

    pieces = 2
    rows = tok_rows // pieces

    def project(block):
        return lax.optimization_barrier(
            jnp.dot(block, weight, preferred_element_type=f32).astype(bf16)
        )

    def at(h, q, x):
        return (h * group + q) * 2 + x

    ring_pairs, cross_pairs = [], []
    for q in range(group):
        ring_pairs += [(at(x, q, x), at(x, q, 1 - x)) for x in (0, 1)]
        ring_pairs += [(at(1 - x, q, x), at(x, q, x)) for x in (0, 1)]
        cross_pairs += [(at(1 - x, q, x), at(x, q, 1 - x)) for x in (0, 1)]
    inward_pairs = [(at(1 - x, q, x), at(1 - x, q, 1 - x)) for q in range(group) for x in (0, 1)]
    outward_pairs = [(at(x, q, x), at(x, q, 1 - x)) for q in range(group) for x in (0, 1)]

    near_blocks = [context] + [swap(context, "fsdp", r) for r in range(1, group)]
    slices = [
        [lax.dynamic_slice_in_dim(array, (low ^ r) * cols, cols, axis=1) for r in range(group)]
        for array in (residual, cotangent)
    ]
    moved = [[swap(parts[r], "fsdp", r) if r else parts[r] for r in range(group)] for parts in slices]
    held = together(swap(context, "fsdp", group), *moved[0], *moved[1])
    residual_parts, cotangent_parts = held[1 : 1 + group], held[1 + group :]
    far_blocks = [held[0]] + [swap(held[0], "fsdp", r) for r in range(1, group)]
    near_out = project(jnp.concatenate(near_blocks, axis=0))
    near_came = lax.ppermute(near_out, ("fsdp", "tp"), inward_pairs)
    far_outs = []
    for r in range(group):
        out = project(far_blocks[r])
        far_outs += [swap(out[p * rows : (p + 1) * rows], "fsdp", group) for p in range(pieces)]
    passed = [lax.ppermute(out, ("fsdp", "tp"), outward_pairs) for out in far_outs]

    gain_part = lax.dynamic_slice_in_dim(gain, t * (width // 2) + low * cols, cols).astype(f32)

    ready = [
        lax.optimization_barrier((res.astype(f32), gain_part[None, :] * cot.astype(f32)))
        for res, cot in zip(residual_parts, cotangent_parts)
    ]
    hidden, weighted, sums = [], [], []
    for k in range(group * pieces):
        r, p = k // pieces, k % pieces
        span, long_span = slice(p * rows, (p + 1) * rows), slice(k * rows, (k + 1) * rows)
        came = passed[k]
        if sums:
            came, sums[-1] = together(came, sums[-1])
        keep = jnp.where(near, near_out[long_span], far_outs[k])
        came = jnp.where(near, near_came[long_span], came)
        h = ready[r][0][span] + keep.astype(f32) + came.astype(f32)
        w = ready[r][1][span]
        hidden.append(h)
        weighted.append(w)
        sums.append(jnp.stack([jnp.sum(h * h, axis=-1), jnp.sum(h * w, axis=-1)]))
    own_sums = jnp.concatenate(sums, axis=1)
    totals = own_sums
    for r in range(1, group):
        came = swap(own_sums, "fsdp", r)
        order = [r ^ k for k in range(group)]
        came = jnp.concatenate(
            [came[:, k * tok_rows : (k + 1) * tok_rows] for k in order], axis=1
        )
        totals = totals + came
    totals = totals + swap(totals, "tp", 1)
    inv_rms = lax.rsqrt(totals[0] / width + norm_eps)
    pull = inv_rms**3 * totals[1] / width

    context_all = jnp.concatenate(near_blocks + far_blocks, axis=0)
    narrow = 128
    units = cols // narrow
    widths = [1, 3, units - 4]
    islands = lax.axis_size("island")
    line = IslandLine(units)
    parts, locals_, rings, crosses = [], [], [], []

    def move(c):
        cols_at = slice(sum(widths[:c]) * narrow, sum(widths[: c + 1]) * narrow)
        d_local = jnp.concatenate(
            [
                weighted[j][:, cols_at] * inv_rms[j * rows : (j + 1) * rows, None]
                - hidden[j][:, cols_at] * pull[j * rows : (j + 1) * rows, None]
                for j in range(group * pieces)
            ],
            axis=0,
        ).astype(bf16)
        if c == 1:
            d_local, rings[0] = together(d_local, rings[0])
        elif c == 2:
            d_local, crosses[0] = together(d_local, crosses[0])
        locals_.append(d_local)
        rings.append(lax.ppermute(d_local, ("fsdp", "tp"), ring_pairs))
        crosses.append(lax.ppermute(d_local, ("fsdp", "tp"), cross_pairs))

    def gathered(c):
        d_near = jnp.where(near, locals_[c], rings[c])
        d_far = jnp.where(near, rings[c], crosses[c])
        return jnp.concatenate([d_near, d_far], axis=0)

    def add_pseudo(d_all, lo, hi, after=None):
        at_cols = slice(lo * narrow, hi * narrow)
        piece = d_all[:, : (hi - lo) * narrow]
        if after in line.paid:
            piece, line.paid[after] = together(piece, line.paid[after])
        piece, first, second, outer = together(piece, first_moment, second_moment, weight)
        grad = lax.dot_general(
            context_all, piece, (((0,), (0,)), ((), ())), preferred_element_type=f32
        ) / (tok_rows * fsdp_count)
        first = first[0, :, at_cols].astype(f32)
        second = second[0, :, at_cols].astype(f32)
        m_new = beta_one * first + (1.0 - beta_one) * grad
        v_new = beta_two * second + (1.0 - beta_two) * grad * grad
        update = m_new / bias_one / (
            jnp.sqrt(v_new / bias_two) + adam_eps
        ) + decay_rate * outer[:, at_cols].astype(f32)
        pseudo = lax.optimization_barrier(update.astype(bf16))
        for u in range(hi - lo):
            line.part[len(parts)] = pseudo[:, u * narrow : (u + 1) * narrow]
            parts.append(line.part[len(parts)])

    for c in range(len(widths)):
        move(c)
    add_pseudo(gathered(0), 0, 1)
    found = gathered(1)
    early = sum(widths[:2])
    add_pseudo(found, 1, 2)
    add_pseudo(found[:, narrow:], 2, early)
    last = gathered(2)
    todo = [(lo, min(lo + 2, units)) for lo in range(early, units, 2)]
    if islands == 4:
        for s in range(2):
            line.send_outer(s)
        for s in range(units + 3):
            while todo and todo[0][0] - 3 <= s:
                lo, hi = todo.pop(0)
                add_pseudo(last[:, (lo - early) * narrow :], lo, hi, s + 1)
            line.step(s)
        sums = [line.totals[k] for k in range(units)]
    else:
        for lo, hi in todo:
            add_pseudo(last[:, (lo - early) * narrow :], lo, hi)
        sums = [lax.psum(part, "island") for part in parts]
    momentum_out, step_out = [], []
    for k, total in enumerate(sums):
        cols_at = slice(k * narrow, (k + 1) * narrow)
        delta = total.astype(f32) / islands
        new_momentum, outer_step = outer_update(delta, momentum[:, cols_at])
        momentum_out.append(new_momentum)
        step_out.append(outer_step)
    return (jnp.concatenate(momentum_out, axis=1), jnp.concatenate(step_out, axis=1))


def solution(mesh):
    in_specs = (
        P(("island", "fsdp"), "tp"),
        P(("island", "fsdp"), "tp"),
        P(("island", "fsdp"), "tp"),
        P(),
        P("tp", "fsdp"),
        P("island", "tp", "fsdp"),
        P("island", "tp", "fsdp"),
        P("tp", "fsdp"),
    )
    out_specs = (P("tp", "fsdp"), P("tp", "fsdp"))
    return jax.shard_map(body, mesh=mesh, in_specs=in_specs, out_specs=out_specs, check_vma=False)
```

```python
import functools

import jax
import jax.numpy as jnp
from jax import lax
from jax.experimental import pallas as pl
from jax.experimental.pallas import tpu as pltpu
from jax.sharding import PartitionSpec as P

norm_eps = 1e-06
adam_eps = 1e-08
beta_one = 0.9
beta_two = 0.999
bias_one = 1.0 - 0.9**10
bias_two = 1.0 - 0.999**10
decay_rate = 0.1
outer_mu = 0.9

f32 = jnp.float32
bf16 = jnp.bfloat16


def outer_update(delta, momentum):
    new_momentum = outer_mu * momentum + delta
    outer_step = (delta + outer_mu * new_momentum).astype(bf16)
    return (new_momentum, outer_step)


def swap(value, axis, bit):
    count = lax.axis_size(axis)
    return lax.ppermute(value, axis, [(i, i ^ bit) for i in range(count)])


def finish_kernel(count, start, narrow, islands, *refs):
    totals, momentum = refs[:count], refs[count]
    new_out, step_out, held, fresh, step, sems = refs[-6:]
    columns = pl.ds(start, count * narrow)
    load = pltpu.make_async_copy(momentum.at[:, columns], held, sems.at[0])
    load.start()
    load.wait()
    for k in range(count):
        at = slice(k * narrow, (k + 1) * narrow)
        delta = totals[k][...].astype(f32) / islands
        fresh[:, at], step[:, at] = outer_update(delta, held[:, at])
    stores = [
        pltpu.make_async_copy(fresh, new_out.at[:, columns], sems.at[1]),
        pltpu.make_async_copy(step, step_out.at[:, columns], sems.at[2]),
    ]
    for store in stores:
        store.start()
    for store in stores:
        store.wait()


def finish(totals, start, islands, momentum, outputs):
    rows, narrow = totals[0].shape
    count = len(totals)
    wide = count * narrow
    in_hbm = pl.BlockSpec(memory_space=pltpu.HBM)
    in_vmem = pl.BlockSpec(memory_space=pltpu.VMEM)
    return pl.pallas_call(
        functools.partial(finish_kernel, count, start, narrow, islands),
        out_shape=(
            jax.ShapeDtypeStruct(momentum.shape, f32),
            jax.ShapeDtypeStruct(momentum.shape, bf16),
        ),
        in_specs=[in_vmem] * count + [in_hbm] * (1 + len(outputs)),
        out_specs=(in_hbm, in_hbm),
        scratch_shapes=[
            pltpu.VMEM((rows, wide), f32),
            pltpu.VMEM((rows, wide), f32),
            pltpu.VMEM((rows, wide), bf16),
            pltpu.SemaphoreType.DMA((3,)),
        ],
        input_output_aliases={count + 1 + k: k for k in range(len(outputs))},
        compiler_params=pltpu.CompilerParams(vmem_limit_bytes=16 * 1024 * 1024),
        cost_estimate=pl.CostEstimate(
            flops=5 * rows * wide, bytes_accessed=12 * rows * wide, transcendentals=0
        ),
    )(*totals, momentum, *outputs)


def together(*values):
    return lax.optimization_barrier(values)


class IslandLine:
    def __init__(self, chunks):
        self.chunks = chunks
        me = lax.axis_index("island")
        self.outer = (me == 0) | (me == 3)
        self.part, self.paid, self.edge, self.mid, self.sums, self.totals = {}, {}, {}, {}, {}, {}

    def send_outer(self, s):
        if s >= self.chunks + 3:
            return
        pairs = [(0, 1), (3, 2)] if s < self.chunks else []
        if s >= 3:
            pairs = pairs + [(1, 0), (2, 3)]
            total = (self.sums[s - 3].astype(f32) + self.mid[s - 3].astype(f32)).astype(bf16)
            payload = jnp.where(self.outer, self.part[s], total) if s < self.chunks else total
        else:
            payload = self.part[s]
        self.paid[s] = payload
        self.edge[s] = lax.ppermute(payload, "island", pairs)

    def step(self, s):
        edge = self.edge[s]
        if s + 1 in self.paid:
            edge, self.paid[s + 1] = together(edge, self.paid[s + 1])
        if s < self.chunks:
            self.sums[s] = (edge.astype(f32) + self.part[s].astype(f32)).astype(bf16)
            self.mid[s] = lax.ppermute(self.sums[s], "island", [(1, 2), (2, 1)])
            if s >= 1:
                self.mid[s - 1], self.sums[s] = together(self.mid[s - 1], self.sums[s])
        self.send_outer(s + 2)
        if s >= 3:
            if s + 2 in self.paid:
                edge, self.paid[s], self.paid[s + 2] = together(edge, self.paid[s], self.paid[s + 2])
            else:
                edge, self.paid[s] = together(edge, self.paid[s])
            self.totals[s - 3] = jnp.where(self.outer, edge, self.paid[s])


def body(context, residual, cotangent, gain, weight, first_moment, second_moment, momentum):
    tok_rows = context.shape[0]
    width = gain.shape[0]
    fsdp_count = lax.axis_size("fsdp")
    group = fsdp_count // 2
    cols = weight.shape[1]
    t = lax.axis_index("tp")
    f = lax.axis_index("fsdp")
    high = f // group
    low = f % group
    near = t == high

    pieces = 2
    rows = tok_rows // pieces

    def project(block):
        return lax.optimization_barrier(
            jnp.dot(block, weight, preferred_element_type=f32).astype(bf16)
        )

    def at(h, q, x):
        return (h * group + q) * 2 + x

    ring_pairs, cross_pairs = [], []
    for q in range(group):
        ring_pairs += [(at(x, q, x), at(x, q, 1 - x)) for x in (0, 1)]
        ring_pairs += [(at(1 - x, q, x), at(x, q, x)) for x in (0, 1)]
        cross_pairs += [(at(1 - x, q, x), at(x, q, 1 - x)) for x in (0, 1)]
    inward_pairs = [(at(1 - x, q, x), at(1 - x, q, 1 - x)) for q in range(group) for x in (0, 1)]
    outward_pairs = [(at(x, q, x), at(x, q, 1 - x)) for q in range(group) for x in (0, 1)]

    near_blocks = [context] + [swap(context, "fsdp", r) for r in range(1, group)]
    slices = [
        [lax.dynamic_slice_in_dim(array, (low ^ r) * cols, cols, axis=1) for r in range(group)]
        for array in (residual, cotangent)
    ]
    moved = [[swap(parts[r], "fsdp", r) if r else parts[r] for r in range(group)] for parts in slices]
    held = together(swap(context, "fsdp", group), *moved[0], *moved[1])
    residual_parts, cotangent_parts = held[1 : 1 + group], held[1 + group :]
    far_blocks = [held[0]] + [swap(held[0], "fsdp", r) for r in range(1, group)]
    near_out = project(jnp.concatenate(near_blocks, axis=0))
    near_came = lax.ppermute(near_out, ("fsdp", "tp"), inward_pairs)
    far_outs = []
    for r in range(group):
        out = project(far_blocks[r])
        far_outs += [swap(out[p * rows : (p + 1) * rows], "fsdp", group) for p in range(pieces)]
    passed = [lax.ppermute(out, ("fsdp", "tp"), outward_pairs) for out in far_outs]

    gain_part = lax.dynamic_slice_in_dim(gain, t * (width // 2) + low * cols, cols).astype(f32)

    hidden, weighted, sums = [], [], []
    for k in range(group * pieces):
        r, p = k // pieces, k % pieces
        span, long_span = slice(p * rows, (p + 1) * rows), slice(k * rows, (k + 1) * rows)
        res, cot, came = residual_parts[r], cotangent_parts[r], passed[k]
        if sums:
            came, sums[-1] = together(came, sums[-1])
        keep = jnp.where(near, near_out[long_span], far_outs[k])
        came = jnp.where(near, near_came[long_span], came)
        h = res[span].astype(f32) + keep.astype(f32) + came.astype(f32)
        w = gain_part[None, :] * cot[span].astype(f32)
        hidden.append(h)
        weighted.append(w)
        sums.append(jnp.stack([jnp.sum(h * h, axis=-1), jnp.sum(h * w, axis=-1)]))
    own_sums = jnp.concatenate(sums, axis=1)
    totals = own_sums
    for r in range(1, group):
        came = swap(own_sums, "fsdp", r)
        order = [r ^ k for k in range(group)]
        came = jnp.concatenate(
            [came[:, k * tok_rows : (k + 1) * tok_rows] for k in order], axis=1
        )
        totals = totals + came
    totals = totals + swap(totals, "tp", 1)
    inv_rms = lax.rsqrt(totals[0] / width + norm_eps)
    pull = inv_rms**3 * totals[1] / width

    context_all = jnp.concatenate(near_blocks + far_blocks, axis=0)
    narrow = 128
    units = cols // narrow
    widths = [1, 3, units - 4]
    islands = lax.axis_size("island")
    line = IslandLine(units)
    parts, locals_, rings, crosses = [], [], [], []

    def move(c):
        cols_at = slice(sum(widths[:c]) * narrow, sum(widths[: c + 1]) * narrow)
        d_local = jnp.concatenate(
            [
                weighted[j][:, cols_at] * inv_rms[j * rows : (j + 1) * rows, None]
                - hidden[j][:, cols_at] * pull[j * rows : (j + 1) * rows, None]
                for j in range(group * pieces)
            ],
            axis=0,
        ).astype(bf16)
        if c == 1:
            d_local, rings[0] = together(d_local, rings[0])
        elif c == 2:
            d_local, crosses[0] = together(d_local, crosses[0])
        locals_.append(d_local)
        rings.append(lax.ppermute(d_local, ("fsdp", "tp"), ring_pairs))
        crosses.append(lax.ppermute(d_local, ("fsdp", "tp"), cross_pairs))

    def gathered(c):
        d_near = jnp.where(near, locals_[c], rings[c])
        d_far = jnp.where(near, rings[c], crosses[c])
        return jnp.concatenate([d_near, d_far], axis=0)

    def add_pseudo(d_all, lo, hi, after=None):
        at_cols = slice(lo * narrow, hi * narrow)
        piece = d_all[:, : (hi - lo) * narrow]
        if after in line.sums:
            piece, line.sums[after] = together(piece, line.sums[after])
        piece, first, second, outer = together(piece, first_moment, second_moment, weight)
        grad = lax.dot_general(
            context_all, piece, (((0,), (0,)), ((), ())), preferred_element_type=f32
        ) / (tok_rows * fsdp_count)
        first = first[0, :, at_cols].astype(f32)
        second = second[0, :, at_cols].astype(f32)
        m_new = beta_one * first + (1.0 - beta_one) * grad
        v_new = beta_two * second + (1.0 - beta_two) * grad * grad
        update = m_new / bias_one / (
            jnp.sqrt(v_new / bias_two) + adam_eps
        ) + decay_rate * outer[:, at_cols].astype(f32)
        pseudo = lax.optimization_barrier(update.astype(bf16))
        for u in range(hi - lo):
            line.part[len(parts)] = pseudo[:, u * narrow : (u + 1) * narrow]
            parts.append(line.part[len(parts)])

    for c in range(len(widths)):
        move(c)
    add_pseudo(gathered(0), 0, 1)
    found = gathered(1)
    early = sum(widths[:2])
    add_pseudo(found, 1, 2)
    add_pseudo(found[:, narrow:], 2, early)
    last = gathered(2)
    todo = [(lo, min(lo + 2, units)) for lo in range(early, units, 2)]
    if islands == 4:
        for s in range(2):
            line.send_outer(s)
        for s in range(units + 3):
            while todo and todo[0][0] - 3 <= s:
                lo, hi = todo.pop(0)
                add_pseudo(last[:, (lo - early) * narrow :], lo, hi, s - 1)
            line.step(s)
        sums = [line.totals[k] for k in range(units)]
    else:
        for lo, hi in todo:
            add_pseudo(last[:, (lo - early) * narrow :], lo, hi)
        sums = [lax.psum(part, "island") for part in parts]
    ends = list(range(3, units - 3, 3)) + [units - 3, units - 1, units]
    outputs, start = (), 0
    for end in ends:
        outputs = finish(sums[start:end], start * narrow, islands, momentum, outputs)
        start = end
    return outputs


def solution(mesh):
    in_specs = (
        P(("island", "fsdp"), "tp"),
        P(("island", "fsdp"), "tp"),
        P(("island", "fsdp"), "tp"),
        P(),
        P("tp", "fsdp"),
        P("island", "tp", "fsdp"),
        P("island", "tp", "fsdp"),
        P("tp", "fsdp"),
    )
    out_specs = (P("tp", "fsdp"), P("tp", "fsdp"))
    return jax.shard_map(body, mesh=mesh, in_specs=in_specs, out_specs=out_specs, check_vma=False)
```

```python
import functools

import jax
import jax.numpy as jnp
from jax import lax
from jax.experimental import pallas as pl
from jax.experimental.pallas import tpu as pltpu
from jax.sharding import PartitionSpec as P

norm_eps = 1e-06
adam_eps = 1e-08
beta_one = 0.9
beta_two = 0.999
bias_one = 1.0 - 0.9**10
bias_two = 1.0 - 0.999**10
decay_rate = 0.1
outer_mu = 0.9

f32 = jnp.float32
bf16 = jnp.bfloat16


def outer_update(delta, momentum):
    new_momentum = outer_mu * momentum + delta
    outer_step = (delta + outer_mu * new_momentum).astype(bf16)
    return (new_momentum, outer_step)


def swap(value, axis, bit):
    count = lax.axis_size(axis)
    return lax.ppermute(value, axis, [(i, i ^ bit) for i in range(count)])


def finish_kernel(count, start, narrow, islands, *refs):
    totals, momentum = refs[:count], refs[count]
    new_out, step_out, held, fresh, step, sems = refs[-6:]
    columns = pl.ds(start, count * narrow)
    load = pltpu.make_async_copy(momentum.at[:, columns], held, sems.at[0])
    load.start()
    load.wait()
    for k in range(count):
        at = slice(k * narrow, (k + 1) * narrow)
        delta = totals[k][...].astype(f32) / islands
        fresh[:, at], step[:, at] = outer_update(delta, held[:, at])
    stores = [
        pltpu.make_async_copy(fresh, new_out.at[:, columns], sems.at[1]),
        pltpu.make_async_copy(step, step_out.at[:, columns], sems.at[2]),
    ]
    for store in stores:
        store.start()
    for store in stores:
        store.wait()


def finish(totals, start, islands, momentum, outputs):
    rows, narrow = totals[0].shape
    count = len(totals)
    wide = count * narrow
    in_hbm = pl.BlockSpec(memory_space=pltpu.HBM)
    in_vmem = pl.BlockSpec(memory_space=pltpu.VMEM)
    return pl.pallas_call(
        functools.partial(finish_kernel, count, start, narrow, islands),
        out_shape=(
            jax.ShapeDtypeStruct(momentum.shape, f32),
            jax.ShapeDtypeStruct(momentum.shape, bf16),
        ),
        in_specs=[in_vmem] * count + [in_hbm] * (1 + len(outputs)),
        out_specs=(in_hbm, in_hbm),
        scratch_shapes=[
            pltpu.VMEM((rows, wide), f32),
            pltpu.VMEM((rows, wide), f32),
            pltpu.VMEM((rows, wide), bf16),
            pltpu.SemaphoreType.DMA((3,)),
        ],
        input_output_aliases={count + 1 + k: k for k in range(len(outputs))},
        compiler_params=pltpu.CompilerParams(vmem_limit_bytes=16 * 1024 * 1024),
        cost_estimate=pl.CostEstimate(
            flops=5 * rows * wide, bytes_accessed=12 * rows * wide, transcendentals=0
        ),
    )(*totals, momentum, *outputs)


def together(*values):
    return lax.optimization_barrier(values)


class IslandLine:
    def __init__(self, chunks):
        self.chunks = chunks
        me = lax.axis_index("island")
        self.outer = (me == 0) | (me == 3)
        self.part, self.paid, self.edge, self.mid, self.sums, self.totals = {}, {}, {}, {}, {}, {}

    def send_outer(self, s):
        if s >= self.chunks + 3:
            return
        pairs = [(0, 1), (3, 2)] if s < self.chunks else []
        if s >= 3:
            pairs = pairs + [(1, 0), (2, 3)]
            total = (self.sums[s - 3].astype(f32) + self.mid[s - 3].astype(f32)).astype(bf16)
            payload = jnp.where(self.outer, self.part[s], total) if s < self.chunks else total
        else:
            payload = self.part[s]
            if s == 2:
                payload, self.sums[0] = together(payload, self.sums[0])
        self.paid[s] = payload
        self.edge[s] = lax.ppermute(payload, "island", pairs)

    def step(self, s):
        edge = self.edge[s]
        if s + 1 in self.paid:
            edge, self.paid[s + 1] = together(edge, self.paid[s + 1])
        if s < self.chunks:
            self.sums[s] = (edge.astype(f32) + self.part[s].astype(f32)).astype(bf16)
            self.mid[s] = lax.ppermute(self.sums[s], "island", [(1, 2), (2, 1)])
            if s >= 1:
                self.mid[s - 1], self.sums[s] = together(self.mid[s - 1], self.sums[s])
        self.send_outer(s + 2)
        if s >= 3:
            if s + 2 in self.paid:
                edge, self.paid[s], self.paid[s + 2] = together(edge, self.paid[s], self.paid[s + 2])
            else:
                edge, self.paid[s] = together(edge, self.paid[s])
            self.totals[s - 3] = jnp.where(self.outer, edge, self.paid[s])


def body(context, residual, cotangent, gain, weight, first_moment, second_moment, momentum):
    tok_rows = context.shape[0]
    width = gain.shape[0]
    fsdp_count = lax.axis_size("fsdp")
    group = fsdp_count // 2
    cols = weight.shape[1]
    t = lax.axis_index("tp")
    f = lax.axis_index("fsdp")
    high = f // group
    low = f % group
    near = t == high

    pieces = 2
    rows = tok_rows // pieces

    def project(block):
        return lax.optimization_barrier(
            jnp.dot(block, weight, preferred_element_type=f32).astype(bf16)
        )

    def at(h, q, x):
        return (h * group + q) * 2 + x

    ring_pairs, cross_pairs = [], []
    for q in range(group):
        ring_pairs += [(at(x, q, x), at(x, q, 1 - x)) for x in (0, 1)]
        ring_pairs += [(at(1 - x, q, x), at(x, q, x)) for x in (0, 1)]
        cross_pairs += [(at(1 - x, q, x), at(x, q, 1 - x)) for x in (0, 1)]
    inward_pairs = [(at(1 - x, q, x), at(1 - x, q, 1 - x)) for q in range(group) for x in (0, 1)]
    outward_pairs = [(at(x, q, x), at(x, q, 1 - x)) for q in range(group) for x in (0, 1)]

    near_blocks = [context] + [swap(context, "fsdp", r) for r in range(1, group)]
    slices = [
        [lax.dynamic_slice_in_dim(array, (low ^ r) * cols, cols, axis=1) for r in range(group)]
        for array in (residual, cotangent)
    ]
    moved = [[swap(parts[r], "fsdp", r) if r else parts[r] for r in range(group)] for parts in slices]
    held = together(swap(context, "fsdp", group), *moved[0], *moved[1])
    residual_parts, cotangent_parts = held[1 : 1 + group], held[1 + group :]
    far_blocks = [held[0]] + [swap(held[0], "fsdp", r) for r in range(1, group)]
    near_out = project(jnp.concatenate(near_blocks, axis=0))
    near_came = lax.ppermute(near_out, ("fsdp", "tp"), inward_pairs)
    far_outs = []
    for r in range(group):
        out = project(far_blocks[r])
        far_outs += [swap(out[p * rows : (p + 1) * rows], "fsdp", group) for p in range(pieces)]
    passed = [lax.ppermute(out, ("fsdp", "tp"), outward_pairs) for out in far_outs]

    gain_part = lax.dynamic_slice_in_dim(gain, t * (width // 2) + low * cols, cols).astype(f32)

    hidden, weighted, sums = [], [], []
    for k in range(group * pieces):
        r, p = k // pieces, k % pieces
        span, long_span = slice(p * rows, (p + 1) * rows), slice(k * rows, (k + 1) * rows)
        res, cot, came = residual_parts[r], cotangent_parts[r], passed[k]
        if sums:
            came, sums[-1] = together(came, sums[-1])
        keep = jnp.where(near, near_out[long_span], far_outs[k])
        came = jnp.where(near, near_came[long_span], came)
        h = res[span].astype(f32) + keep.astype(f32) + came.astype(f32)
        w = gain_part[None, :] * cot[span].astype(f32)
        hidden.append(h)
        weighted.append(w)
        sums.append(jnp.stack([jnp.sum(h * h, axis=-1), jnp.sum(h * w, axis=-1)]))
    own_sums = jnp.concatenate(sums, axis=1)
    totals = own_sums
    for r in range(1, group):
        came = swap(own_sums, "fsdp", r)
        order = [r ^ k for k in range(group)]
        came = jnp.concatenate(
            [came[:, k * tok_rows : (k + 1) * tok_rows] for k in order], axis=1
        )
        totals = totals + came
    totals = totals + swap(totals, "tp", 1)
    inv_rms = lax.rsqrt(totals[0] / width + norm_eps)
    pull = inv_rms**3 * totals[1] / width

    context_all = jnp.concatenate(near_blocks + far_blocks, axis=0)
    narrow = 128
    units = cols // narrow
    widths = [1, 3, units - 4]
    islands = lax.axis_size("island")
    line = IslandLine(units)
    locals_, rings, crosses = [], [], []

    def move(c):
        cols_at = slice(sum(widths[:c]) * narrow, sum(widths[: c + 1]) * narrow)
        d_local = jnp.concatenate(
            [
                weighted[j][:, cols_at] * inv_rms[j * rows : (j + 1) * rows, None]
                - hidden[j][:, cols_at] * pull[j * rows : (j + 1) * rows, None]
                for j in range(group * pieces)
            ],
            axis=0,
        ).astype(bf16)
        if c == 1:
            d_local, rings[0] = together(d_local, rings[0])
        elif c == 2:
            d_local, crosses[0] = together(d_local, crosses[0])
        locals_.append(d_local)
        rings.append(lax.ppermute(d_local, ("fsdp", "tp"), ring_pairs))
        d_cross = d_local
        if c == 1:
            d_cross, crosses[0] = together(d_local, crosses[0])
        crosses.append(lax.ppermute(d_cross, ("fsdp", "tp"), cross_pairs))

    def gathered(c):
        d_near = jnp.where(near, locals_[c], rings[c])
        d_far = jnp.where(near, rings[c], crosses[c])
        return jnp.concatenate([d_near, d_far], axis=0)

    def add_pseudo(d_all, lo, hi, after=None, behind=None):
        at_cols = slice(lo * narrow, hi * narrow)
        piece = d_all[:, : (hi - lo) * narrow]
        if after in line.sums:
            piece, line.sums[after] = together(piece, line.sums[after])
        if behind is not None:
            piece, line.part[behind] = together(piece, line.part[behind])
        piece, first, second, outer = together(piece, first_moment, second_moment, weight)
        grad = lax.dot_general(
            context_all, piece, (((0,), (0,)), ((), ())), preferred_element_type=f32
        ) / (tok_rows * fsdp_count)
        first = first[0, :, at_cols].astype(f32)
        second = second[0, :, at_cols].astype(f32)
        m_new = beta_one * first + (1.0 - beta_one) * grad
        v_new = beta_two * second + (1.0 - beta_two) * grad * grad
        update = m_new / bias_one / (
            jnp.sqrt(v_new / bias_two) + adam_eps
        ) + decay_rate * outer[:, at_cols].astype(f32)
        pseudo = lax.optimization_barrier(update.astype(bf16))
        for u in range(hi - lo):
            line.part[lo + u] = pseudo[:, u * narrow : (u + 1) * narrow]

    for c in range(len(widths)):
        move(c)
    add_pseudo(gathered(0), 0, 1)
    found = gathered(1)
    early = sum(widths[:2])
    add_pseudo(found, 1, 2)
    add_pseudo(found[:, narrow:], 2, early, behind=1)
    last = gathered(2)
    todo = [(lo, min(lo + 2, units)) for lo in range(early, units, 2)]
    if islands == 4:
        for s in range(2):
            line.send_outer(s)
        for s in range(units + 3):
            while todo and todo[0][0] - 3 <= s:
                lo, hi = todo.pop(0)
                add_pseudo(last[:, (lo - early) * narrow :], lo, hi, s - 1)
            line.step(s)
        sums = [line.totals[k] for k in range(units)]
    else:
        for lo, hi in todo:
            add_pseudo(last[:, (lo - early) * narrow :], lo, hi)
        sums = [lax.psum(line.part[k], "island") for k in range(units)]
    ends = list(range(3, units - 3, 3)) + [units - 3, units - 1, units]
    outputs, start = (), 0
    for end in ends:
        outputs = finish(sums[start:end], start * narrow, islands, momentum, outputs)
        start = end
    return outputs


def solution(mesh):
    in_specs = (
        P(("island", "fsdp"), "tp"),
        P(("island", "fsdp"), "tp"),
        P(("island", "fsdp"), "tp"),
        P(),
        P("tp", "fsdp"),
        P("island", "tp", "fsdp"),
        P("island", "tp", "fsdp"),
        P("tp", "fsdp"),
    )
    out_specs = (P("tp", "fsdp"), P("tp", "fsdp"))
    return jax.shard_map(body, mesh=mesh, in_specs=in_specs, out_specs=out_specs, check_vma=False)
```

```python
import functools

import jax
import jax.numpy as jnp
from jax import lax
from jax.experimental import pallas as pl
from jax.experimental.pallas import tpu as pltpu
from jax.sharding import PartitionSpec as P

norm_eps = 1e-06
adam_eps = 1e-08
beta_one = 0.9
beta_two = 0.999
bias_one = 1.0 - 0.9**10
bias_two = 1.0 - 0.999**10
decay_rate = 0.1
outer_mu = 0.9

f32 = jnp.float32
bf16 = jnp.bfloat16


def outer_update(delta, momentum):
    new_momentum = outer_mu * momentum + delta
    outer_step = (delta + outer_mu * new_momentum).astype(bf16)
    return (new_momentum, outer_step)


def swap(value, axis, bit):
    count = lax.axis_size(axis)
    return lax.ppermute(value, axis, [(i, i ^ bit) for i in range(count)])


def finish_kernel(count, start, narrow, islands, *refs):
    totals, momentum = refs[:count], refs[count]
    new_out, step_out, held, fresh, step, sems = refs[-6:]
    columns = pl.ds(start, count * narrow)
    load = pltpu.make_async_copy(momentum.at[:, columns], held, sems.at[0])
    load.start()
    load.wait()
    for k in range(count):
        at = slice(k * narrow, (k + 1) * narrow)
        delta = totals[k][...].astype(f32) / islands
        fresh[:, at], step[:, at] = outer_update(delta, held[:, at])
    stores = [
        pltpu.make_async_copy(fresh, new_out.at[:, columns], sems.at[1]),
        pltpu.make_async_copy(step, step_out.at[:, columns], sems.at[2]),
    ]
    for store in stores:
        store.start()
    for store in stores:
        store.wait()


def finish(totals, start, islands, momentum, outputs):
    rows, narrow = totals[0].shape
    count = len(totals)
    wide = count * narrow
    in_hbm = pl.BlockSpec(memory_space=pltpu.HBM)
    in_vmem = pl.BlockSpec(memory_space=pltpu.VMEM)
    return pl.pallas_call(
        functools.partial(finish_kernel, count, start, narrow, islands),
        out_shape=(
            jax.ShapeDtypeStruct(momentum.shape, f32),
            jax.ShapeDtypeStruct(momentum.shape, bf16),
        ),
        in_specs=[in_vmem] * count + [in_hbm] * (1 + len(outputs)),
        out_specs=(in_hbm, in_hbm),
        scratch_shapes=[
            pltpu.VMEM((rows, wide), f32),
            pltpu.VMEM((rows, wide), f32),
            pltpu.VMEM((rows, wide), bf16),
            pltpu.SemaphoreType.DMA((3,)),
        ],
        input_output_aliases={count + 1 + k: k for k in range(len(outputs))},
        compiler_params=pltpu.CompilerParams(vmem_limit_bytes=16 * 1024 * 1024),
        cost_estimate=pl.CostEstimate(
            flops=5 * rows * wide, bytes_accessed=12 * rows * wide, transcendentals=0
        ),
    )(*totals, momentum, *outputs)


def together(*values):
    return lax.optimization_barrier(values)


class IslandLine:
    def __init__(self, chunks):
        self.chunks = chunks
        me = lax.axis_index("island")
        self.outer = (me == 0) | (me == 3)
        self.part, self.paid, self.edge, self.mid, self.sums, self.totals = {}, {}, {}, {}, {}, {}

    def send_outer(self, s):
        if s >= self.chunks + 3:
            return
        pairs = [(0, 1), (3, 2)] if s < self.chunks else []
        if s >= 3:
            pairs = pairs + [(1, 0), (2, 3)]
            total = (self.sums[s - 3].astype(f32) + self.mid[s - 3].astype(f32)).astype(bf16)
            payload = jnp.where(self.outer, self.part[s], total) if s < self.chunks else total
        else:
            payload = self.part[s]
            if s == 2:
                payload, self.sums[0] = together(payload, self.sums[0])
        self.paid[s] = payload
        self.edge[s] = lax.ppermute(payload, "island", pairs)

    def step(self, s):
        edge = self.edge[s]
        if s + 1 in self.paid:
            edge, self.paid[s + 1] = together(edge, self.paid[s + 1])
        if s < self.chunks:
            self.sums[s] = (edge.astype(f32) + self.part[s].astype(f32)).astype(bf16)
            self.mid[s] = lax.ppermute(self.sums[s], "island", [(1, 2), (2, 1)])
            if s >= 1:
                self.mid[s - 1], self.sums[s] = together(self.mid[s - 1], self.sums[s])
        self.send_outer(s + 2)
        if s >= 3:
            if s + 2 in self.paid:
                edge, self.paid[s], self.paid[s + 2] = together(edge, self.paid[s], self.paid[s + 2])
            else:
                edge, self.paid[s] = together(edge, self.paid[s])
            self.totals[s - 3] = jnp.where(self.outer, edge, self.paid[s])


def body(context, residual, cotangent, gain, weight, first_moment, second_moment, momentum):
    tok_rows = context.shape[0]
    width = gain.shape[0]
    fsdp_count = lax.axis_size("fsdp")
    group = fsdp_count // 2
    cols = weight.shape[1]
    t = lax.axis_index("tp")
    f = lax.axis_index("fsdp")
    high = f // group
    low = f % group
    near = t == high

    pieces = 2
    rows = tok_rows // pieces

    def project(block):
        return lax.optimization_barrier(
            jnp.dot(block, weight, preferred_element_type=f32).astype(bf16)
        )

    def at(h, q, x):
        return (h * group + q) * 2 + x

    ring_pairs, cross_pairs = [], []
    for q in range(group):
        ring_pairs += [(at(x, q, x), at(x, q, 1 - x)) for x in (0, 1)]
        ring_pairs += [(at(1 - x, q, x), at(x, q, x)) for x in (0, 1)]
        cross_pairs += [(at(1 - x, q, x), at(x, q, 1 - x)) for x in (0, 1)]
    inward_pairs = [(at(1 - x, q, x), at(1 - x, q, 1 - x)) for q in range(group) for x in (0, 1)]
    outward_pairs = [(at(x, q, x), at(x, q, 1 - x)) for q in range(group) for x in (0, 1)]

    near_blocks = [context] + [swap(context, "fsdp", r) for r in range(1, group)]
    slices = [
        [lax.dynamic_slice_in_dim(array, (low ^ r) * cols, cols, axis=1) for r in range(group)]
        for array in (residual, cotangent)
    ]
    moved = [[swap(parts[r], "fsdp", r) if r else parts[r] for r in range(group)] for parts in slices]
    held = together(swap(context, "fsdp", group), *moved[0], *moved[1])
    residual_parts, cotangent_parts = held[1 : 1 + group], held[1 + group :]
    far_blocks = [held[0]] + [swap(held[0], "fsdp", r) for r in range(1, group)]
    near_out = project(jnp.concatenate(near_blocks, axis=0))
    near_came = lax.ppermute(near_out, ("fsdp", "tp"), inward_pairs)
    far_outs = []
    for r in range(group):
        out = project(far_blocks[r])
        far_outs += [swap(out[p * rows : (p + 1) * rows], "fsdp", group) for p in range(pieces)]
    passed = [lax.ppermute(out, ("fsdp", "tp"), outward_pairs) for out in far_outs]

    gain_part = lax.dynamic_slice_in_dim(gain, t * (width // 2) + low * cols, cols).astype(f32)

    hidden, weighted, sums = [], [], []
    for k in range(group * pieces):
        r, p = k // pieces, k % pieces
        span, long_span = slice(p * rows, (p + 1) * rows), slice(k * rows, (k + 1) * rows)
        res, cot, came = residual_parts[r], cotangent_parts[r], passed[k]
        if sums:
            came, sums[-1] = together(came, sums[-1])
        keep = jnp.where(near, near_out[long_span], far_outs[k])
        came = jnp.where(near, near_came[long_span], came)
        h = res[span].astype(f32) + keep.astype(f32) + came.astype(f32)
        w = gain_part[None, :] * cot[span].astype(f32)
        hidden.append(h)
        weighted.append(w)
        sums.append(jnp.stack([jnp.sum(h * h, axis=-1), jnp.sum(h * w, axis=-1)]))
    own_sums = jnp.concatenate(sums, axis=1)
    totals = own_sums
    for r in range(1, group):
        came = swap(own_sums, "fsdp", r)
        order = [r ^ k for k in range(group)]
        came = jnp.concatenate(
            [came[:, k * tok_rows : (k + 1) * tok_rows] for k in order], axis=1
        )
        totals = totals + came
    totals = totals + swap(totals, "tp", 1)
    inv_rms = lax.rsqrt(totals[0] / width + norm_eps)
    pull = inv_rms**3 * totals[1] / width

    context_all = jnp.concatenate(near_blocks + far_blocks, axis=0)
    narrow = 128
    units = cols // narrow
    widths = [1, 3, units - 4]
    islands = lax.axis_size("island")
    line = IslandLine(units)
    locals_, rings, crosses = [], [], []

    def move(c):
        cols_at = slice(sum(widths[:c]) * narrow, sum(widths[: c + 1]) * narrow)
        d_local = jnp.concatenate(
            [
                weighted[j][:, cols_at] * inv_rms[j * rows : (j + 1) * rows, None]
                - hidden[j][:, cols_at] * pull[j * rows : (j + 1) * rows, None]
                for j in range(group * pieces)
            ],
            axis=0,
        ).astype(bf16)
        if c == 1:
            d_local, rings[0] = together(d_local, rings[0])
        elif c == 2:
            d_local, crosses[0] = together(d_local, crosses[0])
        locals_.append(d_local)
        rings.append(lax.ppermute(d_local, ("fsdp", "tp"), ring_pairs))
        crosses.append(lax.ppermute(d_local, ("fsdp", "tp"), cross_pairs))

    def gathered(c):
        d_near = jnp.where(near, locals_[c], rings[c])
        d_far = jnp.where(near, rings[c], crosses[c])
        return jnp.concatenate([d_near, d_far], axis=0)

    def add_pseudo(d_all, lo, hi, after=None, behind=None):
        at_cols = slice(lo * narrow, hi * narrow)
        piece = d_all[:, : (hi - lo) * narrow]
        if after in line.sums:
            piece, line.sums[after] = together(piece, line.sums[after])
        if behind is not None:
            piece, line.part[behind] = together(piece, line.part[behind])
        piece, first, second, outer = together(piece, first_moment, second_moment, weight)
        grad = lax.dot_general(
            context_all, piece, (((0,), (0,)), ((), ())), preferred_element_type=f32
        ) / (tok_rows * fsdp_count)
        first = first[0, :, at_cols].astype(f32)
        second = second[0, :, at_cols].astype(f32)
        m_new = beta_one * first + (1.0 - beta_one) * grad
        v_new = beta_two * second + (1.0 - beta_two) * grad * grad
        update = m_new / bias_one / (
            jnp.sqrt(v_new / bias_two) + adam_eps
        ) + decay_rate * outer[:, at_cols].astype(f32)
        pseudo = lax.optimization_barrier(update.astype(bf16))
        for u in range(hi - lo):
            line.part[lo + u] = pseudo[:, u * narrow : (u + 1) * narrow]

    for c in range(len(widths)):
        move(c)
    add_pseudo(gathered(0), 0, 1)
    found = gathered(1)
    early = sum(widths[:2])
    add_pseudo(found, 1, 2)
    add_pseudo(found[:, narrow:], 2, early, behind=1)
    last = gathered(2)
    todo = [(lo, min(lo + 2, units)) for lo in range(early, units, 2)]
    if islands == 4:
        for s in range(2):
            line.send_outer(s)
        for s in range(units + 3):
            while todo and todo[0][0] - 3 <= s:
                lo, hi = todo.pop(0)
                add_pseudo(last[:, (lo - early) * narrow :], lo, hi, s - 1)
            line.step(s)
        sums = [line.totals[k] for k in range(units)]
    else:
        for lo, hi in todo:
            add_pseudo(last[:, (lo - early) * narrow :], lo, hi)
        sums = [lax.psum(line.part[k], "island") for k in range(units)]
    ends = list(range(3, units - 3, 3)) + [units - 3, units - 1, units]
    outputs, start = (), 0
    for end in ends:
        outputs = finish(sums[start:end], start * narrow, islands, momentum, outputs)
        start = end
    return outputs


def solution(mesh):
    in_specs = (
        P(("island", "fsdp"), "tp"),
        P(("island", "fsdp"), "tp"),
        P(("island", "fsdp"), "tp"),
        P(),
        P("tp", "fsdp"),
        P("island", "tp", "fsdp"),
        P("island", "tp", "fsdp"),
        P("tp", "fsdp"),
    )
    out_specs = (P("tp", "fsdp"), P("tp", "fsdp"))
    return jax.shard_map(body, mesh=mesh, in_specs=in_specs, out_specs=out_specs, check_vma=False)
```

```python
import functools

import jax
import jax.numpy as jnp
from jax import lax
from jax.experimental import pallas as pl
from jax.experimental.pallas import tpu as pltpu
from jax.sharding import PartitionSpec as P

norm_eps = 1e-06
adam_eps = 1e-08
beta_one = 0.9
beta_two = 0.999
bias_one = 1.0 - 0.9**10
bias_two = 1.0 - 0.999**10
decay_rate = 0.1
outer_mu = 0.9

f32 = jnp.float32
bf16 = jnp.bfloat16


def outer_update(delta, momentum):
    new_momentum = outer_mu * momentum + delta
    outer_step = (delta + outer_mu * new_momentum).astype(bf16)
    return (new_momentum, outer_step)


def swap(value, axis, bit):
    count = lax.axis_size(axis)
    return lax.ppermute(value, axis, [(i, i ^ bit) for i in range(count)])


def finish_kernel(count, start, narrow, islands, *refs):
    totals, momentum = refs[:count], refs[count]
    new_out, step_out, held, fresh, step, sems = refs[-6:]
    columns = pl.ds(start, count * narrow)
    load = pltpu.make_async_copy(momentum.at[:, columns], held, sems.at[0])
    load.start()
    load.wait()
    for k in range(count):
        at = slice(k * narrow, (k + 1) * narrow)
        delta = totals[k][...].astype(f32) / islands
        fresh[:, at], step[:, at] = outer_update(delta, held[:, at])
    stores = [
        pltpu.make_async_copy(fresh, new_out.at[:, columns], sems.at[1]),
        pltpu.make_async_copy(step, step_out.at[:, columns], sems.at[2]),
    ]
    for store in stores:
        store.start()
    for store in stores:
        store.wait()


def finish(totals, start, islands, momentum, outputs):
    rows, narrow = totals[0].shape
    count = len(totals)
    wide = count * narrow
    in_hbm = pl.BlockSpec(memory_space=pltpu.HBM)
    in_vmem = pl.BlockSpec(memory_space=pltpu.VMEM)
    return pl.pallas_call(
        functools.partial(finish_kernel, count, start, narrow, islands),
        out_shape=(
            jax.ShapeDtypeStruct(momentum.shape, f32),
            jax.ShapeDtypeStruct(momentum.shape, bf16),
        ),
        in_specs=[in_vmem] * count + [in_hbm] * (1 + len(outputs)),
        out_specs=(in_hbm, in_hbm),
        scratch_shapes=[
            pltpu.VMEM((rows, wide), f32),
            pltpu.VMEM((rows, wide), f32),
            pltpu.VMEM((rows, wide), bf16),
            pltpu.SemaphoreType.DMA((3,)),
        ],
        input_output_aliases={count + 1 + k: k for k in range(len(outputs))},
        compiler_params=pltpu.CompilerParams(vmem_limit_bytes=16 * 1024 * 1024),
        cost_estimate=pl.CostEstimate(
            flops=5 * rows * wide, bytes_accessed=12 * rows * wide, transcendentals=0
        ),
    )(*totals, momentum, *outputs)


def together(*values):
    return lax.optimization_barrier(values)


class IslandLine:
    def __init__(self, chunks):
        self.chunks = chunks
        me = lax.axis_index("island")
        self.outer = (me == 0) | (me == 3)
        self.part, self.paid, self.edge, self.mid, self.sums, self.totals = {}, {}, {}, {}, {}, {}

    def send_outer(self, s):
        if s >= self.chunks + 3:
            return
        pairs = [(0, 1), (3, 2)] if s < self.chunks else []
        if s >= 3:
            pairs = pairs + [(1, 0), (2, 3)]
            total = (self.sums[s - 3].astype(f32) + self.mid[s - 3].astype(f32)).astype(bf16)
            payload = jnp.where(self.outer, self.part[s], total) if s < self.chunks else total
        else:
            payload = self.part[s]
            if s == 2:
                payload, self.sums[0] = together(payload, self.sums[0])
        self.paid[s] = payload
        self.edge[s] = lax.ppermute(payload, "island", pairs)

    def step(self, s):
        edge = self.edge[s]
        if s + 1 in self.paid:
            edge, self.paid[s + 1] = together(edge, self.paid[s + 1])
        if s < self.chunks:
            self.sums[s] = (edge.astype(f32) + self.part[s].astype(f32)).astype(bf16)
            self.mid[s] = lax.ppermute(self.sums[s], "island", [(1, 2), (2, 1)])
            if s >= 1:
                self.mid[s - 1], self.sums[s] = together(self.mid[s - 1], self.sums[s])
        self.send_outer(s + 2)
        if s >= 3:
            if s + 2 in self.paid:
                edge, self.paid[s], self.paid[s + 2] = together(edge, self.paid[s], self.paid[s + 2])
            else:
                edge, self.paid[s] = together(edge, self.paid[s])
            self.totals[s - 3] = jnp.where(self.outer, edge, self.paid[s])


def body(context, residual, cotangent, gain, weight, first_moment, second_moment, momentum):
    tok_rows = context.shape[0]
    width = gain.shape[0]
    fsdp_count = lax.axis_size("fsdp")
    group = fsdp_count // 2
    cols = weight.shape[1]
    t = lax.axis_index("tp")
    f = lax.axis_index("fsdp")
    high = f // group
    low = f % group
    near = t == high

    pieces = 2
    rows = tok_rows // pieces

    def project(block):
        return lax.optimization_barrier(
            jnp.dot(block, weight, preferred_element_type=f32).astype(bf16)
        )

    def at(h, q, x):
        return (h * group + q) * 2 + x

    ring_pairs, cross_pairs = [], []
    for q in range(group):
        ring_pairs += [(at(x, q, x), at(x, q, 1 - x)) for x in (0, 1)]
        ring_pairs += [(at(1 - x, q, x), at(x, q, x)) for x in (0, 1)]
        cross_pairs += [(at(1 - x, q, x), at(x, q, 1 - x)) for x in (0, 1)]
    inward_pairs = [(at(1 - x, q, x), at(1 - x, q, 1 - x)) for q in range(group) for x in (0, 1)]
    outward_pairs = [(at(x, q, x), at(x, q, 1 - x)) for q in range(group) for x in (0, 1)]

    near_blocks = [context] + [swap(context, "fsdp", r) for r in range(1, group)]
    slices = [
        [lax.dynamic_slice_in_dim(array, (low ^ r) * cols, cols, axis=1) for r in range(group)]
        for array in (residual, cotangent)
    ]
    moved = [[swap(parts[r], "fsdp", r) if r else parts[r] for r in range(group)] for parts in slices]
    held = together(swap(context, "fsdp", group), *moved[0], *moved[1])
    residual_parts, cotangent_parts = held[1 : 1 + group], held[1 + group :]
    far_blocks = [held[0]] + [swap(held[0], "fsdp", r) for r in range(1, group)]
    near_out = project(jnp.concatenate(near_blocks, axis=0))
    near_came = lax.ppermute(near_out, ("fsdp", "tp"), inward_pairs)
    far_outs = []
    for r in range(group):
        out = project(far_blocks[r])
        far_outs += [swap(out[p * rows : (p + 1) * rows], "fsdp", group) for p in range(pieces)]
    passed = [lax.ppermute(out, ("fsdp", "tp"), outward_pairs) for out in far_outs]

    gain_part = lax.dynamic_slice_in_dim(gain, t * (width // 2) + low * cols, cols).astype(f32)

    hidden, weighted, sums = [], [], []
    for k in range(group * pieces):
        r, p = k // pieces, k % pieces
        span, long_span = slice(p * rows, (p + 1) * rows), slice(k * rows, (k + 1) * rows)
        res, cot, came = residual_parts[r], cotangent_parts[r], passed[k]
        if sums:
            came, sums[-1] = together(came, sums[-1])
        keep = jnp.where(near, near_out[long_span], far_outs[k])
        came = jnp.where(near, near_came[long_span], came)
        h = res[span].astype(f32) + keep.astype(f32) + came.astype(f32)
        w = gain_part[None, :] * cot[span].astype(f32)
        hidden.append(h)
        weighted.append(w)
        sums.append(jnp.stack([jnp.sum(h * h, axis=-1), jnp.sum(h * w, axis=-1)]))
    own_sums = jnp.concatenate(sums, axis=1)
    totals = own_sums
    for r in range(1, group):
        came = swap(own_sums, "fsdp", r)
        order = [r ^ k for k in range(group)]
        came = jnp.concatenate(
            [came[:, k * tok_rows : (k + 1) * tok_rows] for k in order], axis=1
        )
        totals = totals + came
    totals = totals + swap(totals, "tp", 1)
    inv_rms = lax.rsqrt(totals[0] / width + norm_eps)
    pull = inv_rms**3 * totals[1] / width

    context_all = jnp.concatenate(near_blocks + far_blocks, axis=0)
    narrow = 128
    units = cols // narrow
    widths = [1, 3, units - 4]
    islands = lax.axis_size("island")
    line = IslandLine(units)
    locals_, rings, crosses = [], [], []

    def move(c):
        cols_at = slice(sum(widths[:c]) * narrow, sum(widths[: c + 1]) * narrow)
        d_local = jnp.concatenate(
            [
                weighted[j][:, cols_at] * inv_rms[j * rows : (j + 1) * rows, None]
                - hidden[j][:, cols_at] * pull[j * rows : (j + 1) * rows, None]
                for j in range(group * pieces)
            ],
            axis=0,
        ).astype(bf16)
        if c == 1:
            d_local, rings[0] = together(d_local, rings[0])
        elif c == 2:
            d_local, crosses[0] = together(d_local, crosses[0])
        locals_.append(d_local)
        rings.append(lax.ppermute(d_local, ("fsdp", "tp"), ring_pairs))
        crosses.append(lax.ppermute(d_local, ("fsdp", "tp"), cross_pairs))

    def gathered(c):
        d_near = jnp.where(near, locals_[c], rings[c])
        d_far = jnp.where(near, rings[c], crosses[c])
        return jnp.concatenate([d_near, d_far], axis=0)

    def add_pseudo(d_all, lo, hi, after=None, behind=None):
        at_cols = slice(lo * narrow, hi * narrow)
        piece = d_all[:, : (hi - lo) * narrow]
        if after in line.sums:
            piece, line.sums[after] = together(piece, line.sums[after])
        if behind is not None:
            piece, line.part[behind] = together(piece, line.part[behind])
        piece, first, second, outer = together(piece, first_moment, second_moment, weight)
        grad = lax.dot_general(
            context_all, piece, (((0,), (0,)), ((), ())), preferred_element_type=f32
        ) / (tok_rows * fsdp_count)
        first = first[0, :, at_cols].astype(f32)
        second = second[0, :, at_cols].astype(f32)
        m_new = beta_one * first + (1.0 - beta_one) * grad
        v_new = beta_two * second + (1.0 - beta_two) * grad * grad
        update = m_new / bias_one / (
            jnp.sqrt(v_new / bias_two) + adam_eps
        ) + decay_rate * outer[:, at_cols].astype(f32)
        pseudo = lax.optimization_barrier(update.astype(bf16))
        for u in range(hi - lo):
            line.part[lo + u] = pseudo[:, u * narrow : (u + 1) * narrow]

    for c in range(len(widths)):
        move(c)
    add_pseudo(gathered(0), 0, 1)
    found = gathered(1)
    early = sum(widths[:2])
    add_pseudo(found, 1, 2)
    add_pseudo(found[:, narrow:], 2, early, behind=1)
    last = gathered(2)
    todo = [(lo, min(lo + 2, units)) for lo in range(early, units, 2)]
    if islands == 4:
        for s in range(2):
            line.send_outer(s)
        for s in range(units + 3):
            while todo and todo[0][0] - 3 <= s:
                lo, hi = todo.pop(0)
                add_pseudo(last[:, (lo - early) * narrow :], lo, hi, s - 1)
            line.step(s)
            first = 3 * (s - units + 2)
            if first >= 0 and s + 2 in line.paid and first in line.totals:
                line.totals[first], line.paid[s + 2] = together(line.totals[first], line.paid[s + 2])
        sums = [line.totals[k] for k in range(units)]
    else:
        for lo, hi in todo:
            add_pseudo(last[:, (lo - early) * narrow :], lo, hi)
        sums = [lax.psum(line.part[k], "island") for k in range(units)]
    ends = list(range(3, units - 3, 3)) + [units - 3, units - 1, units]
    outputs, start = (), 0
    for end in ends:
        outputs = finish(sums[start:end], start * narrow, islands, momentum, outputs)
        start = end
    return outputs


def solution(mesh):
    in_specs = (
        P(("island", "fsdp"), "tp"),
        P(("island", "fsdp"), "tp"),
        P(("island", "fsdp"), "tp"),
        P(),
        P("tp", "fsdp"),
        P("island", "tp", "fsdp"),
        P("island", "tp", "fsdp"),
        P("tp", "fsdp"),
    )
    out_specs = (P("tp", "fsdp"), P("tp", "fsdp"))
    return jax.shard_map(body, mesh=mesh, in_specs=in_specs, out_specs=out_specs, check_vma=False)
```

```python
import functools

import jax
import jax.numpy as jnp
from jax import lax
from jax.experimental import pallas as pl
from jax.experimental.pallas import tpu as pltpu
from jax.sharding import PartitionSpec as P

norm_eps = 1e-06
adam_eps = 1e-08
beta_one = 0.9
beta_two = 0.999
bias_one = 1.0 - 0.9**10
bias_two = 1.0 - 0.999**10
decay_rate = 0.1
outer_mu = 0.9

f32 = jnp.float32
bf16 = jnp.bfloat16


def outer_update(delta, momentum):
    new_momentum = outer_mu * momentum + delta
    outer_step = (delta + outer_mu * new_momentum).astype(bf16)
    return (new_momentum, outer_step)


def swap(value, axis, bit):
    count = lax.axis_size(axis)
    return lax.ppermute(value, axis, [(i, i ^ bit) for i in range(count)])


def finish_kernel(count, start, narrow, islands, *refs):
    totals, momentum = refs[:count], refs[count]
    new_out, step_out, held, fresh, step, sems = refs[-6:]
    columns = pl.ds(start, count * narrow)
    load = pltpu.make_async_copy(momentum.at[:, columns], held, sems.at[0])
    load.start()
    load.wait()
    for k in range(count):
        at = slice(k * narrow, (k + 1) * narrow)
        delta = totals[k][...].astype(f32) / islands
        fresh[:, at], step[:, at] = outer_update(delta, held[:, at])
    stores = [
        pltpu.make_async_copy(fresh, new_out.at[:, columns], sems.at[1]),
        pltpu.make_async_copy(step, step_out.at[:, columns], sems.at[2]),
    ]
    for store in stores:
        store.start()
    for store in stores:
        store.wait()


def finish(totals, start, islands, momentum, outputs):
    rows, narrow = totals[0].shape
    count = len(totals)
    wide = count * narrow
    in_hbm = pl.BlockSpec(memory_space=pltpu.HBM)
    in_vmem = pl.BlockSpec(memory_space=pltpu.VMEM)
    return pl.pallas_call(
        functools.partial(finish_kernel, count, start, narrow, islands),
        out_shape=(
            jax.ShapeDtypeStruct(momentum.shape, f32),
            jax.ShapeDtypeStruct(momentum.shape, bf16),
        ),
        in_specs=[in_vmem] * count + [in_hbm] * (1 + len(outputs)),
        out_specs=(in_hbm, in_hbm),
        scratch_shapes=[
            pltpu.VMEM((rows, wide), f32),
            pltpu.VMEM((rows, wide), f32),
            pltpu.VMEM((rows, wide), bf16),
            pltpu.SemaphoreType.DMA((3,)),
        ],
        input_output_aliases={count + 1 + k: k for k in range(len(outputs))},
        compiler_params=pltpu.CompilerParams(vmem_limit_bytes=16 * 1024 * 1024),
        cost_estimate=pl.CostEstimate(
            flops=5 * rows * wide, bytes_accessed=12 * rows * wide, transcendentals=0
        ),
    )(*totals, momentum, *outputs)


def together(*values):
    return lax.optimization_barrier(values)


class IslandLine:
    def __init__(self, chunks):
        self.chunks = chunks
        me = lax.axis_index("island")
        self.outer = (me == 0) | (me == 3)
        self.part, self.paid, self.edge, self.mid, self.sums, self.totals = {}, {}, {}, {}, {}, {}

    def send_outer(self, s):
        if s >= self.chunks + 3:
            return
        pairs = [(0, 1), (3, 2)] if s < self.chunks else []
        if s >= 3:
            pairs = pairs + [(1, 0), (2, 3)]
            total = (self.sums[s - 3].astype(f32) + self.mid[s - 3].astype(f32)).astype(bf16)
            payload = jnp.where(self.outer, self.part[s], total) if s < self.chunks else total
        else:
            payload = self.part[s]
            if s == 2:
                payload, self.sums[0] = together(payload, self.sums[0])
        self.paid[s] = payload
        self.edge[s] = lax.ppermute(payload, "island", pairs)

    def step(self, s):
        edge = self.edge[s]
        if s + 1 in self.paid:
            edge, self.paid[s + 1] = together(edge, self.paid[s + 1])
        if s < self.chunks:
            self.sums[s] = (edge.astype(f32) + self.part[s].astype(f32)).astype(bf16)
            self.mid[s] = lax.ppermute(self.sums[s], "island", [(1, 2), (2, 1)])
            if s >= 1:
                self.mid[s - 1], self.sums[s] = together(self.mid[s - 1], self.sums[s])
        self.send_outer(s + 2)
        if s >= 3:
            if s + 2 in self.paid:
                edge, self.paid[s], self.paid[s + 2] = together(edge, self.paid[s], self.paid[s + 2])
            else:
                edge, self.paid[s] = together(edge, self.paid[s])
            self.totals[s - 3] = jnp.where(self.outer, edge, self.paid[s])


def body(context, residual, cotangent, gain, weight, first_moment, second_moment, momentum):
    tok_rows = context.shape[0]
    width = gain.shape[0]
    fsdp_count = lax.axis_size("fsdp")
    group = fsdp_count // 2
    cols = weight.shape[1]
    t = lax.axis_index("tp")
    f = lax.axis_index("fsdp")
    high = f // group
    low = f % group
    near = t == high

    pieces = 2
    rows = tok_rows // pieces

    def project(block):
        return lax.optimization_barrier(
            jnp.dot(block, weight, preferred_element_type=f32).astype(bf16)
        )

    def at(h, q, x):
        return (h * group + q) * 2 + x

    ring_pairs, cross_pairs = [], []
    for q in range(group):
        ring_pairs += [(at(x, q, x), at(x, q, 1 - x)) for x in (0, 1)]
        ring_pairs += [(at(1 - x, q, x), at(x, q, x)) for x in (0, 1)]
        cross_pairs += [(at(1 - x, q, x), at(x, q, 1 - x)) for x in (0, 1)]
    inward_pairs = [(at(1 - x, q, x), at(1 - x, q, 1 - x)) for q in range(group) for x in (0, 1)]
    outward_pairs = [(at(x, q, x), at(x, q, 1 - x)) for q in range(group) for x in (0, 1)]

    near_blocks = [context] + [swap(context, "fsdp", r) for r in range(1, group)]
    slices = [
        [lax.dynamic_slice_in_dim(array, (low ^ r) * cols, cols, axis=1) for r in range(group)]
        for array in (residual, cotangent)
    ]
    moved = [[swap(parts[r], "fsdp", r) if r else parts[r] for r in range(group)] for parts in slices]
    held = together(swap(context, "fsdp", group), *moved[0], *moved[1])
    residual_parts, cotangent_parts = held[1 : 1 + group], held[1 + group :]
    far_blocks = [held[0]] + [swap(held[0], "fsdp", r) for r in range(1, group)]
    near_out = project(jnp.concatenate(near_blocks, axis=0))
    near_came = lax.ppermute(near_out, ("fsdp", "tp"), inward_pairs)
    far_outs = []
    for r in range(group):
        out = project(far_blocks[r])
        far_outs += [swap(out[p * rows : (p + 1) * rows], "fsdp", group) for p in range(pieces)]
    passed = [lax.ppermute(out, ("fsdp", "tp"), outward_pairs) for out in far_outs]

    gain_part = lax.dynamic_slice_in_dim(gain, t * (width // 2) + low * cols, cols).astype(f32)

    hidden, weighted, sums = [], [], []
    for k in range(group * pieces):
        r, p = k // pieces, k % pieces
        span, long_span = slice(p * rows, (p + 1) * rows), slice(k * rows, (k + 1) * rows)
        res, cot, came = residual_parts[r], cotangent_parts[r], passed[k]
        if sums:
            came, sums[-1] = together(came, sums[-1])
        keep = jnp.where(near, near_out[long_span], far_outs[k])
        came = jnp.where(near, near_came[long_span], came)
        h = res[span].astype(f32) + keep.astype(f32) + came.astype(f32)
        w = gain_part[None, :] * cot[span].astype(f32)
        hidden.append(h)
        weighted.append(w)
        sums.append(jnp.stack([jnp.sum(h * h, axis=-1), jnp.sum(h * w, axis=-1)]))
    own_sums = jnp.concatenate(sums, axis=1)
    totals = own_sums
    for r in range(1, group):
        came = swap(own_sums, "fsdp", r)
        order = [r ^ k for k in range(group)]
        came = jnp.concatenate(
            [came[:, k * tok_rows : (k + 1) * tok_rows] for k in order], axis=1
        )
        totals = totals + came
    totals = totals + swap(totals, "tp", 1)
    inv_rms = lax.rsqrt(totals[0] / width + norm_eps)
    pull = inv_rms**3 * totals[1] / width

    context_all = jnp.concatenate(near_blocks + far_blocks, axis=0)
    narrow = 128
    units = cols // narrow
    widths = [1, min(4, units - 2), units - 1 - min(4, units - 2)]
    islands = lax.axis_size("island")
    line = IslandLine(units)
    locals_, rings, crosses = [], [], []

    def move(c):
        cols_at = slice(sum(widths[:c]) * narrow, sum(widths[: c + 1]) * narrow)
        d_local = jnp.concatenate(
            [
                weighted[j][:, cols_at] * inv_rms[j * rows : (j + 1) * rows, None]
                - hidden[j][:, cols_at] * pull[j * rows : (j + 1) * rows, None]
                for j in range(group * pieces)
            ],
            axis=0,
        ).astype(bf16)
        if c == 1:
            d_local, rings[0] = together(d_local, rings[0])
        elif c == 2 and 0 in line.sums:
            d_local, line.sums[0] = together(d_local, line.sums[0])
        locals_.append(d_local)
        rings.append(lax.ppermute(d_local, ("fsdp", "tp"), ring_pairs))
        crosses.append(lax.ppermute(d_local, ("fsdp", "tp"), cross_pairs))

    def gathered(c):
        d_near = jnp.where(near, locals_[c], rings[c])
        d_far = jnp.where(near, rings[c], crosses[c])
        return jnp.concatenate([d_near, d_far], axis=0)

    def add_pseudo(d_all, lo, hi, after=None, behind=None):
        at_cols = slice(lo * narrow, hi * narrow)
        piece = d_all[:, : (hi - lo) * narrow]
        if after in line.sums:
            piece, line.sums[after] = together(piece, line.sums[after])
        if behind is not None:
            piece, line.part[behind] = together(piece, line.part[behind])
        piece, first, second, outer = together(piece, first_moment, second_moment, weight)
        grad = lax.dot_general(
            context_all, piece, (((0,), (0,)), ((), ())), preferred_element_type=f32
        ) / (tok_rows * fsdp_count)
        first = first[0, :, at_cols].astype(f32)
        second = second[0, :, at_cols].astype(f32)
        m_new = beta_one * first + (1.0 - beta_one) * grad
        v_new = beta_two * second + (1.0 - beta_two) * grad * grad
        update = m_new / bias_one / (
            jnp.sqrt(v_new / bias_two) + adam_eps
        ) + decay_rate * outer[:, at_cols].astype(f32)
        pseudo = lax.optimization_barrier(update.astype(bf16))
        for u in range(hi - lo):
            line.part[lo + u] = pseudo[:, u * narrow : (u + 1) * narrow]

    move(0)
    move(1)
    add_pseudo(gathered(0), 0, 1)
    found = gathered(1)
    early = sum(widths[:2])
    add_pseudo(found, 1, 2)
    for lo in range(2, early, 2):
        add_pseudo(found[:, (lo - 1) * narrow :], lo, min(lo + 2, early), behind=1)
    todo = [(lo, min(lo + 2, units)) for lo in range(early, units, 2)]
    if islands == 4:
        for s in range(2):
            line.send_outer(s)
        for s in range(units + 3):
            while todo and todo[0][0] - 3 <= s:
                lo, hi = todo.pop(0)
                add_pseudo(last[:, (lo - early) * narrow :], lo, hi, s - 1)
            line.step(s)
            if s == 0:
                move(2)
                last = gathered(2)
            first = 3 * (s - units + 2)
            if first >= 0 and s + 2 in line.paid and first in line.totals:
                line.totals[first], line.paid[s + 2] = together(line.totals[first], line.paid[s + 2])
        sums = [line.totals[k] for k in range(units)]
    else:
        move(2)
        last = gathered(2)
        for lo, hi in todo:
            add_pseudo(last[:, (lo - early) * narrow :], lo, hi)
        sums = [lax.psum(line.part[k], "island") for k in range(units)]
    ends = list(range(3, units - 3, 3)) + [units - 3, units - 1, units]
    outputs, start = (), 0
    for end in ends:
        outputs = finish(sums[start:end], start * narrow, islands, momentum, outputs)
        start = end
    return outputs


def solution(mesh):
    in_specs = (
        P(("island", "fsdp"), "tp"),
        P(("island", "fsdp"), "tp"),
        P(("island", "fsdp"), "tp"),
        P(),
        P("tp", "fsdp"),
        P("island", "tp", "fsdp"),
        P("island", "tp", "fsdp"),
        P("tp", "fsdp"),
    )
    out_specs = (P("tp", "fsdp"), P("tp", "fsdp"))
    return jax.shard_map(body, mesh=mesh, in_specs=in_specs, out_specs=out_specs, check_vma=False)
```

```python
import functools

import jax
import jax.numpy as jnp
from jax import lax
from jax.experimental import pallas as pl
from jax.experimental.pallas import tpu as pltpu
from jax.sharding import PartitionSpec as P

norm_eps = 1e-06
adam_eps = 1e-08
beta_one = 0.9
beta_two = 0.999
bias_one = 1.0 - 0.9**10
bias_two = 1.0 - 0.999**10
decay_rate = 0.1
outer_mu = 0.9

f32 = jnp.float32
bf16 = jnp.bfloat16


def outer_update(delta, momentum):
    new_momentum = outer_mu * momentum + delta
    outer_step = (delta + outer_mu * new_momentum).astype(bf16)
    return (new_momentum, outer_step)


def swap(value, axis, bit):
    count = lax.axis_size(axis)
    return lax.ppermute(value, axis, [(i, i ^ bit) for i in range(count)])


def finish_kernel(count, start, narrow, islands, *refs):
    totals, momentum = refs[:count], refs[count]
    new_out, step_out, held, fresh, step, sems = refs[-6:]
    columns = pl.ds(start, count * narrow)
    load = pltpu.make_async_copy(momentum.at[:, columns], held, sems.at[0])
    load.start()
    load.wait()
    for k in range(count):
        at = slice(k * narrow, (k + 1) * narrow)
        delta = totals[k][...].astype(f32) / islands
        fresh[:, at], step[:, at] = outer_update(delta, held[:, at])
    stores = [
        pltpu.make_async_copy(fresh, new_out.at[:, columns], sems.at[1]),
        pltpu.make_async_copy(step, step_out.at[:, columns], sems.at[2]),
    ]
    for store in stores:
        store.start()
    for store in stores:
        store.wait()


def finish(totals, start, islands, momentum, outputs):
    rows, narrow = totals[0].shape
    count = len(totals)
    wide = count * narrow
    in_hbm = pl.BlockSpec(memory_space=pltpu.HBM)
    in_vmem = pl.BlockSpec(memory_space=pltpu.VMEM)
    return pl.pallas_call(
        functools.partial(finish_kernel, count, start, narrow, islands),
        out_shape=(
            jax.ShapeDtypeStruct(momentum.shape, f32),
            jax.ShapeDtypeStruct(momentum.shape, bf16),
        ),
        in_specs=[in_vmem] * count + [in_hbm] * (1 + len(outputs)),
        out_specs=(in_hbm, in_hbm),
        scratch_shapes=[
            pltpu.VMEM((rows, wide), f32),
            pltpu.VMEM((rows, wide), f32),
            pltpu.VMEM((rows, wide), bf16),
            pltpu.SemaphoreType.DMA((3,)),
        ],
        input_output_aliases={count + 1 + k: k for k in range(len(outputs))},
        compiler_params=pltpu.CompilerParams(vmem_limit_bytes=16 * 1024 * 1024),
        cost_estimate=pl.CostEstimate(
            flops=5 * rows * wide, bytes_accessed=12 * rows * wide, transcendentals=0
        ),
    )(*totals, momentum, *outputs)


def together(*values):
    return lax.optimization_barrier(values)


class IslandLine:
    def __init__(self, chunks):
        self.chunks = chunks
        me = lax.axis_index("island")
        self.outer = (me == 0) | (me == 3)
        self.part, self.paid, self.edge, self.mid, self.sums, self.totals = {}, {}, {}, {}, {}, {}

    def send_outer(self, s):
        if s >= self.chunks + 3:
            return
        pairs = [(0, 1), (3, 2)] if s < self.chunks else []
        if s >= 3:
            pairs = pairs + [(1, 0), (2, 3)]
            total = (self.sums[s - 3].astype(f32) + self.mid[s - 3].astype(f32)).astype(bf16)
            payload = jnp.where(self.outer, self.part[s], total) if s < self.chunks else total
        else:
            payload = self.part[s]
            if s == 2:
                payload, self.sums[0] = together(payload, self.sums[0])
        self.paid[s] = payload
        self.edge[s] = lax.ppermute(payload, "island", pairs)

    def step(self, s):
        edge = self.edge[s]
        if s + 1 in self.paid:
            edge, self.paid[s + 1] = together(edge, self.paid[s + 1])
        if s < self.chunks:
            self.sums[s] = (edge.astype(f32) + self.part[s].astype(f32)).astype(bf16)
            self.mid[s] = lax.ppermute(self.sums[s], "island", [(1, 2), (2, 1)])
            if s >= 1:
                self.mid[s - 1], self.sums[s] = together(self.mid[s - 1], self.sums[s])
        self.send_outer(s + 2)
        if s >= 3:
            if s + 2 in self.paid:
                edge, self.paid[s], self.paid[s + 2] = together(edge, self.paid[s], self.paid[s + 2])
            else:
                edge, self.paid[s] = together(edge, self.paid[s])
            self.totals[s - 3] = jnp.where(self.outer, edge, self.paid[s])


def body(context, residual, cotangent, gain, weight, first_moment, second_moment, momentum):
    tok_rows = context.shape[0]
    width = gain.shape[0]
    fsdp_count = lax.axis_size("fsdp")
    group = fsdp_count // 2
    cols = weight.shape[1]
    t = lax.axis_index("tp")
    f = lax.axis_index("fsdp")
    high = f // group
    low = f % group
    near = t == high

    pieces = 2
    rows = tok_rows // pieces

    def project(block):
        return lax.optimization_barrier(
            jnp.dot(block, weight, preferred_element_type=f32).astype(bf16)
        )

    def at(h, q, x):
        return (h * group + q) * 2 + x

    ring_pairs, cross_pairs = [], []
    for q in range(group):
        ring_pairs += [(at(x, q, x), at(x, q, 1 - x)) for x in (0, 1)]
        ring_pairs += [(at(1 - x, q, x), at(x, q, x)) for x in (0, 1)]
        cross_pairs += [(at(1 - x, q, x), at(x, q, 1 - x)) for x in (0, 1)]
    inward_pairs = [(at(1 - x, q, x), at(1 - x, q, 1 - x)) for q in range(group) for x in (0, 1)]
    outward_pairs = [(at(x, q, x), at(x, q, 1 - x)) for q in range(group) for x in (0, 1)]

    near_blocks = [context] + [swap(context, "fsdp", r) for r in range(1, group)]
    slices = [
        [lax.dynamic_slice_in_dim(array, (low ^ r) * cols, cols, axis=1) for r in range(group)]
        for array in (residual, cotangent)
    ]
    moved = [[swap(parts[r], "fsdp", r) if r else parts[r] for r in range(group)] for parts in slices]
    held = together(swap(context, "fsdp", group), *moved[0], *moved[1])
    residual_parts, cotangent_parts = held[1 : 1 + group], held[1 + group :]
    far_blocks = [held[0]] + [swap(held[0], "fsdp", r) for r in range(1, group)]
    near_out = project(jnp.concatenate(near_blocks, axis=0))
    near_came = lax.ppermute(near_out, ("fsdp", "tp"), inward_pairs)
    far_outs = []
    for r in range(group):
        out = project(far_blocks[r])
        far_outs += [swap(out[p * rows : (p + 1) * rows], "fsdp", group) for p in range(pieces)]
    passed = [lax.ppermute(out, ("fsdp", "tp"), outward_pairs) for out in far_outs]

    gain_part = lax.dynamic_slice_in_dim(gain, t * (width // 2) + low * cols, cols).astype(f32)

    hidden, weighted, sums = [], [], []
    for k in range(group * pieces):
        r, p = k // pieces, k % pieces
        span, long_span = slice(p * rows, (p + 1) * rows), slice(k * rows, (k + 1) * rows)
        res, cot, came = residual_parts[r], cotangent_parts[r], passed[k]
        if sums:
            came, sums[-1] = together(came, sums[-1])
        keep = jnp.where(near, near_out[long_span], far_outs[k])
        came = jnp.where(near, near_came[long_span], came)
        h = res[span].astype(f32) + keep.astype(f32) + came.astype(f32)
        w = gain_part[None, :] * cot[span].astype(f32)
        hidden.append(h)
        weighted.append(w)
        sums.append(jnp.stack([jnp.sum(h * h, axis=-1), jnp.sum(h * w, axis=-1)]))
    own_sums = jnp.concatenate(sums, axis=1)
    totals = own_sums
    for r in range(1, group):
        came = swap(own_sums, "fsdp", r)
        order = [r ^ k for k in range(group)]
        came = jnp.concatenate(
            [came[:, k * tok_rows : (k + 1) * tok_rows] for k in order], axis=1
        )
        totals = totals + came
    totals = totals + swap(totals, "tp", 1)
    inv_rms = lax.rsqrt(totals[0] / width + norm_eps)
    pull = inv_rms**3 * totals[1] / width

    context_all = jnp.concatenate(near_blocks + far_blocks, axis=0)
    narrow = 128
    units = cols // narrow
    widths = [1, 3, units - 4]
    islands = lax.axis_size("island")
    line = IslandLine(units)
    locals_, rings, crosses = [], [], []

    def move(c):
        cols_at = slice(sum(widths[:c]) * narrow, sum(widths[: c + 1]) * narrow)
        d_local = jnp.concatenate(
            [
                weighted[j][:, cols_at] * inv_rms[j * rows : (j + 1) * rows, None]
                - hidden[j][:, cols_at] * pull[j * rows : (j + 1) * rows, None]
                for j in range(group * pieces)
            ],
            axis=0,
        ).astype(bf16)
        if c == 1:
            d_local, rings[0] = together(d_local, rings[0])
        elif c == 2:
            d_local, crosses[0] = together(d_local, crosses[0])
        locals_.append(d_local)
        crosses.append(lax.ppermute(d_local, ("fsdp", "tp"), cross_pairs))
        rings.append(lax.ppermute(d_local, ("fsdp", "tp"), ring_pairs))

    def gathered(c):
        d_near = jnp.where(near, locals_[c], rings[c])
        d_far = jnp.where(near, rings[c], crosses[c])
        return jnp.concatenate([d_near, d_far], axis=0)

    def add_pseudo(d_all, lo, hi, after=None, behind=None):
        at_cols = slice(lo * narrow, hi * narrow)
        piece = d_all[:, : (hi - lo) * narrow]
        if after in line.sums:
            piece, line.sums[after] = together(piece, line.sums[after])
        if behind is not None:
            piece, line.part[behind] = together(piece, line.part[behind])
        piece, first, second, outer = together(piece, first_moment, second_moment, weight)
        grad = lax.dot_general(
            context_all, piece, (((0,), (0,)), ((), ())), preferred_element_type=f32
        ) / (tok_rows * fsdp_count)
        first = first[0, :, at_cols].astype(f32)
        second = second[0, :, at_cols].astype(f32)
        m_new = beta_one * first + (1.0 - beta_one) * grad
        v_new = beta_two * second + (1.0 - beta_two) * grad * grad
        update = m_new / bias_one / (
            jnp.sqrt(v_new / bias_two) + adam_eps
        ) + decay_rate * outer[:, at_cols].astype(f32)
        pseudo = lax.optimization_barrier(update.astype(bf16))
        for u in range(hi - lo):
            line.part[lo + u] = pseudo[:, u * narrow : (u + 1) * narrow]

    for c in range(len(widths)):
        move(c)
    add_pseudo(gathered(0), 0, 1)
    found = gathered(1)
    early = sum(widths[:2])
    add_pseudo(found, 1, 2)
    add_pseudo(found[:, narrow:], 2, early, behind=1)
    last = gathered(2)
    todo = [(lo, min(lo + 2, units)) for lo in range(early, units, 2)]
    if islands == 4:
        for s in range(2):
            line.send_outer(s)
        for s in range(units + 3):
            while todo and todo[0][0] - 3 <= s:
                lo, hi = todo.pop(0)
                add_pseudo(last[:, (lo - early) * narrow :], lo, hi, s - 1)
            line.step(s)
            first = 3 * (s - units + 2)
            if first >= 0 and s + 2 in line.paid and first in line.totals:
                line.totals[first], line.paid[s + 2] = together(line.totals[first], line.paid[s + 2])
        sums = [line.totals[k] for k in range(units)]
    else:
        for lo, hi in todo:
            add_pseudo(last[:, (lo - early) * narrow :], lo, hi)
        sums = [lax.psum(line.part[k], "island") for k in range(units)]
    ends = list(range(3, units - 3, 3)) + [units - 3, units - 1, units]
    outputs, start = (), 0
    for end in ends:
        outputs = finish(sums[start:end], start * narrow, islands, momentum, outputs)
        start = end
    return outputs


def solution(mesh):
    in_specs = (
        P(("island", "fsdp"), "tp"),
        P(("island", "fsdp"), "tp"),
        P(("island", "fsdp"), "tp"),
        P(),
        P("tp", "fsdp"),
        P("island", "tp", "fsdp"),
        P("island", "tp", "fsdp"),
        P("tp", "fsdp"),
    )
    out_specs = (P("tp", "fsdp"), P("tp", "fsdp"))
    return jax.shard_map(body, mesh=mesh, in_specs=in_specs, out_specs=out_specs, check_vma=False)
```

```python
import functools

import jax
import jax.numpy as jnp
from jax import lax
from jax.experimental import pallas as pl
from jax.experimental.pallas import tpu as pltpu
from jax.sharding import PartitionSpec as P

norm_eps = 1e-06
adam_eps = 1e-08
beta_one = 0.9
beta_two = 0.999
bias_one = 1.0 - 0.9**10
bias_two = 1.0 - 0.999**10
decay_rate = 0.1
outer_mu = 0.9

f32 = jnp.float32
bf16 = jnp.bfloat16


def outer_update(delta, momentum):
    new_momentum = outer_mu * momentum + delta
    outer_step = (delta + outer_mu * new_momentum).astype(bf16)
    return (new_momentum, outer_step)


def swap(value, axis, bit):
    count = lax.axis_size(axis)
    return lax.ppermute(value, axis, [(i, i ^ bit) for i in range(count)])


def finish_kernel(count, start, narrow, islands, *refs):
    totals, momentum = refs[:count], refs[count]
    new_out, step_out, held, step, sems = refs[-5:]
    columns = pl.ds(start, count * narrow)
    load = pltpu.make_async_copy(momentum.at[:, columns], held, sems.at[0])
    load.start()
    load.wait()
    for k in range(count):
        at = slice(k * narrow, (k + 1) * narrow)
        delta = totals[k][...].astype(f32) / islands
        held[:, at], step[:, at] = outer_update(delta, held[:, at])
    stores = [
        pltpu.make_async_copy(held, new_out.at[:, columns], sems.at[1]),
        pltpu.make_async_copy(step, step_out.at[:, columns], sems.at[2]),
    ]
    for store in stores:
        store.start()
    for store in stores:
        store.wait()


def finish(totals, start, islands, momentum, outputs):
    rows, narrow = totals[0].shape
    count = len(totals)
    wide = count * narrow
    in_hbm = pl.BlockSpec(memory_space=pltpu.HBM)
    in_vmem = pl.BlockSpec(memory_space=pltpu.VMEM)
    return pl.pallas_call(
        functools.partial(finish_kernel, count, start, narrow, islands),
        out_shape=(
            jax.ShapeDtypeStruct(momentum.shape, f32),
            jax.ShapeDtypeStruct(momentum.shape, bf16),
        ),
        in_specs=[in_vmem] * count + [in_hbm] * (1 + len(outputs)),
        out_specs=(in_hbm, in_hbm),
        scratch_shapes=[
            pltpu.VMEM((rows, wide), f32),
            pltpu.VMEM((rows, wide), bf16),
            pltpu.SemaphoreType.DMA((3,)),
        ],
        input_output_aliases={count + 1 + k: k for k in range(len(outputs))},
        compiler_params=pltpu.CompilerParams(vmem_limit_bytes=8 * 1024 * 1024),
        cost_estimate=pl.CostEstimate(
            flops=5 * rows * wide, bytes_accessed=12 * rows * wide, transcendentals=0
        ),
    )(*totals, momentum, *outputs)


def together(*values):
    return lax.optimization_barrier(values)


class IslandLine:
    def __init__(self, chunks):
        self.chunks = chunks
        me = lax.axis_index("island")
        self.outer = (me == 0) | (me == 3)
        self.part, self.paid, self.edge, self.mid, self.sums, self.totals = {}, {}, {}, {}, {}, {}

    def send_outer(self, s):
        if s >= self.chunks + 3:
            return
        pairs = [(0, 1), (3, 2)] if s < self.chunks else []
        if s >= 3:
            pairs = pairs + [(1, 0), (2, 3)]
            total = (self.sums[s - 3].astype(f32) + self.mid[s - 3].astype(f32)).astype(bf16)
            payload = jnp.where(self.outer, self.part[s], total) if s < self.chunks else total
        else:
            payload = self.part[s]
            if s == 2:
                payload, self.sums[0] = together(payload, self.sums[0])
        self.paid[s] = payload
        self.edge[s] = lax.ppermute(payload, "island", pairs)

    def step(self, s):
        edge = self.edge[s]
        if s + 1 in self.paid:
            edge, self.paid[s + 1] = together(edge, self.paid[s + 1])
        if s < self.chunks:
            self.sums[s] = (edge.astype(f32) + self.part[s].astype(f32)).astype(bf16)
            self.mid[s] = lax.ppermute(self.sums[s], "island", [(1, 2), (2, 1)])
            if s >= 1:
                self.mid[s - 1], self.sums[s] = together(self.mid[s - 1], self.sums[s])
        self.send_outer(s + 2)
        if s >= 3:
            if s + 2 in self.paid:
                edge, self.paid[s], self.paid[s + 2] = together(edge, self.paid[s], self.paid[s + 2])
            else:
                edge, self.paid[s] = together(edge, self.paid[s])
            self.totals[s - 3] = jnp.where(self.outer, edge, self.paid[s])


def body(context, residual, cotangent, gain, weight, first_moment, second_moment, momentum):
    tok_rows = context.shape[0]
    width = gain.shape[0]
    fsdp_count = lax.axis_size("fsdp")
    group = fsdp_count // 2
    cols = weight.shape[1]
    t = lax.axis_index("tp")
    f = lax.axis_index("fsdp")
    high = f // group
    low = f % group
    near = t == high

    pieces = 2
    rows = tok_rows // pieces

    def project(block):
        return lax.optimization_barrier(
            jnp.dot(block, weight, preferred_element_type=f32).astype(bf16)
        )

    def at(h, q, x):
        return (h * group + q) * 2 + x

    ring_pairs, cross_pairs = [], []
    for q in range(group):
        ring_pairs += [(at(x, q, x), at(x, q, 1 - x)) for x in (0, 1)]
        ring_pairs += [(at(1 - x, q, x), at(x, q, x)) for x in (0, 1)]
        cross_pairs += [(at(1 - x, q, x), at(x, q, 1 - x)) for x in (0, 1)]
    inward_pairs = [(at(1 - x, q, x), at(1 - x, q, 1 - x)) for q in range(group) for x in (0, 1)]
    outward_pairs = [(at(x, q, x), at(x, q, 1 - x)) for q in range(group) for x in (0, 1)]

    near_blocks = [context] + [swap(context, "fsdp", r) for r in range(1, group)]
    slices = [
        [lax.dynamic_slice_in_dim(array, (low ^ r) * cols, cols, axis=1) for r in range(group)]
        for array in (residual, cotangent)
    ]
    moved = [[swap(parts[r], "fsdp", r) if r else parts[r] for r in range(group)] for parts in slices]
    held = together(swap(context, "fsdp", group), *moved[0], *moved[1])
    residual_parts, cotangent_parts = held[1 : 1 + group], held[1 + group :]
    far_blocks = [held[0]] + [swap(held[0], "fsdp", r) for r in range(1, group)]
    near_out = project(jnp.concatenate(near_blocks, axis=0))
    near_came = lax.ppermute(near_out, ("fsdp", "tp"), inward_pairs)
    far_outs = []
    for r in range(group):
        out = project(far_blocks[r])
        far_outs += [swap(out[p * rows : (p + 1) * rows], "fsdp", group) for p in range(pieces)]
    passed = [lax.ppermute(out, ("fsdp", "tp"), outward_pairs) for out in far_outs]

    gain_part = lax.dynamic_slice_in_dim(gain, t * (width // 2) + low * cols, cols).astype(f32)

    hidden, weighted, sums = [], [], []
    for k in range(group * pieces):
        r, p = k // pieces, k % pieces
        span, long_span = slice(p * rows, (p + 1) * rows), slice(k * rows, (k + 1) * rows)
        res, cot, came = residual_parts[r], cotangent_parts[r], passed[k]
        if sums:
            came, sums[-1] = together(came, sums[-1])
        keep = jnp.where(near, near_out[long_span], far_outs[k])
        came = jnp.where(near, near_came[long_span], came)
        h = res[span].astype(f32) + keep.astype(f32) + came.astype(f32)
        w = gain_part[None, :] * cot[span].astype(f32)
        hidden.append(h)
        weighted.append(w)
        sums.append(jnp.stack([jnp.sum(h * h, axis=-1), jnp.sum(h * w, axis=-1)]))
    own_sums = jnp.concatenate(sums, axis=1)
    totals = own_sums
    for r in range(1, group):
        came = swap(own_sums, "fsdp", r)
        order = [r ^ k for k in range(group)]
        came = jnp.concatenate(
            [came[:, k * tok_rows : (k + 1) * tok_rows] for k in order], axis=1
        )
        totals = totals + came
    totals = totals + swap(totals, "tp", 1)
    inv_rms = lax.rsqrt(totals[0] / width + norm_eps)
    pull = inv_rms**3 * totals[1] / width

    context_all = jnp.concatenate(near_blocks + far_blocks, axis=0)
    narrow = 128
    units = cols // narrow
    widths = [1, 3, units - 4]
    islands = lax.axis_size("island")
    line = IslandLine(units)
    locals_, rings, crosses = [], [], []

    def move(c):
        cols_at = slice(sum(widths[:c]) * narrow, sum(widths[: c + 1]) * narrow)
        d_local = jnp.concatenate(
            [
                weighted[j][:, cols_at] * inv_rms[j * rows : (j + 1) * rows, None]
                - hidden[j][:, cols_at] * pull[j * rows : (j + 1) * rows, None]
                for j in range(group * pieces)
            ],
            axis=0,
        ).astype(bf16)
        if c == 1:
            d_local, rings[0] = together(d_local, rings[0])
        elif c == 2:
            d_local, crosses[0] = together(d_local, crosses[0])
        locals_.append(d_local)
        rings.append(lax.ppermute(d_local, ("fsdp", "tp"), ring_pairs))
        crosses.append(lax.ppermute(d_local, ("fsdp", "tp"), cross_pairs))

    def gathered(c):
        d_near = jnp.where(near, locals_[c], rings[c])
        d_far = jnp.where(near, rings[c], crosses[c])
        return jnp.concatenate([d_near, d_far], axis=0)

    def add_pseudo(d_all, lo, hi, after=None, behind=None):
        at_cols = slice(lo * narrow, hi * narrow)
        piece = d_all[:, : (hi - lo) * narrow]
        if after in line.sums:
            piece, line.sums[after] = together(piece, line.sums[after])
        if behind is not None:
            piece, line.part[behind] = together(piece, line.part[behind])
        piece, first, second, outer = together(piece, first_moment, second_moment, weight)
        grad = lax.dot_general(
            context_all, piece, (((0,), (0,)), ((), ())), preferred_element_type=f32
        ) / (tok_rows * fsdp_count)
        first = first[0, :, at_cols].astype(f32)
        second = second[0, :, at_cols].astype(f32)
        m_new = beta_one * first + (1.0 - beta_one) * grad
        v_new = beta_two * second + (1.0 - beta_two) * grad * grad
        update = m_new / bias_one / (
            jnp.sqrt(v_new / bias_two) + adam_eps
        ) + decay_rate * outer[:, at_cols].astype(f32)
        pseudo = lax.optimization_barrier(update.astype(bf16))
        for u in range(hi - lo):
            line.part[lo + u] = pseudo[:, u * narrow : (u + 1) * narrow]

    for c in range(len(widths)):
        move(c)
    add_pseudo(gathered(0), 0, 1)
    found = gathered(1)
    early = sum(widths[:2])
    add_pseudo(found, 1, 2)
    add_pseudo(found[:, narrow:], 2, early, behind=1)
    last = gathered(2)
    todo = [(lo, min(lo + 2, units)) for lo in range(early, units, 2)]
    if islands == 4:
        for s in range(2):
            line.send_outer(s)
        for s in range(units + 3):
            while todo and todo[0][0] - 3 <= s:
                lo, hi = todo.pop(0)
                add_pseudo(last[:, (lo - early) * narrow :], lo, hi, s - 1)
            line.step(s)
            first = 3 * (s - units + 2)
            if first >= 0 and s + 2 in line.paid and first in line.totals:
                line.totals[first], line.paid[s + 2] = together(line.totals[first], line.paid[s + 2])
        sums = [line.totals[k] for k in range(units)]
    else:
        for lo, hi in todo:
            add_pseudo(last[:, (lo - early) * narrow :], lo, hi)
        sums = [lax.psum(line.part[k], "island") for k in range(units)]
    ends = list(range(3, units - 3, 3)) + [units - 3, units - 1, units]
    outputs, start = (), 0
    for end in ends:
        outputs = finish(sums[start:end], start * narrow, islands, momentum, outputs)
        start = end
    return outputs


def solution(mesh):
    in_specs = (
        P(("island", "fsdp"), "tp"),
        P(("island", "fsdp"), "tp"),
        P(("island", "fsdp"), "tp"),
        P(),
        P("tp", "fsdp"),
        P("island", "tp", "fsdp"),
        P("island", "tp", "fsdp"),
        P("tp", "fsdp"),
    )
    out_specs = (P("tp", "fsdp"), P("tp", "fsdp"))
    return jax.shard_map(body, mesh=mesh, in_specs=in_specs, out_specs=out_specs, check_vma=False)
```

```python
import functools

import jax
import jax.numpy as jnp
from jax import lax
from jax.experimental import pallas as pl
from jax.experimental.pallas import tpu as pltpu
from jax.sharding import PartitionSpec as P

norm_eps = 1e-06
adam_eps = 1e-08
beta_one = 0.9
beta_two = 0.999
bias_one = 1.0 - 0.9**10
bias_two = 1.0 - 0.999**10
decay_rate = 0.1
outer_mu = 0.9

f32 = jnp.float32
bf16 = jnp.bfloat16


def outer_update(delta, momentum):
    new_momentum = outer_mu * momentum + delta
    outer_step = (delta + outer_mu * new_momentum).astype(bf16)
    return (new_momentum, outer_step)


def swap(value, axis, bit):
    count = lax.axis_size(axis)
    return lax.ppermute(value, axis, [(i, i ^ bit) for i in range(count)])


def finish_kernel(count, start, narrow, islands, *refs):
    totals, momentum = refs[:count], refs[count]
    new_out, step_out, held, fresh, step, sems = refs[-6:]
    columns = pl.ds(start, count * narrow)
    load = pltpu.make_async_copy(momentum.at[:, columns], held, sems.at[0])
    load.start()
    load.wait()
    for k in range(count):
        at = slice(k * narrow, (k + 1) * narrow)
        delta = totals[k][...].astype(f32) / islands
        fresh[:, at], step[:, at] = outer_update(delta, held[:, at])
    stores = [
        pltpu.make_async_copy(fresh, new_out.at[:, columns], sems.at[1]),
        pltpu.make_async_copy(step, step_out.at[:, columns], sems.at[2]),
    ]
    for store in stores:
        store.start()
    for store in stores:
        store.wait()


def finish(totals, start, islands, momentum, outputs):
    rows, narrow = totals[0].shape
    count = len(totals)
    wide = count * narrow
    in_hbm = pl.BlockSpec(memory_space=pltpu.HBM)
    in_vmem = pl.BlockSpec(memory_space=pltpu.VMEM)
    return pl.pallas_call(
        functools.partial(finish_kernel, count, start, narrow, islands),
        out_shape=(
            jax.ShapeDtypeStruct(momentum.shape, f32),
            jax.ShapeDtypeStruct(momentum.shape, bf16),
        ),
        in_specs=[in_vmem] * count + [in_hbm] * (1 + len(outputs)),
        out_specs=(in_hbm, in_hbm),
        scratch_shapes=[
            pltpu.VMEM((rows, wide), f32),
            pltpu.VMEM((rows, wide), f32),
            pltpu.VMEM((rows, wide), bf16),
            pltpu.SemaphoreType.DMA((3,)),
        ],
        input_output_aliases={count + 1 + k: k for k in range(len(outputs))},
        compiler_params=pltpu.CompilerParams(vmem_limit_bytes=16 * 1024 * 1024),
        cost_estimate=pl.CostEstimate(
            flops=5 * rows * wide, bytes_accessed=12 * rows * wide, transcendentals=0
        ),
    )(*totals, momentum, *outputs)


def together(*values):
    return lax.optimization_barrier(values)


class IslandLine:
    def __init__(self, chunks):
        self.chunks = chunks
        me = lax.axis_index("island")
        self.outer = (me == 0) | (me == 3)
        self.part, self.paid, self.edge, self.mid, self.sums, self.totals = {}, {}, {}, {}, {}, {}

    def send_outer(self, s):
        if s >= self.chunks + 3:
            return
        pairs = [(0, 1), (3, 2)] if s < self.chunks else []
        if s >= 3:
            pairs = pairs + [(1, 0), (2, 3)]
            total = (self.sums[s - 3].astype(f32) + self.mid[s - 3].astype(f32)).astype(bf16)
            payload = jnp.where(self.outer, self.part[s], total) if s < self.chunks else total
        else:
            payload = self.part[s]
            if s == 2:
                payload, self.sums[0] = together(payload, self.sums[0])
        self.paid[s] = payload
        self.edge[s] = lax.ppermute(payload, "island", pairs)

    def step(self, s):
        edge = self.edge[s]
        if s + 1 in self.paid:
            edge, self.paid[s + 1] = together(edge, self.paid[s + 1])
        if s < self.chunks:
            self.sums[s] = (edge.astype(f32) + self.part[s].astype(f32)).astype(bf16)
            self.mid[s] = lax.ppermute(self.sums[s], "island", [(1, 2), (2, 1)])
            if s >= 1:
                self.mid[s - 1], self.sums[s] = together(self.mid[s - 1], self.sums[s])
        self.send_outer(s + 2)
        if s >= 3:
            if s + 2 in self.paid:
                edge, self.paid[s], self.paid[s + 2] = together(edge, self.paid[s], self.paid[s + 2])
            else:
                edge, self.paid[s] = together(edge, self.paid[s])
            self.totals[s - 3] = jnp.where(self.outer, edge, self.paid[s])


def body(context, residual, cotangent, gain, weight, first_moment, second_moment, momentum):
    tok_rows = context.shape[0]
    width = gain.shape[0]
    fsdp_count = lax.axis_size("fsdp")
    group = fsdp_count // 2
    cols = weight.shape[1]
    t = lax.axis_index("tp")
    f = lax.axis_index("fsdp")
    high = f // group
    low = f % group
    near = t == high

    pieces = 2
    rows = tok_rows // pieces

    def project(block):
        return lax.optimization_barrier(
            jnp.dot(block, weight, preferred_element_type=f32).astype(bf16)
        )

    def at(h, q, x):
        return (h * group + q) * 2 + x

    ring_pairs, cross_pairs = [], []
    for q in range(group):
        ring_pairs += [(at(x, q, x), at(x, q, 1 - x)) for x in (0, 1)]
        ring_pairs += [(at(1 - x, q, x), at(x, q, x)) for x in (0, 1)]
        cross_pairs += [(at(1 - x, q, x), at(x, q, 1 - x)) for x in (0, 1)]
    inward_pairs = [(at(1 - x, q, x), at(1 - x, q, 1 - x)) for q in range(group) for x in (0, 1)]
    outward_pairs = [(at(x, q, x), at(x, q, 1 - x)) for q in range(group) for x in (0, 1)]

    near_blocks = [context] + [swap(context, "fsdp", r) for r in range(1, group)]
    slices = [
        [lax.dynamic_slice_in_dim(array, (low ^ r) * cols, cols, axis=1) for r in range(group)]
        for array in (residual, cotangent)
    ]
    moved = [[swap(parts[r], "fsdp", r) if r else parts[r] for r in range(group)] for parts in slices]
    held = together(swap(context, "fsdp", group), *moved[0], *moved[1])
    residual_parts, cotangent_parts = held[1 : 1 + group], held[1 + group :]
    far_blocks = [held[0]] + [swap(held[0], "fsdp", r) for r in range(1, group)]
    near_out = project(jnp.concatenate(near_blocks, axis=0))
    near_came = lax.ppermute(near_out, ("fsdp", "tp"), inward_pairs)
    far_outs = []
    for r in range(group):
        out = project(far_blocks[r])
        far_outs += [swap(out[p * rows : (p + 1) * rows], "fsdp", group) for p in range(pieces)]
    passed = [lax.ppermute(out, ("fsdp", "tp"), outward_pairs) for out in far_outs]

    gain_part = lax.dynamic_slice_in_dim(gain, t * (width // 2) + low * cols, cols).astype(f32)

    ready = [
        lax.optimization_barrier(gain_part[None, :] * cot.astype(f32)) for cot in cotangent_parts
    ]
    hidden, weighted, sums = [], [], []
    for k in range(group * pieces):
        r, p = k // pieces, k % pieces
        span, long_span = slice(p * rows, (p + 1) * rows), slice(k * rows, (k + 1) * rows)
        res, came = residual_parts[r], passed[k]
        if sums:
            came, sums[-1] = together(came, sums[-1])
        keep = jnp.where(near, near_out[long_span], far_outs[k])
        came = jnp.where(near, near_came[long_span], came)
        h = res[span].astype(f32) + keep.astype(f32) + came.astype(f32)
        w = ready[r][span]
        hidden.append(h)
        weighted.append(w)
        sums.append(jnp.stack([jnp.sum(h * h, axis=-1), jnp.sum(h * w, axis=-1)]))
    own_sums = jnp.concatenate(sums, axis=1)
    totals = own_sums
    for r in range(1, group):
        came = swap(own_sums, "fsdp", r)
        order = [r ^ k for k in range(group)]
        came = jnp.concatenate(
            [came[:, k * tok_rows : (k + 1) * tok_rows] for k in order], axis=1
        )
        totals = totals + came
    totals = totals + swap(totals, "tp", 1)
    inv_rms = lax.rsqrt(totals[0] / width + norm_eps)
    pull = inv_rms**3 * totals[1] / width

    context_all = jnp.concatenate(near_blocks + far_blocks, axis=0)
    narrow = 128
    units = cols // narrow
    widths = [1, 3, units - 4]
    islands = lax.axis_size("island")
    line = IslandLine(units)
    locals_, rings, crosses = [], [], []

    def move(c):
        cols_at = slice(sum(widths[:c]) * narrow, sum(widths[: c + 1]) * narrow)
        d_local = jnp.concatenate(
            [
                weighted[j][:, cols_at] * inv_rms[j * rows : (j + 1) * rows, None]
                - hidden[j][:, cols_at] * pull[j * rows : (j + 1) * rows, None]
                for j in range(group * pieces)
            ],
            axis=0,
        ).astype(bf16)
        if c == 1:
            d_local, rings[0] = together(d_local, rings[0])
        elif c == 2:
            d_local, crosses[0] = together(d_local, crosses[0])
        locals_.append(d_local)
        rings.append(lax.ppermute(d_local, ("fsdp", "tp"), ring_pairs))
        crosses.append(lax.ppermute(d_local, ("fsdp", "tp"), cross_pairs))

    def gathered(c):
        d_near = jnp.where(near, locals_[c], rings[c])
        d_far = jnp.where(near, rings[c], crosses[c])
        return jnp.concatenate([d_near, d_far], axis=0)

    def add_pseudo(d_all, lo, hi, after=None, behind=None):
        at_cols = slice(lo * narrow, hi * narrow)
        piece = d_all[:, : (hi - lo) * narrow]
        if after in line.sums:
            piece, line.sums[after] = together(piece, line.sums[after])
        if behind is not None:
            piece, line.part[behind] = together(piece, line.part[behind])
        piece, first, second, outer = together(piece, first_moment, second_moment, weight)
        grad = lax.dot_general(
            context_all, piece, (((0,), (0,)), ((), ())), preferred_element_type=f32
        ) / (tok_rows * fsdp_count)
        first = first[0, :, at_cols].astype(f32)
        second = second[0, :, at_cols].astype(f32)
        m_new = beta_one * first + (1.0 - beta_one) * grad
        v_new = beta_two * second + (1.0 - beta_two) * grad * grad
        update = m_new / bias_one / (
            jnp.sqrt(v_new / bias_two) + adam_eps
        ) + decay_rate * outer[:, at_cols].astype(f32)
        pseudo = lax.optimization_barrier(update.astype(bf16))
        for u in range(hi - lo):
            line.part[lo + u] = pseudo[:, u * narrow : (u + 1) * narrow]

    for c in range(len(widths)):
        move(c)
    add_pseudo(gathered(0), 0, 1)
    found = gathered(1)
    early = sum(widths[:2])
    add_pseudo(found, 1, 2)
    add_pseudo(found[:, narrow:], 2, early, behind=1)
    last = gathered(2)
    todo = [(lo, min(lo + 2, units)) for lo in range(early, units, 2)]
    if islands == 4:
        for s in range(2):
            line.send_outer(s)
        for s in range(units + 3):
            while todo and todo[0][0] - 3 <= s:
                lo, hi = todo.pop(0)
                add_pseudo(last[:, (lo - early) * narrow :], lo, hi, s - 1)
            line.step(s)
        sums = [line.totals[k] for k in range(units)]
    else:
        for lo, hi in todo:
            add_pseudo(last[:, (lo - early) * narrow :], lo, hi)
        sums = [lax.psum(line.part[k], "island") for k in range(units)]
    ends = list(range(3, units - 3, 3)) + [units - 3, units - 1, units]
    outputs, start = (), 0
    for end in ends:
        outputs = finish(sums[start:end], start * narrow, islands, momentum, outputs)
        start = end
    return outputs


def solution(mesh):
    in_specs = (
        P(("island", "fsdp"), "tp"),
        P(("island", "fsdp"), "tp"),
        P(("island", "fsdp"), "tp"),
        P(),
        P("tp", "fsdp"),
        P("island", "tp", "fsdp"),
        P("island", "tp", "fsdp"),
        P("tp", "fsdp"),
    )
    out_specs = (P("tp", "fsdp"), P("tp", "fsdp"))
    return jax.shard_map(body, mesh=mesh, in_specs=in_specs, out_specs=out_specs, check_vma=False)
```
